32 devices in a mesh: lon: 8 (over z, y), lev: 4 (over x, core).
Axes of the slice: x: 2, y: 2, z: 4, core: 2. Of those that a mesh axis runs over, the one named last changes fastest.
Arguments:
- current_vector: float32 [16, 256, 512], P('lev', 'lon'), may hold values from -6 to 6
- previous_vector: float32 [16, 256, 512], P('lev', 'lon')
- beta_previous: float32 [], replicated, may hold values from 0.5 to 1.5
- stored_vectors: float32 [16, 16, 256, 512], P(None, 'lev', 'lon')
- velocity: float32 [2, 3, 16, 256, 512], P(None, None, 'lev', 'lon'), may hold values from -0.6 to 0.6
- level_weight: float32 [16], P('lev'), may hold values from 0.3 to 3
- box_owner: int32 [256, 512], P('lon'), may hold values from 0 to 5, as said below
Outputs:
- next_vector: float32 [16, 256, 512], P('lev', 'lon')
- lanczos_coefficients: float32 [18], replicated
The draws below stay inside these ranges and needn't reach their ends.
Inputs may be any that keep to these rules, and one draw needn't show every extreme that they name: `box_owner`: each box is a rectangle in longitude (possibly across the date line) and latitude; a later box overwrites an earlier one where they meet; box 5 is present in every draw and spans more than half of the 256 longitude columns.
All inputs are finite; a program needn't handle non-finite values.
Results may differ from the reference program's by a relative error of at most 0.000076.
Values sent between devices are 32-bit elements; how exact they have to be, the bound alone decides.
No kernel may reach another device: no remote copies, remote signals or barrier semaphores. Data moves between devices by JAX's collectives and lax.ppermute only.
A program may use at most 64 MiB of HBM per device.

```python
import math
import jax
import jax.numpy as jnp
from jax import lax

LAT = 512
NVEC = 16
NBOX = 5
LEV = 16
LON = 256


def base_field(key, number):
    return jax.random.normal(jax.random.fold_in(key, 100 + number), (LEV, LON, LAT), jnp.float32)


def draw_previous_vector(key, part):
    shared = base_field(key, 0)
    key = jax.random.fold_in(key, 1)
    rough = jax.random.normal(key, (LEV, LON, LAT), jnp.float32)
    return 0.8 * shared + 0.6 * rough


def draw_stored_vectors(key, part):
    shared = base_field(key, 0)
    anchor = key
    key = jax.random.fold_in(key, 2)
    mixing = jax.random.uniform(jax.random.fold_in(key, 5), (NVEC,), jnp.float32, 0.05, 0.35)

    def single(number):
        return 0.9 * base_field(anchor, number + 1) + mixing[number] * shared
    return lax.map(single, jnp.arange(NVEC, dtype=jnp.int32))


def draw_box_owner(key, part):
    key = jax.random.fold_in(key, 3)
    starts = jax.random.randint(jax.random.fold_in(key, 1), (NBOX,), 0, LON)
    narrow = jax.random.randint(jax.random.fold_in(key, 2), (NBOX,), LON // 8, LON // 3 + 1)
    spanning = jax.random.randint(jax.random.fold_in(key, 5), (NBOX,), LON // 2 + 1, 3 * LON // 4 + 1)
    last_box = jnp.arange(NBOX, dtype=jnp.int32) == NBOX - 1
    widths = jnp.where(last_box, spanning, narrow)
    lowest = jax.random.randint(jax.random.fold_in(key, 3), (NBOX,), 0, LAT - LAT // 4)
    heights = jax.random.randint(jax.random.fold_in(key, 4), (NBOX,), LAT // 4, LAT // 2 + 1)
    columns = jnp.arange(LON, dtype=jnp.int32)
    rows_lat = jnp.arange(LAT, dtype=jnp.int32)
    inside_lon = (columns[None, :] - starts[:, None]) % LON < widths[:, None]
    inside_lat = (rows_lat[None, :] >= lowest[:, None]) & (rows_lat[None, :] < lowest[:, None] + heights[:, None])
    inside = inside_lon[:, :, None] & inside_lat[:, None, :]
    labels = jnp.arange(1, NBOX + 1, dtype=jnp.int32)[:, None, None]
    return jnp.max(jnp.where(inside, labels, 0), axis=0).astype(jnp.int32)


def level_of(rng, extent, cuts, least, top_value):
    level = 1.0
    for axis_at, blocks in cuts:
        steps = jax.random.uniform(jax.random.fold_in(jax.random.fold_in(rng, 6), axis_at), (blocks,), jnp.float32, least / len(cuts), top_value / len(cuts))
        level = level * jnp.repeat(jnp.exp(steps), extent[axis_at] // blocks).reshape((-1,) + (1,) * (len(extent) - 1 - axis_at))
    return level


def centred(stream_key, extent, width, reach, pieces=(), kind=jnp.bfloat16):
    entries = jax.random.normal(stream_key, extent, jnp.float32) * width
    if len(pieces) > 0:
        entries = level_of(stream_key, extent, pieces, -0.22, 0.18) * entries
    return jnp.clip(entries, min=-reach, max=reach).astype(kind)


def setup_inputs(seed: int = 0) -> dict:
    seeds = jax.random.split(jax.random.key(seed), 8)
    return {
        "current_vector": centred(seeds[0], (LEV, LON, LAT), 1.0, 6.0, ((0, 4), (1, 8)), jnp.float32),
        "previous_vector": draw_previous_vector(jax.random.fold_in(seeds[7], 71), 0),
        "beta_previous": jnp.clip(jax.random.uniform(seeds[2], (), jnp.float32, 0.5, 1.5), 0.5, 1.5),
        "stored_vectors": draw_stored_vectors(jax.random.fold_in(seeds[7], 71), 0),
        "velocity": jnp.clip(jax.random.uniform(seeds[4], (2, 3, LEV, LON, LAT), jnp.float32, -0.6, 0.6) * level_of(seeds[4], (2, 3, LEV, LON, LAT), ((2, 4), (3, 8)), -0.4, 0.0), -0.6, 0.6),
        "level_weight": jnp.clip(jnp.exp(math.log(3.0) - 2.3025851 * jax.random.uniform(seeds[5], (LEV,), jnp.float32) ** level_of(seeds[5], (LEV,), ((0, 4),), -0.2, 0.2)), 0.3, 3.0),
        "box_owner": draw_box_owner(jax.random.fold_in(seeds[7], 71), 0),
    }


kappa_mix = 0.1
centre_coef = 1.0 - 6.0 * kappa_mix
highest = lax.Precision.HIGHEST

def coefficients(flow):
    return (kappa_mix - 0.5 * flow[0], kappa_mix + 0.5 * flow[0], kappa_mix - 0.5 * flow[1], kappa_mix + 0.5 * flow[1], kappa_mix - 0.5 * flow[2], kappa_mix + 0.5 * flow[2])

def tangent(values, flow):
    stencil = coefficients(flow)
    eastern = jnp.roll(values, -1, axis=1)
    western = jnp.roll(values, 1, axis=1)
    northern = jnp.pad(values[:, :, 1:], ((0, 0), (0, 0), (0, 1)))
    southern = jnp.pad(values[:, :, :-1], ((0, 0), (0, 0), (1, 0)))
    level_above = jnp.pad(values[1:], ((0, 1), (0, 0), (0, 0)))
    level_below = jnp.pad(values[:-1], ((1, 0), (0, 0), (0, 0)))
    return centre_coef * values + stencil[0] * eastern + stencil[1] * western + stencil[2] * northern + stencil[3] * southern + stencil[4] * level_above + stencil[5] * level_below

def adjoint(values, flow):
    stencil = coefficients(flow)
    result = centre_coef * values
    result = result + jnp.roll(stencil[0] * values, 1, axis=1) + jnp.roll(stencil[1] * values, -1, axis=1)
    result = result + jnp.pad((stencil[2] * values)[:, :, :-1], ((0, 0), (0, 0), (1, 0)))
    result = result + jnp.pad((stencil[3] * values)[:, :, 1:], ((0, 0), (0, 0), (0, 1)))
    result = result + jnp.pad((stencil[4] * values)[:-1], ((1, 0), (0, 0), (0, 0)))
    result = result + jnp.pad((stencil[5] * values)[1:], ((0, 1), (0, 0), (0, 0)))
    return result

def reference(current_vector, previous_vector, beta_previous, stored_vectors, velocity, level_weight, box_owner):
    boxes = jnp.arange(1, NBOX + 1, dtype=jnp.int32)
    owner_hot = (box_owner[None] == boxes[:, None, None]).astype(jnp.float32)
    counts = lax.optimization_barrier(jnp.sum(owner_hot, axis=(1, 2)))
    scales = float(LON * LAT) / (NBOX * jnp.maximum(counts, 1.0))
    factor = lax.optimization_barrier(jnp.sum(owner_hot * scales[:, None, None], axis=0))
    first = tangent(current_vector, velocity[0])
    second = tangent(first, velocity[1])
    weighted = level_weight[:, None, None] * factor[None] * second
    applied = adjoint(adjoint(weighted, velocity[1]), velocity[0]) - beta_previous * previous_vector
    cells = float(LEV * LON * LAT)
    alpha_term = jnp.sum(applied * current_vector) / cells
    lanczos = applied - alpha_term * current_vector
    basis = stored_vectors.reshape(NVEC, -1)
    projections = jnp.dot(basis, lanczos.reshape(-1), precision=highest) / cells
    orthogonal = lanczos - jnp.dot(projections, basis, precision=highest).reshape(lanczos.shape)
    beta_norm = jnp.sqrt(jnp.sum(orthogonal * orthogonal) / cells + 1e-12)
    return (orthogonal / beta_norm, jnp.concatenate([alpha_term[None], beta_norm[None], projections]))
```

```python
import functools

import jax
import jax.numpy as jnp
from jax import lax
from jax.experimental import pallas as pl
from jax.experimental.pallas import tpu as pltpu
from jax.sharding import PartitionSpec as P

NBOX = 5
kappa = 0.1
centre = 1.0 - 6.0 * kappa
f32 = jnp.float32

VM = pl.BlockSpec(memory_space=pltpu.VMEM)
SM = pl.BlockSpec(memory_space=pltpu.SMEM)
CHUNK = 8
WIDE = 4
SECOND = 2
V_ROWS, A_ROWS, B_ROWS = 4, 3, 2
LEVEL_ROWS = V_ROWS + 3 * A_ROWS


def sds(*shape):
    return jax.ShapeDtypeStruct(shape, f32)


def call(kernel, outs, operands, specs=None, scratch=(), flops=0):
    nbytes = sum(4 * x.size for x in operands)
    return pl.pallas_call(
        kernel,
        out_shape=outs,
        in_specs=specs or [VM] * len(operands),
        out_specs=jax.tree.map(lambda _: VM, outs),
        scratch_shapes=list(scratch),
        compiler_params=pltpu.CompilerParams(vmem_limit_bytes=40 << 20),
        cost_estimate=pl.CostEstimate(flops=flops, bytes_accessed=nbytes, transcendentals=0),
    )(*operands)


def lane_iota(shape):
    return lax.broadcasted_iota(jnp.int32, shape, len(shape) - 1)


def even_level():
    return lax.rem(lax.axis_index("lev"), 2) == 0


def pack_kernel(levels, cols, v, vel, owner, lo_a, lo_b, hi_a, hi_b, lev_a, lev_b, counts):
    for msg_a, msg_b, low in ((lo_a, lo_b, True), (hi_a, hi_b, False)):

        def edge(n):
            return slice(0, n) if low else slice(cols - n, cols)

        for lev in range(levels):
            base = lev * LEVEL_ROWS
            msg_a[base : base + V_ROWS] = v[lev, edge(V_ROWS)]
            for comp in range(3):
                at = base + V_ROWS + comp * A_ROWS
                msg_a[at : at + A_ROWS] = vel[0, comp, lev, edge(A_ROWS)]
                at = (lev * 3 + comp) * B_ROWS
                msg_b[at : at + B_ROWS] = vel[1, comp, lev, edge(B_ROWS)]
        at = levels * LEVEL_ROWS
        msg_a[at : at + B_ROWS] = owner[edge(B_ROWS)].astype(f32)
    even = even_level()
    for msg, top in ((lev_a, even), (lev_b, jnp.logical_not(even))):
        near = jnp.where(top, levels - 1, 0)
        msg[0] = v[near]
        msg[1] = v[jnp.where(top, levels - 2, 1)]
        for comp in range(3):
            msg[2 + comp] = vel[0, comp, near]
    lanes = lane_iota((1, 128))
    row = jnp.zeros((1, 128), f32)
    held = owner[...]
    for box in range(1, NBOX + 1):
        hot = jnp.sum((held == box).astype(f32), axis=0, keepdims=True)
        row = jnp.where(lanes == box - 1, jnp.sum(hot, axis=1, keepdims=True), row)
    counts[...] = row


def corner_kernel(levels, n_counts, west, east, *refs):
    count_refs, (halo_v, halo_a, corner_a, corner_b, counts) = refs[:n_counts], refs[n_counts:]
    halo_a[...] = jnp.zeros(halo_a.shape, f32)
    for lev in range(levels):
        base = lev * LEVEL_ROWS
        halo_v[lev, 0:V_ROWS] = east[base : base + V_ROWS]
        halo_v[lev, CHUNK - V_ROWS : CHUNK] = west[base : base + V_ROWS]
        for comp in range(3):
            at = base + V_ROWS + comp * A_ROWS
            halo_a[comp, lev, 0:A_ROWS] = east[at : at + A_ROWS]
            halo_a[comp, lev, CHUNK - A_ROWS : CHUNK] = west[at : at + A_ROWS]
    even = even_level()
    for msg, top in ((corner_a, even), (corner_b, jnp.logical_not(even))):
        near = jnp.where(top, levels - 1, 0)
        msg[0] = halo_v[near]
        msg[1] = halo_v[jnp.where(top, levels - 2, 1)]
        for comp in range(3):
            msg[2 + comp] = halo_a[comp, near]
    total = count_refs[0][...]
    for ref in count_refs[1:]:
        total = total + ref[...]
    counts[...] = total


def stencil_kernel(
    levels, cols, lat, columns, n_counts,
    lw, beta_prev, v, prev, vel, owner, west, west_b, east_b, east, halo_v, halo_a,
    lev_a, lev_b, corner_a, corner_b, *refs,
):
    count_refs = refs[:n_counts]
    applied, send_a, send_b = refs[n_counts : n_counts + 3]
    (vv, la, ff, halo_b, own_h, w_in, w_e, w_w, w_u, w_d, u_in, u_e, u_w, u_u, u_d, out) = refs[n_counts + 3 :]
    chunks = cols // CHUNK
    level = lax.axis_index("lev")
    last = lax.axis_size("lev") - 1
    even = even_level()
    has = (level > 0, level < last)
    lanes = lane_iota((CHUNK, lat))
    first_lane, last_lane = lanes == 0, lanes == lat - 1

    def rows(k, shift=0):
        return slice(CHUNK * (k + 1) + shift, CHUNK * (k + 2) + shift)

    def put_west(ref, at, k, value):
        ref[at, rows(k)] = value
        if k == chunks:
            ref[at, 0:CHUNK] = value

    def put_east(ref, at, k, value):
        ref[at, rows(k)] = value
        if k == 0:
            ref[at, rows(chunks + 1)] = value

    def put_both(ref, at, k, value):
        put_west(ref, at, k, value)
        if k == 0:
            ref[at, rows(chunks + 1)] = value

    def from_south(x):
        return jnp.where(first_lane, 0.0, pltpu.roll(x, 1, 1))

    def from_north(x):
        return jnp.where(last_lane, 0.0, pltpu.roll(x, lat - 1, 1))

    for k in range(chunks + 1):
        cells = slice(CHUNK * k, CHUNK * (k + 1))
        got_a, got_b = (lev_a, lev_b) if k < chunks else (corner_a, corner_b)
        src = cells if k < chunks else slice(0, CHUNK)
        for item in range(5):
            a, b = got_a[item, src], got_b[item, src]
            below, above = jnp.where(even, b, a), jnp.where(even, a, b)
            if item < 2:
                put_both(vv, 1 - item, k, jnp.where(has[0], below, 0.0))
                put_both(vv, levels + 2 + item, k, jnp.where(has[1], above, 0.0))
            else:
                la[0, item - 2, cells] = below
                la[1, item - 2, cells] = above
        for lev in range(levels):
            put_both(vv, lev + 2, k, v[lev, cells] if k < chunks else halo_v[lev])
    halo_b[...] = jnp.zeros(halo_b.shape, f32)
    for lev in range(levels):
        for comp in range(3):
            at = (lev * 3 + comp) * B_ROWS
            halo_b[comp, lev, 0:B_ROWS] = east_b[at : at + B_ROWS]
            halo_b[comp, lev, CHUNK - B_ROWS : CHUNK] = west_b[at : at + B_ROWS]
    own_h[...] = jnp.zeros(own_h.shape, f32)
    at = levels * LEVEL_ROWS
    own_h[0:B_ROWS] = east[at : at + B_ROWS]
    own_h[CHUNK - B_ROWS : CHUNK] = west[at : at + B_ROWS]

    def flow(section, k, lev):
        if k < chunks:
            return [vel[section, comp, lev, CHUNK * k : CHUNK * (k + 1)] for comp in range(3)]
        return [(halo_b if section else halo_a)[comp, lev] for comp in range(3)]

    def flow_beyond(side, k):
        return [la[side, comp, CHUNK * k : CHUNK * (k + 1)] for comp in range(3)]

    def tangent(ref, at, k, abc):
        here = ref[at, rows(k)]
        e, w = ref[at, rows(k, 1)], ref[at, rows(k, -1)]
        n, s = from_north(here), from_south(here)
        u, d = ref[at + 1, rows(k)], ref[at - 1, rows(k)]
        a, b, c = abc
        around = ((e + w) + (n + s)) + (u + d)
        drift = a * (w - e) + b * (s - n) + c * (d - u)
        return centre * here + kappa * around + 0.5 * drift

    def push(x, abc, dst, at, k):
        inside, to_e, to_w, to_u, to_d = dst
        a, b, c = abc
        base, half = kappa * x, 0.5 * x
        a, b, c = a * half, b * half, c * half
        inside[at, rows(k)] = centre * x + (from_south(base - b) + from_north(base + b))
        put_west(to_e, at, k, base - a)
        put_east(to_w, at, k, base + a)
        to_u[at, rows(k)] = base - c
        to_d[at, rows(k)] = base + c

    for k in range(chunks + 1):
        for side, at in ((0, 0), (1, levels + 1)):
            value = tangent(vv, at + 1, k, flow_beyond(side, k))
            put_both(ff, at, k, jnp.where(has[side], value, 0.0))

    def first_level(lev, carry):
        for k in range(chunks + 1):
            put_both(ff, lev + 1, k, tangent(vv, lev + 2, k, flow(0, k, lev)))
        return carry

    lax.fori_loop(0, levels, first_level, 0)

    total = count_refs[0][...]
    for ref in count_refs[1:]:
        total = total + ref[...]
    scales = columns / (NBOX * jnp.maximum(total, 1.0))
    for k in range(chunks + 1):
        mine = owner[CHUNK * k : CHUNK * (k + 1)].astype(f32) if k < chunks else own_h[...]
        factor = jnp.zeros((CHUNK, lat), f32)
        for box in range(1, NBOX + 1):
            factor = jnp.where(mine == float(box), jnp.broadcast_to(scales[:, box - 1 : box], (CHUNK, lat)), factor)
        out[0, CHUNK * k : CHUNK * (k + 1)] = factor

    def second_level(lev, carry):
        weight = lw[lev]
        for k in range(chunks + 1):
            abc = flow(1, k, lev)
            x = tangent(ff, lev + 1, k, abc)
            x = (weight * out[0, CHUNK * k : CHUNK * (k + 1)]) * x
            push(x, abc, (w_in, w_e, w_w, w_u, w_d), lev + 1, k)
        return carry

    lax.fori_loop(0, levels, second_level, 0)
    for k in range(chunks + 1):
        w_u[0, rows(k)] = jnp.zeros((CHUNK, lat), f32)
        w_d[levels + 1, rows(k)] = jnp.zeros((CHUNK, lat), f32)

    def third_level(lev, carry):
        for k in range(chunks + 1):
            x = (
                w_in[lev + 1, rows(k)]
                + (w_e[lev + 1, rows(k, -1)] + w_w[lev + 1, rows(k, 1)])
                + (w_u[lev, rows(k)] + w_d[lev + 2, rows(k)])
            )
            push(x, flow(0, k, lev), (u_in, u_e, u_w, u_u, u_d), lev + 1, k)
        return carry

    lax.fori_loop(0, levels, third_level, 0)
    for k in range(chunks + 1):
        for side, at, x in ((0, 0, w_d[1, rows(k)]), (1, levels + 1, w_u[levels, rows(k)])):
            x = jnp.where(has[side], x, 0.0)
            push(x, flow_beyond(side, k), (u_in, u_e, u_w, u_u, u_d), at, k)

    beta = beta_prev[0]
    for k in range(chunks):
        cells = slice(CHUNK * k, CHUNK * (k + 1))
        out[0, cells] = u_d[0, rows(k)]
        out[levels + 3, cells] = u_u[levels + 1, rows(k)]
        for at in range(levels + 2):
            x = u_in[at, rows(k)] + (u_e[at, rows(k, -1)] + u_w[at, rows(k, 1)])
            if at > 0:
                x = x + u_u[at - 1, rows(k)]
            if at < levels + 1:
                x = x + u_d[at + 1, rows(k)]
            if 1 <= at <= levels:
                applied[at - 1, cells] = x - beta * prev[at - 1, cells]
            else:
                out[at + 1, cells] = x
    up = jnp.where(even, levels + 2, 0)
    down = levels + 2 - up
    for i in range(SECOND):
        send_a[i] = out[up + i, 0:cols]
        send_b[i] = out[down + i, 0:cols]


def put_sum(rows_ref, at, acc):
    rows_ref[at : at + 1] = jnp.sum(acc, axis=0, keepdims=True)


def to_lanes(rows_ref, at):
    return jnp.sum(jnp.transpose(rows_ref[at : at + 128, :]), axis=0, keepdims=True)


def tiles(lat):
    return [slice(t, t + 128) for t in range(0, lat, 128)]


def gram_kernel(nvec, levels, cols, lat, s, v, out, sums):
    sums[...] = jnp.zeros(sums.shape, f32)
    steps = levels * (cols // CHUNK)
    block = 4

    def place(step):
        lev = step // (cols // CHUNK)
        row = pl.multiple_of((step - lev * (cols // CHUNK)) * CHUNK, CHUNK)
        return lev, pl.ds(row, CHUNK)

    for i0 in range(0, nvec, block):
        for j0 in range(i0, nvec, block):
            pairs = [(i, j) for i in range(i0, i0 + block) for j in range(j0, j0 + block) if i <= j]

            def body(step, acc, pairs=pairs, need=sorted({*range(i0, i0 + block), *range(j0, j0 + block)})):
                lev, cells = place(step)
                for t in tiles(lat):
                    held = {i: s[i, lev, cells, t] for i in need}
                    acc = tuple(x + held[i] * held[j] for x, (i, j) in zip(acc, pairs))
                return acc

            acc = lax.fori_loop(0, steps, body, tuple(jnp.zeros((CHUNK, 128), f32) for _ in pairs))
            for (i, j), x in zip(pairs, acc):
                put_sum(sums, nvec * i + j, x)

    def body_v(step, acc):
        lev, cells = place(step)
        for t in tiles(lat):
            x = v[lev, cells, t]
            acc = tuple(y + x * s[i, lev, cells, t] for i, y in enumerate(acc[:-1])) + (acc[-1] + x * x,)
        return acc

    acc = lax.fori_loop(0, steps, body_v, tuple(jnp.zeros((CHUNK, 128), f32) for _ in range(nvec + 1)))
    base = nvec * nvec
    for i in range(nvec):
        put_sum(sums, base + nvec + i, acc[i])
    put_sum(sums, base + 2 * nvec + 2, acc[nvec])
    for r in range(base // 128 + 1):
        out[r : r + 1] = to_lanes(sums, 128 * r)


def gather_kernel(nvec, levels, cols, lat, count, part, got_a, got_b, v, s, gram, applied, msg, sums):
    level = lax.axis_index("lev")
    has = (level > 0, level < lax.axis_size("lev") - 1)
    even = even_level()
    for k in range(cols // CHUNK):
        cells = slice(CHUNK * k, CHUNK * (k + 1))
        for i in range(SECOND):
            a, b = got_a[i, cells], got_b[i, cells]
            below, above = jnp.where(even, b, a), jnp.where(even, a, b)
            applied[i, cells] = part[i, cells] + jnp.where(has[0], below, 0.0)
            top = levels - SECOND + i
            applied[top, cells] = part[top, cells] + jnp.where(has[1], above, 0.0)
    sums[...] = jnp.zeros(sums.shape, f32)
    steps = levels * (cols // CHUNK)

    def body(step, acc):
        lev = step // (cols // CHUNK)
        cells = pl.ds(pl.multiple_of((step - lev * (cols // CHUNK)) * CHUNK, CHUNK), CHUNK)
        for t in tiles(lat):
            x = applied[lev, cells, t]
            acc = tuple(y + x * s[i, lev, cells, t] for i, y in enumerate(acc[:nvec])) + (
                acc[nvec] + x * x,
                acc[nvec + 1] + x * v[lev, cells, t],
            )
        return acc

    acc = lax.fori_loop(0, steps, body, tuple(jnp.zeros((CHUNK, 128), f32) for _ in range(nvec + 2)))
    for i in range(nvec):
        put_sum(sums, i, acc[i])
    put_sum(sums, 2 * nvec, acc[nvec])
    put_sum(sums, 2 * nvec + 1, acc[nvec + 1])
    r = gram.shape[0] - 1
    row = to_lanes(sums, 0) + gram[r : r + 1]
    msg[:, 0:r] = jnp.broadcast_to(gram[0:r][None], (count, r, 128))
    msg[:, r : r + 1] = jnp.broadcast_to(row[None], (count, 1, 128))


def finish_kernel(nvec, levels, cols, lat, cells_all, count, msg, applied, v, s, result, coefs, trust):
    total = jnp.sum(msg[...], axis=0) * (1.0 / cells_all)
    r = total.shape[0] - 1
    row = total[r : r + 1]
    aa = row[:, 2 * nvec : 2 * nvec + 1]
    alpha = row[:, 2 * nvec + 1 : 2 * nvec + 2]
    vv = row[:, 2 * nvec + 2 : 2 * nvec + 3]
    lanes = lane_iota((1, 128))
    pv = row - alpha * pltpu.roll(row, 128 - nvec, 1)
    p = [jnp.broadcast_to(pv[:, k : k + 1], (1, 128)) for k in range(nvec)]
    tiled = jnp.zeros((1, 128), f32)
    for k in range(nvec):
        tiled = jnp.where(lax.rem(lanes, nvec) == k, p[k], tiled)
    quad = jnp.zeros((1, 128), f32)
    per = 128 // nvec
    for g in range(r):
        rep = jnp.zeros((1, 128), f32)
        for i in range(per):
            rep = jnp.where(lanes // nvec == i, p[g * per + i], rep)
        i, j = g * per + lanes // nvec, lax.rem(lanes, nvec)
        weight = jnp.where(i == j, 1.0, jnp.where(i < j, 2.0, 0.0))
        quad = quad + weight * rep * tiled * total[g : g + 1]
    quad = jnp.sum(quad, axis=1, keepdims=True)
    pp = jnp.sum(jnp.where(lanes < nvec, pv * pv, 0.0), axis=1, keepdims=True)
    square = (aa - 2.0 * alpha * alpha + alpha * alpha * vv) + (quad - 2.0 * pp)
    size = aa + alpha * alpha * (2.0 + vv) + 2.0 * pp + jnp.abs(quad)
    trust[...] = jnp.where((square > 0.03125 * size) & (size < 1e36), 1.0, 0.0)
    beta = jnp.sqrt(square + 1e-12)
    inverse = 1.0 / beta
    line = jnp.where(lanes == 0, alpha, jnp.where(lanes == 1, beta, pltpu.roll(pv, 2, 1)))
    coefs[...] = line[:, 0 : nvec + 2]
    weights = [jnp.broadcast_to(x * inverse, (CHUNK, 128)) for x in p]
    a_w = jnp.broadcast_to(alpha * inverse, (CHUNK, 128))
    scale = jnp.broadcast_to(inverse, (CHUNK, 128))

    def body(step, carry):
        lev = step // (cols // CHUNK)
        at = pl.ds(pl.multiple_of((step - lev * (cols // CHUNK)) * CHUNK, CHUNK), CHUNK)
        for t in tiles(lat):
            x = scale * applied[lev, at, t] - a_w * v[lev, at, t]
            y = weights[0] * s[0, lev, at, t]
            for k in range(1, nvec):
                y = y + weights[k] * s[k, lev, at, t]
            result[lev, at, t] = x - y
        return carry

    lax.fori_loop(0, levels * (cols // CHUNK), body, 0)


def body(v, prev, beta_prev, s, vel, lw, owner):
    lon_n, lev_n = lax.axis_size("lon"), lax.axis_size("lev")
    count = lon_n * lev_n
    levels, cols, lat = v.shape
    nvec = s.shape[0]
    lines = levels * LEVEL_ROWS + B_ROWS
    lines += -lines % CHUNK
    lines_b = levels * 3 * B_ROWS

    lo_a, lo_b, hi_a, hi_b, lev_a, lev_b, counts = call(
        functools.partial(pack_kernel, levels, cols),
        (sds(lines, lat), sds(lines_b, lat), sds(lines, lat), sds(lines_b, lat),
         sds(5, cols, lat), sds(5, cols, lat), sds(1, 128)),
        (v, vel, owner), flops=1 << 20,
    )
    east_of = [(i, (i + 1) % lon_n) for i in range(lon_n)]
    west_of = [((i + 1) % lon_n, i) for i in range(lon_n)]
    pairs_a = [(i, i ^ 1) for i in range(lev_n)]
    pairs_b = [(i, (i + 1) % lev_n if i % 2 else (i - 1) % lev_n) for i in range(lev_n)]

    def both(a, b):
        return lax.ppermute(a, "lev", pairs_a), lax.ppermute(b, "lev", pairs_b)

    def across(x, k):
        return lax.ppermute(x, "lon", [(i, i ^ k) for i in range(lon_n)])

    west, east = lax.ppermute(hi_a, "lon", east_of), lax.ppermute(lo_a, "lon", west_of)
    lev_a, lev_b = both(lev_a, lev_b)
    near = [counts] + [across(counts, k) for k in (1, 2, 3)]
    west_b, east_b = lax.ppermute(hi_b, "lon", east_of), lax.ppermute(lo_b, "lon", west_of)

    gram_rows = nvec * nvec // 128 + 1
    gram = call(
        functools.partial(gram_kernel, nvec, levels, cols, lat),
        sds(gram_rows, 128), (s, v),
        scratch=[pltpu.VMEM((128 * gram_rows, 128), f32)], flops=20 << 20,
    )

    halo_v, halo_a, corner_a, corner_b, counts = call(
        functools.partial(corner_kernel, levels, len(near)),
        (sds(levels, CHUNK, lat), sds(3, levels, CHUNK, lat), sds(5, CHUNK, lat), sds(5, CHUNK, lat), sds(1, 128)),
        (west, east, *near),
    )
    corner_a, corner_b = both(corner_a, corner_b)
    step = 4
    while 2 * step < lon_n:
        counts = counts + across(counts, step)
        step *= 2
    near = [counts, across(counts, step)]

    padded = cols + 3 * CHUNK
    scratch = [
        pltpu.VMEM((levels + 4, padded, lat), f32),
        pltpu.VMEM((2, 3, cols + CHUNK, lat), f32),
        pltpu.VMEM((levels + 2, padded, lat), f32),
        pltpu.VMEM((3, levels, CHUNK, lat), f32),
        pltpu.VMEM((CHUNK, lat), f32),
    ]
    scratch += [pltpu.VMEM((levels + 2, padded, lat), f32)] * 10
    scratch += [pltpu.VMEM((levels + 4, cols + CHUNK, lat), f32)]
    operands = (lw, beta_prev.reshape(1), v, prev, vel, owner, west, west_b, east_b, east, halo_v, halo_a,
                lev_a, lev_b, corner_a, corner_b, *near)
    part, send_a, send_b = call(
        functools.partial(stencil_kernel, levels, cols, lat, float(cols * lon_n * lat), len(near)),
        (sds(levels, cols, lat), sds(SECOND, cols, lat), sds(SECOND, cols, lat)),
        operands, specs=[SM, SM] + [VM] * (len(operands) - 2), scratch=scratch, flops=8 << 20,
    )
    got_a, got_b = both(send_a, send_b)
    applied, msg = call(
        functools.partial(gather_kernel, nvec, levels, cols, lat, count),
        (sds(levels, cols, lat), sds(count, gram_rows, 128)),
        (part, got_a, got_b, v, s, gram),
        scratch=[pltpu.VMEM((128, 128), f32)],
    )
    msg = lax.all_to_all(msg, ("lon", "lev"), 0, 0, tiled=True)
    cells = float(v.size * count)
    result, coefs, trust = call(
        functools.partial(finish_kernel, nvec, levels, cols, lat, cells, count),
        (sds(levels, cols, lat), sds(1, nvec + 2), sds(1, 1)),
        (msg, applied, v, s),
    )
    coefs = coefs.reshape(nvec + 2)

    def keep():
        return result, coefs

    def direct():
        orthogonal = applied - coefs[0] * v - jnp.sum(coefs[2:, None, None, None] * s, axis=0)
        square = lax.psum(jnp.sum(orthogonal * orthogonal), ("lon", "lev")) / cells
        beta = jnp.sqrt(square + 1e-12)
        return orthogonal / beta, jnp.concatenate([coefs[:1], beta[None], coefs[2:]])

    return lax.cond(trust[0, 0] > 0.5, keep, direct)


def solution(mesh):
    placed = (
        P("lev", "lon", None),
        P("lev", "lon", None),
        P(),
        P(None, "lev", "lon", None),
        P(None, None, "lev", "lon", None),
        P("lev"),
        P("lon", None),
    )
    return jax.shard_map(
        body, mesh=mesh, in_specs=placed, out_specs=(P("lev", "lon", None), P()), check_vma=False
    )
```

```python
import functools

import jax
import jax.numpy as jnp
from jax import lax
from jax.experimental import pallas as pl
from jax.experimental.pallas import tpu as pltpu
from jax.sharding import PartitionSpec as P

NBOX = 5
kappa = 0.1
centre = 1.0 - 6.0 * kappa
f32 = jnp.float32

VM = pl.BlockSpec(memory_space=pltpu.VMEM)
SM = pl.BlockSpec(memory_space=pltpu.SMEM)
ANY = pl.BlockSpec(memory_space=pl.ANY)
CHUNK = 8
WIDE = 4
SECOND = 2
V_ROWS, A_ROWS, B_ROWS = 4, 3, 2
LEVEL_ROWS = V_ROWS + 3 * (A_ROWS + B_ROWS)
B_AT = V_ROWS + 3 * A_ROWS


def sds(*shape):
    return jax.ShapeDtypeStruct(shape, f32)


def call(kernel, outs, operands, specs=None, scratch=(), flops=0, alias=None, out_specs=None):
    nbytes = sum(4 * x.size for x in operands)
    return pl.pallas_call(
        kernel,
        out_shape=outs,
        in_specs=specs or [VM] * len(operands),
        out_specs=out_specs or jax.tree.map(lambda _: VM, outs),
        scratch_shapes=list(scratch),
        input_output_aliases=alias or {},
        compiler_params=pltpu.CompilerParams(vmem_limit_bytes=40 << 20),
        cost_estimate=pl.CostEstimate(flops=flops, bytes_accessed=nbytes, transcendentals=0),
    )(*operands)


def lane_iota(shape):
    return lax.broadcasted_iota(jnp.int32, shape, len(shape) - 1)


def even_level():
    return lax.rem(lax.axis_index("lev"), 2) == 0


def pack_kernel(
    levels, cols, v_hbm, vel_hbm, owner_hbm, lo, hi, lev_a, lev_b, counts, v, vel, owner, sems
):
    copies = [pltpu.make_async_copy(v_hbm, v, sems.at[0]), pltpu.make_async_copy(owner_hbm, owner, sems.at[1])]
    for section in range(2):
        for comp in range(3):
            sem = sems.at[2 + 3 * section + comp]
            copies.append(pltpu.make_async_copy(vel_hbm.at[section, comp], vel.at[section, comp], sem))
    for copy in copies:
        copy.start()

    def edge(low, n):
        return slice(0, n) if low else slice(cols - n, cols)

    sides = ((lo, True), (hi, False))
    even = even_level()
    tops = ((lev_a, even), (lev_b, jnp.logical_not(even)))
    copies[0].wait()
    for msg, low in sides:
        for lev in range(levels):
            msg[lev * LEVEL_ROWS : lev * LEVEL_ROWS + V_ROWS] = v[lev, edge(low, V_ROWS)]
    for msg, top in tops:
        msg[0] = v[jnp.where(top, levels - 1, 0)]
        msg[1] = v[jnp.where(top, levels - 2, 1)]
    copies[1].wait()
    lanes = lane_iota((1, 128))
    row = jnp.zeros((1, 128), f32)
    held = owner[...]
    for box in range(1, NBOX + 1):
        hot = jnp.sum((held == box).astype(f32), axis=0, keepdims=True)
        row = jnp.where(lanes == box - 1, jnp.sum(hot, axis=1, keepdims=True), row)
    counts[...] = row
    at = levels * LEVEL_ROWS
    for msg, low in sides:
        msg[at : at + B_ROWS] = owner[edge(low, B_ROWS)].astype(f32)
        msg[at + B_ROWS : at + B_ROWS + 1, 0:128] = row
    for section, n, start in ((0, A_ROWS, V_ROWS), (1, B_ROWS, B_AT)):
        for comp in range(3):
            copies[2 + 3 * section + comp].wait()
            for msg, low in sides:
                for lev in range(levels):
                    at = lev * LEVEL_ROWS + start + comp * n
                    msg[at : at + n] = vel[section, comp, lev, edge(low, n)]
            if section == 0:
                for msg, top in tops:
                    msg[2 + comp] = vel[0, comp, jnp.where(top, levels - 1, 0)]


def corner_kernel(levels, west, east, counts, counts_2, gram, halo_v, halo_a, halo_b, corner_a, corner_b, window):
    halo_a[...] = jnp.zeros(halo_a.shape, f32)
    halo_b[...] = jnp.zeros(halo_b.shape, f32)
    for lev in range(levels):
        for msg, low in ((east, True), (west, False)):

            def edge(n):
                return slice(0, n) if low else slice(CHUNK - n, CHUNK)

            base = lev * LEVEL_ROWS
            halo_v[lev, edge(V_ROWS)] = msg[base : base + V_ROWS]
            for comp in range(3):
                at = base + V_ROWS + comp * A_ROWS
                halo_a[comp, lev, edge(A_ROWS)] = msg[at : at + A_ROWS]
                at = base + B_AT + comp * B_ROWS
                halo_b[comp, lev, edge(B_ROWS)] = msg[at : at + B_ROWS]
    even = even_level()
    for msg, top in ((corner_a, even), (corner_b, jnp.logical_not(even))):
        near = jnp.where(top, levels - 1, 0)
        msg[0] = halo_v[near]
        msg[1] = halo_v[jnp.where(top, levels - 2, 1)]
        for comp in range(3):
            msg[2 + comp] = halo_a[comp, near]
    at = levels * LEVEL_ROWS + B_ROWS
    window[...] = counts[...] + counts_2[...] + west[at : at + 1, 0:128] + east[at : at + 1, 0:128]


def stencil_kernel(
    levels, cols, lat, columns, n_counts,
    lw, beta_prev, v, prev, vel, owner, west, east, halo_v, halo_a, halo_b,
    lev_a, lev_b, corner_a, corner_b, *refs,
):
    count_refs = refs[:n_counts]
    applied, send_a, send_b = refs[n_counts : n_counts + 3]
    (vv, la, ff, own_h, w_in, w_e, w_w, w_u, w_d, u_in, u_e, u_w, u_u, u_d, out) = refs[n_counts + 3 :]
    chunks = cols // CHUNK
    level = lax.axis_index("lev")
    last = lax.axis_size("lev") - 1
    even = even_level()
    has = (level > 0, level < last)
    lanes = lane_iota((CHUNK, lat))
    first_lane, last_lane = lanes == 0, lanes == lat - 1

    def rows(k, shift=0):
        return slice(CHUNK * (k + 1) + shift, CHUNK * (k + 2) + shift)

    def put_west(ref, at, k, value):
        ref[at, rows(k)] = value
        if k == chunks:
            ref[at, 0:CHUNK] = value

    def put_east(ref, at, k, value):
        ref[at, rows(k)] = value
        if k == 0:
            ref[at, rows(chunks + 1)] = value

    def put_both(ref, at, k, value):
        put_west(ref, at, k, value)
        if k == 0:
            ref[at, rows(chunks + 1)] = value

    def from_south(x):
        return jnp.where(first_lane, 0.0, pltpu.roll(x, 1, 1))

    def from_north(x):
        return jnp.where(last_lane, 0.0, pltpu.roll(x, lat - 1, 1))

    for k in range(chunks + 1):
        cells = slice(CHUNK * k, CHUNK * (k + 1))
        got_a, got_b = (lev_a, lev_b) if k < chunks else (corner_a, corner_b)
        src = cells if k < chunks else slice(0, CHUNK)
        for item in range(5):
            a, b = got_a[item, src], got_b[item, src]
            below, above = jnp.where(even, b, a), jnp.where(even, a, b)
            if item < 2:
                put_both(vv, 1 - item, k, jnp.where(has[0], below, 0.0))
                put_both(vv, levels + 2 + item, k, jnp.where(has[1], above, 0.0))
            else:
                la[0, item - 2, cells] = below
                la[1, item - 2, cells] = above
        for lev in range(levels):
            put_both(vv, lev + 2, k, v[lev, cells] if k < chunks else halo_v[lev])
    own_h[...] = jnp.zeros(own_h.shape, f32)
    at = levels * LEVEL_ROWS
    own_h[0:B_ROWS] = east[at : at + B_ROWS]
    own_h[CHUNK - B_ROWS : CHUNK] = west[at : at + B_ROWS]

    def flow(section, k, lev):
        if k < chunks:
            return [vel[section, comp, lev, CHUNK * k : CHUNK * (k + 1)] for comp in range(3)]
        return [(halo_b if section else halo_a)[comp, lev] for comp in range(3)]

    def flow_beyond(side, k):
        return [la[side, comp, CHUNK * k : CHUNK * (k + 1)] for comp in range(3)]

    def tangent(ref, at, k, abc):
        here = ref[at, rows(k)]
        e, w = ref[at, rows(k, 1)], ref[at, rows(k, -1)]
        n, s = from_north(here), from_south(here)
        u, d = ref[at + 1, rows(k)], ref[at - 1, rows(k)]
        a, b, c = abc
        around = ((e + w) + (n + s)) + (u + d)
        drift = a * (w - e) + b * (s - n) + c * (d - u)
        return centre * here + kappa * around + 0.5 * drift

    def push(x, abc, dst, at, k):
        inside, to_e, to_w, to_u, to_d = dst
        a, b, c = abc
        base, half = kappa * x, 0.5 * x
        a, b, c = a * half, b * half, c * half
        inside[at, rows(k)] = centre * x + (from_south(base - b) + from_north(base + b))
        put_west(to_e, at, k, base - a)
        put_east(to_w, at, k, base + a)
        to_u[at, rows(k)] = base - c
        to_d[at, rows(k)] = base + c

    for k in range(chunks + 1):
        for side, at in ((0, 0), (1, levels + 1)):
            value = tangent(vv, at + 1, k, flow_beyond(side, k))
            put_both(ff, at, k, jnp.where(has[side], value, 0.0))

    def first_level(lev, carry):
        for k in range(chunks + 1):
            put_both(ff, lev + 1, k, tangent(vv, lev + 2, k, flow(0, k, lev)))
        return carry

    lax.fori_loop(0, levels, first_level, 0)

    total = count_refs[0][...]
    for ref in count_refs[1:]:
        total = total + ref[...]
    scales = columns / (NBOX * jnp.maximum(total, 1.0))
    for k in range(chunks + 1):
        mine = owner[CHUNK * k : CHUNK * (k + 1)].astype(f32) if k < chunks else own_h[...]
        factor = jnp.zeros((CHUNK, lat), f32)
        for box in range(1, NBOX + 1):
            factor = jnp.where(mine == float(box), jnp.broadcast_to(scales[:, box - 1 : box], (CHUNK, lat)), factor)
        out[0, CHUNK * k : CHUNK * (k + 1)] = factor

    def second_level(lev, carry):
        weight = lw[lev]
        for k in range(chunks + 1):
            abc = flow(1, k, lev)
            x = tangent(ff, lev + 1, k, abc)
            x = (weight * out[0, CHUNK * k : CHUNK * (k + 1)]) * x
            push(x, abc, (w_in, w_e, w_w, w_u, w_d), lev + 1, k)
        return carry

    lax.fori_loop(0, levels, second_level, 0)
    for k in range(chunks + 1):
        w_u[0, rows(k)] = jnp.zeros((CHUNK, lat), f32)
        w_d[levels + 1, rows(k)] = jnp.zeros((CHUNK, lat), f32)

    def third_level(lev, carry):
        for k in range(chunks + 1):
            x = (
                w_in[lev + 1, rows(k)]
                + (w_e[lev + 1, rows(k, -1)] + w_w[lev + 1, rows(k, 1)])
                + (w_u[lev, rows(k)] + w_d[lev + 2, rows(k)])
            )
            push(x, flow(0, k, lev), (u_in, u_e, u_w, u_u, u_d), lev + 1, k)
        return carry

    lax.fori_loop(0, levels, third_level, 0)
    for k in range(chunks + 1):
        for side, at, x in ((0, 0, w_d[1, rows(k)]), (1, levels + 1, w_u[levels, rows(k)])):
            x = jnp.where(has[side], x, 0.0)
            push(x, flow_beyond(side, k), (u_in, u_e, u_w, u_u, u_d), at, k)

    beta = beta_prev[0]
    for k in range(chunks):
        cells = slice(CHUNK * k, CHUNK * (k + 1))
        out[0, cells] = u_d[0, rows(k)]
        out[levels + 3, cells] = u_u[levels + 1, rows(k)]
        for at in range(levels + 2):
            x = u_in[at, rows(k)] + (u_e[at, rows(k, -1)] + u_w[at, rows(k, 1)])
            if at > 0:
                x = x + u_u[at - 1, rows(k)]
            if at < levels + 1:
                x = x + u_d[at + 1, rows(k)]
            if 1 <= at <= levels:
                applied[at - 1, cells] = x - beta * prev[at - 1, cells]
            else:
                out[at + 1, cells] = x
    up = jnp.where(even, levels + 2, 0)
    down = levels + 2 - up
    for i in range(SECOND):
        send_a[i] = out[up + i, 0:cols]
        send_b[i] = out[down + i, 0:cols]


def put_sum(rows_ref, at, acc):
    rows_ref[at : at + 1] = jnp.sum(acc, axis=0, keepdims=True)


def to_lanes(rows_ref, at):
    return jnp.sum(jnp.transpose(rows_ref[at : at + 128, :]), axis=0, keepdims=True)


def tiles(lat):
    return [slice(t, t + 128) for t in range(0, lat, 128)]


def gram_kernel(nvec, levels, cols, lat, s, v, prev, order, out, s_out, prev_out, sums):
    sums[...] = jnp.zeros(sums.shape, f32)
    steps = levels * (cols // CHUNK)
    block = 4

    def place(step):
        lev = step // (cols // CHUNK)
        row = pl.multiple_of((step - lev * (cols // CHUNK)) * CHUNK, CHUNK)
        return lev, pl.ds(row, CHUNK)

    for i0 in range(0, nvec, block):
        for j0 in range(i0, nvec, block):
            pairs = [(i, j) for i in range(i0, i0 + block) for j in range(j0, j0 + block) if i <= j]

            def body(step, acc, pairs=pairs, need=sorted({*range(i0, i0 + block), *range(j0, j0 + block)})):
                lev, cells = place(step)
                for t in tiles(lat):
                    held = {i: s[i, lev, cells, t] for i in need}
                    acc = tuple(x + held[i] * held[j] for x, (i, j) in zip(acc, pairs))
                return acc

            acc = lax.fori_loop(0, steps, body, tuple(jnp.zeros((CHUNK, 128), f32) for _ in pairs), unroll=4)
            for (i, j), x in zip(pairs, acc):
                put_sum(sums, nvec * i + j, x)

    def body_v(step, acc):
        lev, cells = place(step)
        for t in tiles(lat):
            x = v[lev, cells, t]
            acc = tuple(y + x * s[i, lev, cells, t] for i, y in enumerate(acc[:-1])) + (acc[-1] + x * x,)
        return acc

    acc = lax.fori_loop(0, steps, body_v, tuple(jnp.zeros((CHUNK, 128), f32) for _ in range(nvec + 1)), unroll=2)
    base = nvec * nvec
    for i in range(nvec):
        put_sum(sums, base + nvec + i, acc[i])
    put_sum(sums, base + 2 * nvec + 2, acc[nvec])
    for r in range(base // 128 + 1):
        out[r : r + 1] = to_lanes(sums, 128 * r)


def gather_kernel(nvec, levels, cols, lat, count, part, got_a, got_b, v, s, gram, applied, msg, sums):
    level = lax.axis_index("lev")
    has = (level > 0, level < lax.axis_size("lev") - 1)
    even = even_level()
    for k in range(cols // CHUNK):
        cells = slice(CHUNK * k, CHUNK * (k + 1))
        for i in range(SECOND):
            a, b = got_a[i, cells], got_b[i, cells]
            below, above = jnp.where(even, b, a), jnp.where(even, a, b)
            applied[i, cells] = part[i, cells] + jnp.where(has[0], below, 0.0)
            top = levels - SECOND + i
            applied[top, cells] = part[top, cells] + jnp.where(has[1], above, 0.0)
    sums[...] = jnp.zeros(sums.shape, f32)
    steps = levels * (cols // CHUNK)

    def body(step, acc):
        lev = step // (cols // CHUNK)
        cells = pl.ds(pl.multiple_of((step - lev * (cols // CHUNK)) * CHUNK, CHUNK), CHUNK)
        for t in tiles(lat):
            x = applied[lev, cells, t]
            acc = tuple(y + x * s[i, lev, cells, t] for i, y in enumerate(acc[:nvec])) + (
                acc[nvec] + x * x,
                acc[nvec + 1] + x * v[lev, cells, t],
            )
        return acc

    acc = lax.fori_loop(0, steps, body, tuple(jnp.zeros((CHUNK, 128), f32) for _ in range(nvec + 2)), unroll=2)
    for i in range(nvec):
        put_sum(sums, i, acc[i])
    put_sum(sums, 2 * nvec, acc[nvec])
    put_sum(sums, 2 * nvec + 1, acc[nvec + 1])
    r = gram.shape[0] - 1
    row = to_lanes(sums, 0) + gram[r : r + 1]
    msg[:, 0:r] = jnp.broadcast_to(gram[0:r][None], (count, r, 128))
    msg[:, r : r + 1] = jnp.broadcast_to(row[None], (count, 1, 128))


def finish_kernel(nvec, levels, cols, lat, cells_all, msg, applied, v, s, result_out, coefs_out, trust, result, coefs, sems):
    total = jnp.sum(msg[...], axis=0) * (1.0 / cells_all)
    r = total.shape[0] - 1
    row = total[r : r + 1]
    aa = row[:, 2 * nvec : 2 * nvec + 1]
    alpha = row[:, 2 * nvec + 1 : 2 * nvec + 2]
    vv = row[:, 2 * nvec + 2 : 2 * nvec + 3]
    lanes = lane_iota((1, 128))
    pv = row - alpha * pltpu.roll(row, 128 - nvec, 1)
    p = [jnp.broadcast_to(pv[:, k : k + 1], (1, 128)) for k in range(nvec)]
    tiled = jnp.zeros((1, 128), f32)
    for k in range(nvec):
        tiled = jnp.where(lax.rem(lanes, nvec) == k, p[k], tiled)
    quad = jnp.zeros((1, 128), f32)
    per = 128 // nvec
    for g in range(r):
        rep = jnp.zeros((1, 128), f32)
        for i in range(per):
            rep = jnp.where(lanes // nvec == i, p[g * per + i], rep)
        i, j = g * per + lanes // nvec, lax.rem(lanes, nvec)
        weight = jnp.where(i == j, 1.0, jnp.where(i < j, 2.0, 0.0))
        quad = quad + weight * rep * tiled * total[g : g + 1]
    quad = jnp.sum(quad, axis=1, keepdims=True)
    pp = jnp.sum(jnp.where(lanes < nvec, pv * pv, 0.0), axis=1, keepdims=True)
    square = (aa - 2.0 * alpha * alpha + alpha * alpha * vv) + (quad - 2.0 * pp)
    size = aa + alpha * alpha * (2.0 + vv) + 2.0 * pp + jnp.abs(quad)
    trust[...] = jnp.where((square > 0.03125 * size) & (size < 1e36), 1.0, 0.0)
    beta = jnp.sqrt(square + 1e-12)
    inverse = 1.0 / beta
    line = jnp.where(lanes == 0, alpha, jnp.where(lanes == 1, beta, pltpu.roll(pv, 2, 1)))
    coefs[...] = line[:, 0 : nvec + 2]
    copies = [pltpu.make_async_copy(result.at[lev], result_out.at[lev], sems.at[lev]) for lev in range(levels)]
    copies.append(pltpu.make_async_copy(coefs, coefs_out, sems.at[levels]))
    copies[-1].start()
    weights = [jnp.broadcast_to(x * inverse, (CHUNK, 128)) for x in p]
    a_w = jnp.broadcast_to(alpha * inverse, (CHUNK, 128))
    scale = jnp.broadcast_to(inverse, (CHUNK, 128))

    for lev in range(levels):

        def body(step, carry, lev=lev):
            at = pl.ds(pl.multiple_of(step * CHUNK, CHUNK), CHUNK)
            for t in tiles(lat):
                x = scale * applied[lev, at, t] - a_w * v[lev, at, t]
                y = weights[0] * s[0, lev, at, t]
                for k in range(1, nvec):
                    y = y + weights[k] * s[k, lev, at, t]
                result[lev, at, t] = x - y
            return carry

        lax.fori_loop(0, cols // CHUNK, body, 0)
        copies[lev].start()
    for copy in copies:
        copy.wait()


def body(v, prev, beta_prev, s, vel, lw, owner):
    lon_n, lev_n = lax.axis_size("lon"), lax.axis_size("lev")
    count = lon_n * lev_n
    levels, cols, lat = v.shape
    nvec = s.shape[0]
    lines = levels * LEVEL_ROWS + B_ROWS + 1
    lines += -lines % CHUNK

    lo, hi, lev_a, lev_b, counts, v, vel, owner = call(
        functools.partial(pack_kernel, levels, cols),
        (sds(lines, lat), sds(lines, lat), sds(5, cols, lat), sds(5, cols, lat), sds(1, 128),
         sds(*v.shape), sds(*vel.shape), jax.ShapeDtypeStruct(owner.shape, owner.dtype)),
        (v, vel, owner), specs=[ANY] * 3, scratch=[pltpu.SemaphoreType.DMA((8,))], flops=1 << 20,
    )
    east_of = [(i, (i + 1) % lon_n) for i in range(lon_n)]
    west_of = [((i + 1) % lon_n, i) for i in range(lon_n)]
    pairs_a = [(i, i ^ 1) for i in range(lev_n)]
    pairs_b = [(i, (i + 1) % lev_n if i % 2 else (i - 1) % lev_n) for i in range(lev_n)]

    def both(a, b):
        return lax.ppermute(a, "lev", pairs_a), lax.ppermute(b, "lev", pairs_b)

    west, east = lax.ppermute(hi, "lon", east_of), lax.ppermute(lo, "lon", west_of)
    lev_a, lev_b = both(lev_a, lev_b)
    counts_2 = lax.ppermute(counts, "lon", [((i + 2) % lon_n, i) for i in range(lon_n)])

    gram_rows = nvec * nvec // 128 + 1
    gram, s, prev = call(
        functools.partial(gram_kernel, nvec, levels, cols, lat),
        (sds(gram_rows, 128), sds(*s.shape), sds(*prev.shape)), (s, v, prev, counts),
        scratch=[pltpu.VMEM((128 * gram_rows, 128), f32)], flops=20 << 20, alias={0: 1, 2: 2},
    )

    halo_v, halo_a, halo_b, corner_a, corner_b, window = call(
        functools.partial(corner_kernel, levels),
        (sds(levels, CHUNK, lat), sds(3, levels, CHUNK, lat), sds(3, levels, CHUNK, lat),
         sds(5, CHUNK, lat), sds(5, CHUNK, lat), sds(1, 128)),
        (west, east, counts, counts_2, gram),
    )
    corner_a, corner_b = both(corner_a, corner_b)
    if lon_n == 8:
        near = [window, lax.ppermute(window, "lon", [(i, i ^ 4) for i in range(lon_n)])]
    else:
        near = [lax.psum(counts, "lon")]

    padded = cols + 3 * CHUNK
    scratch = [
        pltpu.VMEM((levels + 4, padded, lat), f32),
        pltpu.VMEM((2, 3, cols + CHUNK, lat), f32),
        pltpu.VMEM((levels + 2, padded, lat), f32),
        pltpu.VMEM((CHUNK, lat), f32),
    ]
    scratch += [pltpu.VMEM((levels + 2, padded, lat), f32)] * 10
    scratch += [pltpu.VMEM((levels + 4, cols + CHUNK, lat), f32)]
    operands = (lw, beta_prev.reshape(1), v, prev, vel, owner, west, east, halo_v, halo_a, halo_b,
                lev_a, lev_b, corner_a, corner_b, *near)
    part, send_a, send_b = call(
        functools.partial(stencil_kernel, levels, cols, lat, float(cols * lon_n * lat), len(near)),
        (sds(levels, cols, lat), sds(SECOND, cols, lat), sds(SECOND, cols, lat)),
        operands, specs=[SM, SM] + [VM] * (len(operands) - 2), scratch=scratch, flops=8 << 20,
    )
    got_a, got_b = both(send_a, send_b)
    applied, msg = call(
        functools.partial(gather_kernel, nvec, levels, cols, lat, count),
        (sds(levels, cols, lat), sds(count, gram_rows, 128)),
        (part, got_a, got_b, v, s, gram),
        scratch=[pltpu.VMEM((128, 128), f32)],
    )
    msg = lax.all_to_all(msg, ("lon", "lev"), 0, 0, tiled=True)
    cells = float(v.size * count)
    result, coefs, trust = call(
        functools.partial(finish_kernel, nvec, levels, cols, lat, cells),
        (sds(levels, cols, lat), sds(1, nvec + 2), sds(1, 1)),
        (msg, applied, v, s), out_specs=(ANY, ANY, VM),
        scratch=[pltpu.VMEM((levels, cols, lat), f32), pltpu.VMEM((1, nvec + 2), f32),
                 pltpu.SemaphoreType.DMA((levels + 1,))],
    )
    coefs = coefs.reshape(nvec + 2)

    def keep():
        return result, coefs

    def direct():
        orthogonal = applied - coefs[0] * v - jnp.sum(coefs[2:, None, None, None] * s, axis=0)
        square = lax.psum(jnp.sum(orthogonal * orthogonal), ("lon", "lev")) / cells
        beta = jnp.sqrt(square + 1e-12)
        return orthogonal / beta, jnp.concatenate([coefs[:1], beta[None], coefs[2:]])

    return lax.cond(trust[0, 0] > 0.5, keep, direct)


def solution(mesh):
    placed = (
        P("lev", "lon", None),
        P("lev", "lon", None),
        P(),
        P(None, "lev", "lon", None),
        P(None, None, "lev", "lon", None),
        P("lev"),
        P("lon", None),
    )
    return jax.shard_map(
        body, mesh=mesh, in_specs=placed, out_specs=(P("lev", "lon", None), P()), check_vma=False
    )
```

```python
import functools

import jax
import jax.numpy as jnp
from jax import lax
from jax.experimental import pallas as pl
from jax.experimental.pallas import tpu as pltpu
from jax.sharding import PartitionSpec as P

NBOX = 5
kappa = 0.1
centre = 1.0 - 6.0 * kappa
f32 = jnp.float32

VM = pl.BlockSpec(memory_space=pltpu.VMEM)
SM = pl.BlockSpec(memory_space=pltpu.SMEM)
HBM = pl.BlockSpec(memory_space=pltpu.HBM)
CHUNK = 8
WIDE = 4
SECOND = 2
V_ROWS, A_ROWS, B_ROWS = 4, 3, 2
LEVEL_ROWS = V_ROWS + 3 * (A_ROWS + B_ROWS)
B_AT = V_ROWS + 3 * A_ROWS


def sds(*shape):
    return jax.ShapeDtypeStruct(shape, f32)


def call(kernel, outs, operands, specs=None, scratch=(), flops=0, alias=None, out_specs=None):
    nbytes = sum(4 * x.size for x in operands)
    return pl.pallas_call(
        kernel,
        out_shape=outs,
        in_specs=specs or [VM] * len(operands),
        out_specs=out_specs or jax.tree.map(lambda _: VM, outs),
        scratch_shapes=list(scratch),
        input_output_aliases=alias or {},
        compiler_params=pltpu.CompilerParams(vmem_limit_bytes=16 << 20),
        cost_estimate=pl.CostEstimate(flops=flops, bytes_accessed=nbytes, transcendentals=0),
    )(*operands)


def lane_iota(shape):
    return lax.broadcasted_iota(jnp.int32, shape, len(shape) - 1)


def even_level():
    return lax.rem(lax.axis_index("lev"), 2) == 0


def pack_kernel(levels, cols, v, vel, owner, lo, hi, lev_a, lev_b, counts, v_out, vel_out, owner_out):
    def edge(low, n):
        return slice(0, n) if low else slice(cols - n, cols)

    sides = ((lo, True), (hi, False))
    even = even_level()
    tops = ((lev_a, even), (lev_b, jnp.logical_not(even)))
    for msg, low in sides:
        for lev in range(levels):
            msg[lev * LEVEL_ROWS : lev * LEVEL_ROWS + V_ROWS] = v[lev, edge(low, V_ROWS)]
    for msg, top in tops:
        msg[0] = v[jnp.where(top, levels - 1, 0)]
        msg[1] = v[jnp.where(top, levels - 2, 1)]
    lanes = lane_iota((1, 128))
    row = jnp.zeros((1, 128), f32)
    held = owner[...]
    for box in range(1, NBOX + 1):
        hot = jnp.sum((held == box).astype(f32), axis=0, keepdims=True)
        row = jnp.where(lanes == box - 1, jnp.sum(hot, axis=1, keepdims=True), row)
    counts[...] = row
    at = levels * LEVEL_ROWS
    for msg, low in sides:
        msg[at : at + B_ROWS] = owner[edge(low, B_ROWS)].astype(f32)
        msg[at + B_ROWS : at + B_ROWS + 1, 0:128] = row
    for section, n, start in ((0, A_ROWS, V_ROWS), (1, B_ROWS, B_AT)):
        for comp in range(3):
            for msg, low in sides:
                for lev in range(levels):
                    at = lev * LEVEL_ROWS + start + comp * n
                    msg[at : at + n] = vel[section, comp, lev, edge(low, n)]
            if section == 0:
                for msg, top in tops:
                    msg[2 + comp] = vel[0, comp, jnp.where(top, levels - 1, 0)]


def corner_kernel(levels, west, east, counts, counts_2, gram, halo_v, halo_a, halo_b, corner_a, corner_b, window):
    halo_a[...] = jnp.zeros(halo_a.shape, f32)
    halo_b[...] = jnp.zeros(halo_b.shape, f32)
    for lev in range(levels):
        for msg, low in ((east, True), (west, False)):

            def edge(n):
                return slice(0, n) if low else slice(CHUNK - n, CHUNK)

            base = lev * LEVEL_ROWS
            halo_v[lev, edge(V_ROWS)] = msg[base : base + V_ROWS]
            for comp in range(3):
                at = base + V_ROWS + comp * A_ROWS
                halo_a[comp, lev, edge(A_ROWS)] = msg[at : at + A_ROWS]
                at = base + B_AT + comp * B_ROWS
                halo_b[comp, lev, edge(B_ROWS)] = msg[at : at + B_ROWS]
    even = even_level()
    for msg, top in ((corner_a, even), (corner_b, jnp.logical_not(even))):
        near = jnp.where(top, levels - 1, 0)
        msg[0] = halo_v[near]
        msg[1] = halo_v[jnp.where(top, levels - 2, 1)]
        for comp in range(3):
            msg[2 + comp] = halo_a[comp, near]
    at = levels * LEVEL_ROWS + B_ROWS
    window[...] = counts[...] + counts_2[...] + west[at : at + 1, 0:128] + east[at : at + 1, 0:128]


class Block:
    def __init__(self, levels, cols, lat):
        self.levels, self.lat, self.chunks = levels, lat, cols // CHUNK
        level = lax.axis_index("lev")
        self.has = (level > 0, level < lax.axis_size("lev") - 1)
        self.even = even_level()
        lanes = lane_iota((CHUNK, lat))
        self.first_lane, self.last_lane = lanes == 0, lanes == lat - 1

    def put_west(self, ref, at, k, value):
        ref[at, rows(k)] = value
        if k == self.chunks:
            ref[at, 0:CHUNK] = value

    def put_east(self, ref, at, k, value):
        ref[at, rows(k)] = value
        if k == 0:
            ref[at, rows(self.chunks + 1)] = value

    def put_both(self, ref, at, k, value):
        self.put_west(ref, at, k, value)
        if k == 0:
            ref[at, rows(self.chunks + 1)] = value

    def from_south(self, x):
        return jnp.where(self.first_lane, 0.0, pltpu.roll(x, 1, 1))

    def from_north(self, x):
        return jnp.where(self.last_lane, 0.0, pltpu.roll(x, self.lat - 1, 1))

    def beyond(self, got_a, got_b, src, k, vv, la):
        for item in range(5):
            a, b = got_a[item, src], got_b[item, src]
            below, above = jnp.where(self.even, b, a), jnp.where(self.even, a, b)
            if item < 2:
                self.put_both(vv, 1 - item, k, jnp.where(self.has[0], below, 0.0))
                self.put_both(vv, self.levels + 2 + item, k, jnp.where(self.has[1], above, 0.0))
            else:
                la[0, item - 2, tile(k)] = below
                la[1, item - 2, tile(k)] = above

    def tangent(self, ref, at, k, abc):
        here = ref[at, rows(k)]
        e, w = ref[at, rows(k, 1)], ref[at, rows(k, -1)]
        n, s = self.from_north(here), self.from_south(here)
        u, d = ref[at + 1, rows(k)], ref[at - 1, rows(k)]
        a, b, c = abc
        around = ((e + w) + (n + s)) + (u + d)
        drift = a * (w - e) + b * (s - n) + c * (d - u)
        return centre * here + kappa * around + 0.5 * drift

    def push(self, x, abc, dst, at, k):
        inside, to_e, to_w, to_u, to_d = dst
        a, b, c = abc
        base, half = kappa * x, 0.5 * x
        a, b, c = a * half, b * half, c * half
        inside[at, rows(k)] = centre * x + (self.from_south(base - b) + self.from_north(base + b))
        self.put_west(to_e, at, k, base - a)
        self.put_east(to_w, at, k, base + a)
        to_u[at, rows(k)] = base - c
        to_d[at, rows(k)] = base + c


def rows(k, shift=0):
    return slice(CHUNK * (k + 1) + shift, CHUNK * (k + 2) + shift)


def tile(k):
    return slice(CHUNK * k, CHUNK * (k + 1))


def first_kernel(levels, cols, lat, v, vel, halo_v, lev_a, lev_b, vv, la, ff):
    block = Block(levels, cols, lat)
    for k in range(block.chunks):
        block.beyond(lev_a, lev_b, tile(k), k, vv, la)
    for k in range(block.chunks + 1):
        for lev in range(levels):
            block.put_both(vv, lev + 2, k, v[lev, tile(k)] if k < block.chunks else halo_v[lev])

    def first_level(lev, carry):
        for k in range(block.chunks):
            abc = [vel[0, comp, lev, tile(k)] for comp in range(3)]
            block.put_both(ff, lev + 1, k, block.tangent(vv, lev + 2, k, abc))
        return carry

    lax.fori_loop(0, levels, first_level, 0)


def stencil_kernel(
    levels, cols, lat, columns, n_counts,
    lw, beta_prev, prev, vel, owner, west, east, halo_a, halo_b,
    vv_in, la_in, ff_in, corner_a, corner_b, *refs,
):
    count_refs = refs[:n_counts]
    applied, send_a, send_b, vv, la, ff = refs[n_counts : n_counts + 6]
    (own_h, w_in, w_e, w_w, w_u, w_d, u_in, u_e, u_w, u_u, u_d, out) = refs[n_counts + 6 :]
    block = Block(levels, cols, lat)
    chunks, has, even = block.chunks, block.has, block.even
    tangent, push, put_both = block.tangent, block.push, block.put_both

    block.beyond(corner_a, corner_b, slice(0, CHUNK), chunks, vv, la)
    own_h[...] = jnp.zeros(own_h.shape, f32)
    at = levels * LEVEL_ROWS
    own_h[0:B_ROWS] = east[at : at + B_ROWS]
    own_h[CHUNK - B_ROWS : CHUNK] = west[at : at + B_ROWS]

    def flow(section, k, lev):
        if k < chunks:
            return [vel[section, comp, lev, tile(k)] for comp in range(3)]
        return [(halo_b if section else halo_a)[comp, lev] for comp in range(3)]

    def flow_beyond(side, k):
        return [la[side, comp, tile(k)] for comp in range(3)]

    for k in range(chunks + 1):
        for side, at in ((0, 0), (1, levels + 1)):
            value = tangent(vv, at + 1, k, flow_beyond(side, k))
            put_both(ff, at, k, jnp.where(has[side], value, 0.0))

    def first_level(lev, carry):
        put_both(ff, lev + 1, chunks, tangent(vv, lev + 2, chunks, flow(0, chunks, lev)))
        return carry

    lax.fori_loop(0, levels, first_level, 0)

    total = count_refs[0][...]
    for ref in count_refs[1:]:
        total = total + ref[...]
    scales = columns / (NBOX * jnp.maximum(total, 1.0))
    for k in range(chunks + 1):
        mine = owner[CHUNK * k : CHUNK * (k + 1)].astype(f32) if k < chunks else own_h[...]
        factor = jnp.zeros((CHUNK, lat), f32)
        for box in range(1, NBOX + 1):
            factor = jnp.where(mine == float(box), jnp.broadcast_to(scales[:, box - 1 : box], (CHUNK, lat)), factor)
        out[0, CHUNK * k : CHUNK * (k + 1)] = factor

    def second_level(lev, carry):
        weight = lw[lev]
        for k in range(chunks + 1):
            abc = flow(1, k, lev)
            x = tangent(ff, lev + 1, k, abc)
            x = (weight * out[0, CHUNK * k : CHUNK * (k + 1)]) * x
            push(x, abc, (w_in, w_e, w_w, w_u, w_d), lev + 1, k)
        return carry

    lax.fori_loop(0, levels, second_level, 0)
    for k in range(chunks + 1):
        w_u[0, rows(k)] = jnp.zeros((CHUNK, lat), f32)
        w_d[levels + 1, rows(k)] = jnp.zeros((CHUNK, lat), f32)

    def third_level(lev, carry):
        for k in range(chunks + 1):
            x = (
                w_in[lev + 1, rows(k)]
                + (w_e[lev + 1, rows(k, -1)] + w_w[lev + 1, rows(k, 1)])
                + (w_u[lev, rows(k)] + w_d[lev + 2, rows(k)])
            )
            push(x, flow(0, k, lev), (u_in, u_e, u_w, u_u, u_d), lev + 1, k)
        return carry

    lax.fori_loop(0, levels, third_level, 0)
    for k in range(chunks + 1):
        for side, at, x in ((0, 0, w_d[1, rows(k)]), (1, levels + 1, w_u[levels, rows(k)])):
            x = jnp.where(has[side], x, 0.0)
            push(x, flow_beyond(side, k), (u_in, u_e, u_w, u_u, u_d), at, k)

    beta = beta_prev[0]
    for k in range(chunks):
        cells = slice(CHUNK * k, CHUNK * (k + 1))
        out[0, cells] = u_d[0, rows(k)]
        out[levels + 3, cells] = u_u[levels + 1, rows(k)]
        for at in range(levels + 2):
            x = u_in[at, rows(k)] + (u_e[at, rows(k, -1)] + u_w[at, rows(k, 1)])
            if at > 0:
                x = x + u_u[at - 1, rows(k)]
            if at < levels + 1:
                x = x + u_d[at + 1, rows(k)]
            if 1 <= at <= levels:
                applied[at - 1, cells] = x - beta * prev[at - 1, cells]
            else:
                out[at + 1, cells] = x
    up = jnp.where(even, levels + 2, 0)
    down = levels + 2 - up
    for i in range(SECOND):
        send_a[i] = out[up + i, 0:cols]
        send_b[i] = out[down + i, 0:cols]


def put_sum(rows_ref, at, acc):
    rows_ref[at : at + 1] = jnp.sum(acc, axis=0, keepdims=True)


def to_lanes(rows_ref, at):
    return jnp.sum(jnp.transpose(rows_ref[at : at + 128, :]), axis=0, keepdims=True)


def tiles(lat):
    return [slice(t, t + 128) for t in range(0, lat, 128)]


def gram_kernel(nvec, levels, cols, lat, s, v, prev, order, out, s_out, prev_out, sums):
    sums[...] = jnp.zeros(sums.shape, f32)
    steps = levels * (cols // CHUNK)
    block = 4

    def place(step):
        lev = step // (cols // CHUNK)
        row = pl.multiple_of((step - lev * (cols // CHUNK)) * CHUNK, CHUNK)
        return lev, pl.ds(row, CHUNK)

    for i0 in range(0, nvec, block):
        for j0 in range(i0, nvec, block):
            pairs = [(i, j) for i in range(i0, i0 + block) for j in range(j0, j0 + block) if i <= j]

            def body(step, acc, pairs=pairs, need=sorted({*range(i0, i0 + block), *range(j0, j0 + block)})):
                lev, cells = place(step)
                for t in tiles(lat):
                    held = {i: s[i, lev, cells, t] for i in need}
                    acc = tuple(x + held[i] * held[j] for x, (i, j) in zip(acc, pairs))
                return acc

            acc = lax.fori_loop(0, steps, body, tuple(jnp.zeros((CHUNK, 128), f32) for _ in pairs), unroll=4)
            for (i, j), x in zip(pairs, acc):
                put_sum(sums, nvec * i + j, x)

    def body_v(step, acc):
        lev, cells = place(step)
        for t in tiles(lat):
            x = v[lev, cells, t]
            acc = tuple(y + x * s[i, lev, cells, t] for i, y in enumerate(acc[:-1])) + (acc[-1] + x * x,)
        return acc

    acc = lax.fori_loop(0, steps, body_v, tuple(jnp.zeros((CHUNK, 128), f32) for _ in range(nvec + 1)), unroll=2)
    base = nvec * nvec
    for i in range(nvec):
        put_sum(sums, base + nvec + i, acc[i])
    put_sum(sums, base + 2 * nvec + 2, acc[nvec])
    for r in range(base // 128 + 1):
        out[r : r + 1] = to_lanes(sums, 128 * r)


def gather_kernel(nvec, levels, cols, lat, count, part, got_a, got_b, v, s, gram, applied, msg, sums):
    level = lax.axis_index("lev")
    has = (level > 0, level < lax.axis_size("lev") - 1)
    even = even_level()
    for k in range(cols // CHUNK):
        cells = slice(CHUNK * k, CHUNK * (k + 1))
        for i in range(SECOND):
            a, b = got_a[i, cells], got_b[i, cells]
            below, above = jnp.where(even, b, a), jnp.where(even, a, b)
            applied[i, cells] = part[i, cells] + jnp.where(has[0], below, 0.0)
            top = levels - SECOND + i
            applied[top, cells] = part[top, cells] + jnp.where(has[1], above, 0.0)
    sums[...] = jnp.zeros(sums.shape, f32)
    steps = levels * (cols // CHUNK)

    def body(step, acc):
        lev = step // (cols // CHUNK)
        cells = pl.ds(pl.multiple_of((step - lev * (cols // CHUNK)) * CHUNK, CHUNK), CHUNK)
        for t in tiles(lat):
            x = applied[lev, cells, t]
            acc = tuple(y + x * s[i, lev, cells, t] for i, y in enumerate(acc[:nvec])) + (
                acc[nvec] + x * x,
                acc[nvec + 1] + x * v[lev, cells, t],
            )
        return acc

    acc = lax.fori_loop(0, steps, body, tuple(jnp.zeros((CHUNK, 128), f32) for _ in range(nvec + 2)), unroll=2)
    for i in range(nvec):
        put_sum(sums, i, acc[i])
    put_sum(sums, 2 * nvec, acc[nvec])
    put_sum(sums, 2 * nvec + 1, acc[nvec + 1])
    r = gram.shape[0] - 1
    row = to_lanes(sums, 0) + gram[r : r + 1]
    msg[:, 0:r] = jnp.broadcast_to(gram[0:r][None], (count, r, 128))
    msg[:, r : r + 1] = jnp.broadcast_to(row[None], (count, 1, 128))


def scalar_kernel(nvec, cells_all, msg, out, trust):
    total = jnp.sum(msg[...], axis=0) * (1.0 / cells_all)
    r = total.shape[0] - 1
    row = total[r : r + 1]
    aa = row[:, 2 * nvec : 2 * nvec + 1]
    alpha = row[:, 2 * nvec + 1 : 2 * nvec + 2]
    vv = row[:, 2 * nvec + 2 : 2 * nvec + 3]
    lanes = lane_iota((1, 128))
    pv = row - alpha * pltpu.roll(row, 128 - nvec, 1)
    p = [jnp.broadcast_to(pv[:, k : k + 1], (1, 128)) for k in range(nvec)]
    tiled = jnp.zeros((1, 128), f32)
    for k in range(nvec):
        tiled = jnp.where(lax.rem(lanes, nvec) == k, p[k], tiled)
    quad = jnp.zeros((1, 128), f32)
    per = 128 // nvec
    for g in range(r):
        rep = jnp.zeros((1, 128), f32)
        for i in range(per):
            rep = jnp.where(lanes // nvec == i, p[g * per + i], rep)
        i, j = g * per + lanes // nvec, lax.rem(lanes, nvec)
        weight = jnp.where(i == j, 1.0, jnp.where(i < j, 2.0, 0.0))
        quad = quad + weight * rep * tiled * total[g : g + 1]
    quad = jnp.sum(quad, axis=1, keepdims=True)
    pp = jnp.sum(jnp.where(lanes < nvec, pv * pv, 0.0), axis=1, keepdims=True)
    square = (aa - 2.0 * alpha * alpha + alpha * alpha * vv) + (quad - 2.0 * pp)
    size = aa + alpha * alpha * (2.0 + vv) + 2.0 * pp + jnp.abs(quad)
    trust[...] = jnp.where((square > 0.03125 * size) & (size < 1e36), 1.0, 0.0)
    beta = jnp.sqrt(square + 1e-12)
    out[...] = jnp.where(lanes == 0, alpha, jnp.where(lanes == 1, beta, pltpu.roll(pv, 2, 1)))


def finish_kernel(nvec, levels, cols, lat, row, applied, v, s, result_out, coefs_out, result, coefs, sems):
    line = row[...]
    coefs[...] = line[:, 0 : nvec + 2]
    inverse = 1.0 / line[:, 1:2]
    a_w = jnp.broadcast_to(line[:, 0:1] * inverse, (CHUNK, 128))
    scale = jnp.broadcast_to(inverse, (CHUNK, 128))
    weights = [jnp.broadcast_to(line[:, 2 + k : 3 + k] * inverse, (CHUNK, 128)) for k in range(nvec)]
    copies = [pltpu.make_async_copy(result.at[lev], result_out.at[lev], sems.at[lev]) for lev in range(levels)]
    copies.append(pltpu.make_async_copy(coefs, coefs_out, sems.at[levels]))
    copies[-1].start()

    for lev in range(levels):

        def body(step, carry, lev=lev):
            at = pl.ds(pl.multiple_of(step * CHUNK, CHUNK), CHUNK)
            for t in tiles(lat):
                x = scale * applied[lev, at, t] - a_w * v[lev, at, t]
                y = weights[0] * s[0, lev, at, t]
                for k in range(1, nvec):
                    y = y + weights[k] * s[k, lev, at, t]
                result[lev, at, t] = x - y
            return carry

        lax.fori_loop(0, cols // CHUNK, body, 0)
        copies[lev].start()
    for copy in copies:
        copy.wait()


def body(v, prev, beta_prev, s, vel, lw, owner):
    lon_n, lev_n = lax.axis_size("lon"), lax.axis_size("lev")
    count = lon_n * lev_n
    levels, cols, lat = v.shape
    nvec = s.shape[0]
    lines = levels * LEVEL_ROWS + B_ROWS + 1
    lines += -lines % CHUNK

    lo, hi, lev_a, lev_b, counts, v, vel, owner = call(
        functools.partial(pack_kernel, levels, cols),
        (sds(lines, lat), sds(lines, lat), sds(5, cols, lat), sds(5, cols, lat), sds(1, 128),
         sds(*v.shape), sds(*vel.shape), jax.ShapeDtypeStruct(owner.shape, owner.dtype)),
        (v, vel, owner), flops=1 << 20, alias={0: 5, 1: 6, 2: 7},
    )
    east_of = [(i, (i + 1) % lon_n) for i in range(lon_n)]
    west_of = [((i + 1) % lon_n, i) for i in range(lon_n)]
    pairs_a = [(i, i ^ 1) for i in range(lev_n)]
    pairs_b = [(i, (i + 1) % lev_n if i % 2 else (i - 1) % lev_n) for i in range(lev_n)]

    def both(a, b):
        return lax.ppermute(a, "lev", pairs_a), lax.ppermute(b, "lev", pairs_b)

    west, east = lax.ppermute(hi, "lon", east_of), lax.ppermute(lo, "lon", west_of)
    lev_a, lev_b = both(lev_a, lev_b)
    counts_2 = lax.ppermute(counts, "lon", [((i + 2) % lon_n, i) for i in range(lon_n)])

    gram_rows = nvec * nvec // 128 + 1
    gram, s, prev = call(
        functools.partial(gram_kernel, nvec, levels, cols, lat),
        (sds(gram_rows, 128), sds(*s.shape), sds(*prev.shape)), (s, v, prev, counts),
        scratch=[pltpu.VMEM((128 * gram_rows, 128), f32)], flops=20 << 20, alias={0: 1, 2: 2},
    )

    halo_v, halo_a, halo_b, corner_a, corner_b, window = call(
        functools.partial(corner_kernel, levels),
        (sds(levels, CHUNK, lat), sds(3, levels, CHUNK, lat), sds(3, levels, CHUNK, lat),
         sds(5, CHUNK, lat), sds(5, CHUNK, lat), sds(1, 128)),
        (west, east, counts, counts_2, gram),
    )
    if lon_n == 8:
        near = [window, lax.ppermute(window, "lon", [(i, i ^ 4) for i in range(lon_n)])]
    else:
        near = [lax.psum(counts, "lon")]
    corner_a, corner_b = both(corner_a, corner_b)

    padded = cols + 3 * CHUNK
    state = (sds(levels + 4, padded, lat), sds(2, 3, cols + CHUNK, lat), sds(levels + 2, padded, lat))
    state = call(
        functools.partial(first_kernel, levels, cols, lat), state, (v, vel, halo_v, lev_a, lev_b), flops=4 << 20
    )
    scratch = [pltpu.VMEM((CHUNK, lat), f32)]
    scratch += [pltpu.VMEM((levels + 2, padded, lat), f32)] * 10
    scratch += [pltpu.VMEM((levels + 4, cols + CHUNK, lat), f32)]
    operands = (lw, beta_prev.reshape(1), prev, vel, owner, west, east, halo_a, halo_b, *state,
                corner_a, corner_b, *near)
    part, send_a, send_b = call(
        functools.partial(stencil_kernel, levels, cols, lat, float(cols * lon_n * lat), len(near)),
        (sds(levels, cols, lat), sds(SECOND, cols, lat), sds(SECOND, cols, lat), *(sds(*x.shape) for x in state)),
        operands, specs=[SM, SM] + [VM] * (len(operands) - 2), scratch=scratch, flops=8 << 20,
        alias={9: 3, 10: 4, 11: 5},
    )[:3]
    got_a, got_b = both(send_a, send_b)
    applied, msg = call(
        functools.partial(gather_kernel, nvec, levels, cols, lat, count),
        (sds(levels, cols, lat), sds(count, gram_rows, 128)),
        (part, got_a, got_b, v, s, gram),
        scratch=[pltpu.VMEM((128, 128), f32)],
    )
    msg = lax.all_to_all(msg, ("lon", "lev"), 0, 0, tiled=True)
    cells = float(v.size * count)
    row, trust = call(functools.partial(scalar_kernel, nvec, cells), (sds(1, 128), sds(1, 1)), (msg,))

    def direct():
        weights = row[0, 2 : nvec + 2]
        orthogonal = applied - row[0, 0] * v - jnp.sum(weights[:, None, None, None] * s, axis=0)
        square = lax.psum(jnp.sum(orthogonal * orthogonal), ("lon", "lev")) / cells
        return row.at[0, 1].set(jnp.sqrt(square + 1e-12))

    row = lax.cond(trust[0, 0] > 0.5, lambda: row, direct)
    result, coefs = call(
        functools.partial(finish_kernel, nvec, levels, cols, lat),
        (sds(levels, cols, lat), sds(1, nvec + 2)),
        (row, applied, v, s), out_specs=(HBM, HBM),
        scratch=[pltpu.VMEM((levels, cols, lat), f32), pltpu.VMEM((1, nvec + 2), f32),
                 pltpu.SemaphoreType.DMA((levels + 1,))],
    )
    return result, coefs.reshape(nvec + 2)


def solution(mesh):
    placed = (
        P("lev", "lon", None),
        P("lev", "lon", None),
        P(),
        P(None, "lev", "lon", None),
        P(None, None, "lev", "lon", None),
        P("lev"),
        P("lon", None),
    )
    return jax.shard_map(
        body, mesh=mesh, in_specs=placed, out_specs=(P("lev", "lon", None), P()), check_vma=False
    )
```

```python
import functools

import jax
import jax.numpy as jnp
from jax import lax
from jax.experimental import pallas as pl
from jax.experimental.pallas import tpu as pltpu
from jax.sharding import PartitionSpec as P

NBOX = 5
kappa = 0.1
centre = 1.0 - 6.0 * kappa
f32 = jnp.float32

VM = pl.BlockSpec(memory_space=pltpu.VMEM)
SM = pl.BlockSpec(memory_space=pltpu.SMEM)
HBM = pl.BlockSpec(memory_space=pltpu.HBM)
CHUNK = 8
WIDE = 4
SECOND = 2
V_ROWS, A_ROWS, B_ROWS = 4, 3, 2
LEVEL_ROWS = V_ROWS + 3 * (A_ROWS + B_ROWS)
B_AT = V_ROWS + 3 * A_ROWS


def sds(*shape):
    return jax.ShapeDtypeStruct(shape, f32)


def call(kernel, outs, operands, specs=None, scratch=(), flops=0, alias=None, out_specs=None):
    nbytes = sum(4 * x.size for x in operands)
    return pl.pallas_call(
        kernel,
        out_shape=outs,
        in_specs=specs or [VM] * len(operands),
        out_specs=out_specs or jax.tree.map(lambda _: VM, outs),
        scratch_shapes=list(scratch),
        input_output_aliases=alias or {},
        compiler_params=pltpu.CompilerParams(vmem_limit_bytes=16 << 20),
        cost_estimate=pl.CostEstimate(flops=flops, bytes_accessed=nbytes, transcendentals=0),
    )(*operands)


def lane_iota(shape):
    return lax.broadcasted_iota(jnp.int32, shape, len(shape) - 1)


def even_level():
    return lax.rem(lax.axis_index("lev"), 2) == 0


def pack_kernel(levels, cols, v_hbm, vel_hbm, owner_hbm, lo, hi, lev_a, lev_b, counts, v, vel, owner, sems):
    copies = [pltpu.make_async_copy(v_hbm, v, sems.at[0]), pltpu.make_async_copy(owner_hbm, owner, sems.at[1])]
    for section in range(2):
        for comp in range(3):
            sem = sems.at[2 + 3 * section + comp]
            copies.append(pltpu.make_async_copy(vel_hbm.at[section, comp], vel.at[section, comp], sem))
    for copy in copies:
        copy.start()

    def edge(low, n):
        return slice(0, n) if low else slice(cols - n, cols)

    sides = ((lo, True), (hi, False))
    even = even_level()
    tops = ((lev_a, even), (lev_b, jnp.logical_not(even)))
    copies[0].wait()
    for msg, low in sides:
        for lev in range(levels):
            msg[lev * LEVEL_ROWS : lev * LEVEL_ROWS + V_ROWS] = v[lev, edge(low, V_ROWS)]
    for msg, top in tops:
        msg[0] = v[jnp.where(top, levels - 1, 0)]
        msg[1] = v[jnp.where(top, levels - 2, 1)]
    copies[1].wait()
    lanes = lane_iota((1, 128))
    row = jnp.zeros((1, 128), f32)
    held = owner[...]
    for box in range(1, NBOX + 1):
        hot = jnp.sum((held == box).astype(f32), axis=0, keepdims=True)
        row = jnp.where(lanes == box - 1, jnp.sum(hot, axis=1, keepdims=True), row)
    counts[...] = row
    at = levels * LEVEL_ROWS
    for msg, low in sides:
        msg[at : at + B_ROWS] = owner[edge(low, B_ROWS)].astype(f32)
        msg[at + B_ROWS : at + B_ROWS + 1, 0:128] = row
    for section, n, start in ((0, A_ROWS, V_ROWS), (1, B_ROWS, B_AT)):
        for comp in range(3):
            copies[2 + 3 * section + comp].wait()
            for msg, low in sides:
                for lev in range(levels):
                    at = lev * LEVEL_ROWS + start + comp * n
                    msg[at : at + n] = vel[section, comp, lev, edge(low, n)]
            if section == 0:
                for msg, top in tops:
                    msg[2 + comp] = vel[0, comp, jnp.where(top, levels - 1, 0)]


def unpack(west, east, n, at):
    gap = jnp.zeros((CHUNK - 2 * n, west.shape[1]), f32)
    parts = [east[at : at + n], gap, west[at : at + n]]
    return jnp.concatenate([x for x in parts if x.shape[0]], axis=0)


def corner_kernel(levels, west, east, counts, counts_2, gram, corner_a, corner_b, window):
    even = even_level()

    def put(item, top, bottom):
        corner_a[item] = jnp.where(even, top, bottom)
        corner_b[item] = jnp.where(even, bottom, top)

    def both(n, start, near=0):
        return [unpack(west, east, n, lev * LEVEL_ROWS + start) for lev in (levels - 1 - near, near)]

    put(0, *both(V_ROWS, 0))
    put(1, *both(V_ROWS, 0, 1))
    for comp in range(3):
        put(2 + comp, *both(A_ROWS, V_ROWS + comp * A_ROWS))
    at = levels * LEVEL_ROWS + B_ROWS
    window[...] = counts[...] + counts_2[...] + west[at : at + 1, 0:128] + east[at : at + 1, 0:128]


class Block:
    def __init__(self, levels, cols, lat):
        self.levels, self.lat, self.chunks = levels, lat, cols // CHUNK
        level = lax.axis_index("lev")
        self.has = (level > 0, level < lax.axis_size("lev") - 1)
        self.even = even_level()
        lanes = lane_iota((CHUNK, lat))
        self.first_lane, self.last_lane = lanes == 0, lanes == lat - 1

    def put_west(self, ref, at, k, value):
        ref[at, rows(k)] = value
        if k == self.chunks:
            ref[at, 0:CHUNK] = value

    def put_east(self, ref, at, k, value):
        ref[at, rows(k)] = value
        if k == 0:
            ref[at, rows(self.chunks + 1)] = value

    def put_both(self, ref, at, k, value):
        self.put_west(ref, at, k, value)
        if k == 0:
            ref[at, rows(self.chunks + 1)] = value

    def from_south(self, x):
        return jnp.where(self.first_lane, 0.0, pltpu.roll(x, 1, 1))

    def from_north(self, x):
        return jnp.where(self.last_lane, 0.0, pltpu.roll(x, self.lat - 1, 1))

    def beyond(self, got_a, got_b, src, k, vv, la):
        for item in range(5):
            a, b = got_a[item, src], got_b[item, src]
            below, above = jnp.where(self.even, b, a), jnp.where(self.even, a, b)
            if item < 2:
                self.put_both(vv, 1 - item, k, jnp.where(self.has[0], below, 0.0))
                self.put_both(vv, self.levels + 2 + item, k, jnp.where(self.has[1], above, 0.0))
            else:
                la[0, item - 2, tile(k)] = below
                la[1, item - 2, tile(k)] = above

    def tangent(self, ref, at, k, abc):
        here = ref[at, rows(k)]
        e, w = ref[at, rows(k, 1)], ref[at, rows(k, -1)]
        n, s = self.from_north(here), self.from_south(here)
        u, d = ref[at + 1, rows(k)], ref[at - 1, rows(k)]
        a, b, c = abc
        around = ((e + w) + (n + s)) + (u + d)
        drift = a * (w - e) + b * (s - n) + c * (d - u)
        return centre * here + kappa * around + 0.5 * drift

    def push(self, x, abc, dst, at, k):
        inside, to_e, to_w, to_u, to_d = dst
        a, b, c = abc
        base, half = kappa * x, 0.5 * x
        a, b, c = a * half, b * half, c * half
        inside[at, rows(k)] = centre * x + (self.from_south(base - b) + self.from_north(base + b))
        self.put_west(to_e, at, k, base - a)
        self.put_east(to_w, at, k, base + a)
        to_u[at, rows(k)] = base - c
        to_d[at, rows(k)] = base + c


def rows(k, shift=0):
    return slice(CHUNK * (k + 1) + shift, CHUNK * (k + 2) + shift)


def tile(k):
    return slice(CHUNK * k, CHUNK * (k + 1))


def first_kernel(levels, cols, lat, v, vel, west, east, lev_a, lev_b, vv, la, ff, halo_a, halo_b):
    block = Block(levels, cols, lat)
    for k in range(block.chunks):
        block.beyond(lev_a, lev_b, tile(k), k, vv, la)
    for k in range(block.chunks + 1):
        for lev in range(levels):
            value = v[lev, tile(k)] if k < block.chunks else unpack(west, east, V_ROWS, lev * LEVEL_ROWS)
            block.put_both(vv, lev + 2, k, value)

    for lev in range(levels):
        for comp in range(3):
            base = lev * LEVEL_ROWS + V_ROWS
            halo_a[comp, lev] = unpack(west, east, A_ROWS, base + comp * A_ROWS)
            halo_b[comp, lev] = unpack(west, east, B_ROWS, base + 3 * A_ROWS + comp * B_ROWS)

    def first_level(lev, carry):
        for k in range(block.chunks):
            abc = [vel[0, comp, lev, tile(k)] for comp in range(3)]
            block.put_both(ff, lev + 1, k, block.tangent(vv, lev + 2, k, abc))
        return carry

    lax.fori_loop(0, levels, first_level, 0)


def stencil_kernel(
    levels, cols, lat, columns, n_counts,
    lw, beta_prev, prev, vel, owner, west, east, halo_a, halo_b,
    vv_in, la_in, ff_in, corner_a, corner_b, *refs,
):
    count_refs = refs[:n_counts]
    applied, send_a, send_b, vv, la, ff = refs[n_counts : n_counts + 6]
    (own_h, w_in, w_e, w_w, w_u, w_d, u_in, u_e, u_w, u_u, u_d, out) = refs[n_counts + 6 :]
    block = Block(levels, cols, lat)
    chunks, has, even = block.chunks, block.has, block.even
    tangent, push, put_both = block.tangent, block.push, block.put_both

    block.beyond(corner_a, corner_b, slice(0, CHUNK), chunks, vv, la)
    own_h[...] = unpack(west, east, B_ROWS, levels * LEVEL_ROWS)

    def flow(section, k, lev):
        if k < chunks:
            return [vel[section, comp, lev, tile(k)] for comp in range(3)]
        return [(halo_b if section else halo_a)[comp, lev] for comp in range(3)]

    def flow_beyond(side, k):
        return [la[side, comp, tile(k)] for comp in range(3)]

    for k in range(chunks + 1):
        for side, at in ((0, 0), (1, levels + 1)):
            value = tangent(vv, at + 1, k, flow_beyond(side, k))
            put_both(ff, at, k, jnp.where(has[side], value, 0.0))

    def first_level(lev, carry):
        put_both(ff, lev + 1, chunks, tangent(vv, lev + 2, chunks, flow(0, chunks, lev)))
        return carry

    lax.fori_loop(0, levels, first_level, 0)

    total = count_refs[0][...]
    for ref in count_refs[1:]:
        total = total + ref[...]
    scales = columns / (NBOX * jnp.maximum(total, 1.0))
    for k in range(chunks + 1):
        mine = owner[CHUNK * k : CHUNK * (k + 1)].astype(f32) if k < chunks else own_h[...]
        factor = jnp.zeros((CHUNK, lat), f32)
        for box in range(1, NBOX + 1):
            factor = jnp.where(mine == float(box), jnp.broadcast_to(scales[:, box - 1 : box], (CHUNK, lat)), factor)
        out[0, CHUNK * k : CHUNK * (k + 1)] = factor

    def second_level(lev, carry):
        weight = lw[lev]
        for k in range(chunks + 1):
            abc = flow(1, k, lev)
            x = tangent(ff, lev + 1, k, abc)
            x = (weight * out[0, CHUNK * k : CHUNK * (k + 1)]) * x
            push(x, abc, (w_in, w_e, w_w, w_u, w_d), lev + 1, k)
        return carry

    lax.fori_loop(0, levels, second_level, 0)
    for k in range(chunks + 1):
        w_u[0, rows(k)] = jnp.zeros((CHUNK, lat), f32)
        w_d[levels + 1, rows(k)] = jnp.zeros((CHUNK, lat), f32)

    def third_level(lev, carry):
        for k in range(chunks + 1):
            x = (
                w_in[lev + 1, rows(k)]
                + (w_e[lev + 1, rows(k, -1)] + w_w[lev + 1, rows(k, 1)])
                + (w_u[lev, rows(k)] + w_d[lev + 2, rows(k)])
            )
            push(x, flow(0, k, lev), (u_in, u_e, u_w, u_u, u_d), lev + 1, k)
        return carry

    lax.fori_loop(0, levels, third_level, 0)
    for k in range(chunks + 1):
        for side, at, x in ((0, 0, w_d[1, rows(k)]), (1, levels + 1, w_u[levels, rows(k)])):
            x = jnp.where(has[side], x, 0.0)
            push(x, flow_beyond(side, k), (u_in, u_e, u_w, u_u, u_d), at, k)

    beta = jnp.broadcast_to(beta_prev[:, 0:1], (CHUNK, lat))
    for k in range(chunks):
        cells = slice(CHUNK * k, CHUNK * (k + 1))
        out[0, cells] = u_d[0, rows(k)]
        out[levels + 3, cells] = u_u[levels + 1, rows(k)]
        for at in range(levels + 2):
            x = u_in[at, rows(k)] + (u_e[at, rows(k, -1)] + u_w[at, rows(k, 1)])
            if at > 0:
                x = x + u_u[at - 1, rows(k)]
            if at < levels + 1:
                x = x + u_d[at + 1, rows(k)]
            if 1 <= at <= levels:
                applied[at - 1, cells] = x - beta * prev[at - 1, cells]
            else:
                out[at + 1, cells] = x
    up = jnp.where(even, levels + 2, 0)
    down = levels + 2 - up
    for i in range(SECOND):
        send_a[i] = out[up + i, 0:cols]
        send_b[i] = out[down + i, 0:cols]


def put_sum(rows_ref, at, acc):
    rows_ref[at : at + 1] = jnp.sum(acc, axis=0, keepdims=True)


def to_lanes(rows_ref, at):
    return jnp.sum(jnp.transpose(rows_ref[at : at + 128, :]), axis=0, keepdims=True)


def tiles(lat):
    return [slice(t, t + 128) for t in range(0, lat, 128)]


def gram_kernel(nvec, levels, cols, lat, beta_prev, s, v, order, out, beta_out, sums):
    beta_out[...] = jnp.full((1, 128), beta_prev[0], f32)
    sums[...] = jnp.zeros(sums.shape, f32)
    steps = levels * (cols // CHUNK)
    block = 4

    def place(step):
        lev = step // (cols // CHUNK)
        row = pl.multiple_of((step - lev * (cols // CHUNK)) * CHUNK, CHUNK)
        return lev, pl.ds(row, CHUNK)

    for i0 in range(0, nvec, block):
        for j0 in range(i0, nvec, block):
            pairs = [(i, j) for i in range(i0, i0 + block) for j in range(j0, j0 + block) if i <= j]

            def body(step, acc, pairs=pairs, need=sorted({*range(i0, i0 + block), *range(j0, j0 + block)})):
                lev, cells = place(step)
                for t in tiles(lat):
                    held = {i: s[i, lev, cells, t] for i in need}
                    acc = tuple(x + held[i] * held[j] for x, (i, j) in zip(acc, pairs))
                return acc

            acc = lax.fori_loop(0, steps, body, tuple(jnp.zeros((CHUNK, 128), f32) for _ in pairs), unroll=4)
            for (i, j), x in zip(pairs, acc):
                put_sum(sums, nvec * i + j, x)

    def body_v(step, acc):
        lev, cells = place(step)
        for t in tiles(lat):
            x = v[lev, cells, t]
            acc = tuple(y + x * s[i, lev, cells, t] for i, y in enumerate(acc[:-1])) + (acc[-1] + x * x,)
        return acc

    acc = lax.fori_loop(0, steps, body_v, tuple(jnp.zeros((CHUNK, 128), f32) for _ in range(nvec + 1)), unroll=2)
    base = nvec * nvec
    for i in range(nvec):
        put_sum(sums, base + nvec + i, acc[i])
    put_sum(sums, base + 2 * nvec + 2, acc[nvec])
    for r in range(base // 128 + 1):
        out[r : r + 1] = to_lanes(sums, 128 * r)


def gather_kernel(nvec, levels, cols, lat, count, part, got_a, got_b, v, s, gram, applied, msg, sums):
    level = lax.axis_index("lev")
    has = (level > 0, level < lax.axis_size("lev") - 1)
    even = even_level()
    for k in range(cols // CHUNK):
        cells = slice(CHUNK * k, CHUNK * (k + 1))
        for i in range(SECOND):
            a, b = got_a[i, cells], got_b[i, cells]
            below, above = jnp.where(even, b, a), jnp.where(even, a, b)
            applied[i, cells] = part[i, cells] + jnp.where(has[0], below, 0.0)
            top = levels - SECOND + i
            applied[top, cells] = part[top, cells] + jnp.where(has[1], above, 0.0)
    sums[...] = jnp.zeros(sums.shape, f32)
    steps = levels * (cols // CHUNK)

    def body(step, acc):
        lev = step // (cols // CHUNK)
        cells = pl.ds(pl.multiple_of((step - lev * (cols // CHUNK)) * CHUNK, CHUNK), CHUNK)
        for t in tiles(lat):
            x = applied[lev, cells, t]
            acc = tuple(y + x * s[i, lev, cells, t] for i, y in enumerate(acc[:nvec])) + (
                acc[nvec] + x * x,
                acc[nvec + 1] + x * v[lev, cells, t],
            )
        return acc

    acc = lax.fori_loop(0, steps, body, tuple(jnp.zeros((CHUNK, 128), f32) for _ in range(nvec + 2)), unroll=2)
    for i in range(nvec):
        put_sum(sums, i, acc[i])
    put_sum(sums, 2 * nvec, acc[nvec])
    put_sum(sums, 2 * nvec + 1, acc[nvec + 1])
    r = gram.shape[0] - 1
    row = to_lanes(sums, 0) + gram[r : r + 1]
    msg[:, 0:r] = jnp.broadcast_to(gram[0:r][None], (count, r, 128))
    msg[:, r : r + 1] = jnp.broadcast_to(row[None], (count, 1, 128))


def orthogonal_kernel(nvec, levels, cols, lat, cells_all, msg, applied, v, s, orthogonal, out, trust):
    total = jnp.sum(msg[...], axis=0) * (1.0 / cells_all)
    r = total.shape[0] - 1
    row = total[r : r + 1]
    aa = row[:, 2 * nvec : 2 * nvec + 1]
    alpha = row[:, 2 * nvec + 1 : 2 * nvec + 2]
    vv = row[:, 2 * nvec + 2 : 2 * nvec + 3]
    lanes = lane_iota((1, 128))
    pv = row - alpha * pltpu.roll(row, 128 - nvec, 1)
    p = [jnp.broadcast_to(pv[:, k : k + 1], (1, 128)) for k in range(nvec)]
    tiled = jnp.zeros((1, 128), f32)
    for k in range(nvec):
        tiled = jnp.where(lax.rem(lanes, nvec) == k, p[k], tiled)
    quad = jnp.zeros((1, 128), f32)
    per = 128 // nvec
    for g in range(r):
        rep = jnp.zeros((1, 128), f32)
        for i in range(per):
            rep = jnp.where(lanes // nvec == i, p[g * per + i], rep)
        i, j = g * per + lanes // nvec, lax.rem(lanes, nvec)
        weight = jnp.where(i == j, 1.0, jnp.where(i < j, 2.0, 0.0))
        quad = quad + weight * rep * tiled * total[g : g + 1]
    quad = jnp.sum(quad, axis=1, keepdims=True)
    pp = jnp.sum(jnp.where(lanes < nvec, pv * pv, 0.0), axis=1, keepdims=True)
    square = (aa - 2.0 * alpha * alpha + alpha * alpha * vv) + (quad - 2.0 * pp)
    size = aa + alpha * alpha * (2.0 + vv) + 2.0 * pp + jnp.abs(quad)
    trust[...] = jnp.where((square > 0.03125 * size) & (size < 1e36), 1.0, 0.0)
    beta = jnp.sqrt(square + 1e-12)
    out[...] = jnp.where(lanes == 0, alpha, jnp.where(lanes == 1, beta, pltpu.roll(pv, 2, 1)))


    a_w = jnp.broadcast_to(alpha, (CHUNK, 128))
    weights = [jnp.broadcast_to(x, (CHUNK, 128)) for x in p]

    def body(step, carry):
        lev = step // (cols // CHUNK)
        at = pl.ds(pl.multiple_of((step - lev * (cols // CHUNK)) * CHUNK, CHUNK), CHUNK)
        for t in tiles(lat):
            x = applied[lev, at, t] - a_w * v[lev, at, t]
            y = weights[0] * s[0, lev, at, t]
            for k in range(1, nvec):
                y = y + weights[k] * s[k, lev, at, t]
            orthogonal[lev, at, t] = x - y
        return carry

    lax.fori_loop(0, levels * (cols // CHUNK), body, 0)


def scale_kernel(nvec, row, orthogonal, result_out, coefs_out, result, coefs, sems):
    line = row[...]
    coefs[...] = line[:, 0 : nvec + 2]
    copies = [pltpu.make_async_copy(result.at[i], result_out.at[i], sems.at[i]) for i in range(result.shape[0])]
    copies.append(pltpu.make_async_copy(coefs, coefs_out, sems.at[result.shape[0]]))
    copies[-1].start()
    inverse = 1.0 / line[:, 1:2]
    for i in range(result.shape[0]):
        result[i] = orthogonal[i] * inverse
        copies[i].start()
    for copy in copies:
        copy.wait()


def body(v, prev, beta_prev, s, vel, lw, owner):
    lon_n, lev_n = lax.axis_size("lon"), lax.axis_size("lev")
    count = lon_n * lev_n
    levels, cols, lat = v.shape
    nvec = s.shape[0]
    lines = levels * LEVEL_ROWS + B_ROWS + 1
    lines += -lines % CHUNK

    lo, hi, lev_a, lev_b, counts, v, vel, owner = call(
        functools.partial(pack_kernel, levels, cols),
        (sds(lines, lat), sds(lines, lat), sds(5, cols, lat), sds(5, cols, lat), sds(1, 128),
         sds(*v.shape), sds(*vel.shape), jax.ShapeDtypeStruct(owner.shape, owner.dtype)),
        tuple(pltpu.with_memory_space_constraint(x, pltpu.HBM) for x in (v, vel, owner)), specs=[HBM] * 3, scratch=[pltpu.SemaphoreType.DMA((8,))], flops=1 << 20,
    )
    east_of = [(i, (i + 1) % lon_n) for i in range(lon_n)]
    west_of = [((i + 1) % lon_n, i) for i in range(lon_n)]
    pairs_a = [(i, i ^ 1) for i in range(lev_n)]
    pairs_b = []
    for i in range(count):
        at, level = divmod(i, lev_n)
        if level in (0, lev_n - 1):
            pairs_b.append((i, (at ^ 1) * lev_n + level))
        else:
            pairs_b.append((i, i + 1 if level % 2 else i - 1))

    def both(a, b):
        return lax.ppermute(a, "lev", pairs_a), lax.ppermute(b, ("lon", "lev"), pairs_b)

    west, east = lax.ppermute(hi, "lon", east_of), lax.ppermute(lo, "lon", west_of)
    lev_a, lev_b = both(lev_a, lev_b)
    counts_2 = lax.ppermute(counts, "lon", [((i + 2) % lon_n, i) for i in range(lon_n)])

    gram_rows = nvec * nvec // 128 + 1
    gram, beta_row = call(
        functools.partial(gram_kernel, nvec, levels, cols, lat),
        (sds(gram_rows, 128), sds(1, 128)), (beta_prev.reshape(1), s, v, counts), specs=[SM, VM, VM, VM],
        scratch=[pltpu.VMEM((128 * gram_rows, 128), f32)], flops=20 << 20,
    )

    corner_a, corner_b, window = call(
        functools.partial(corner_kernel, levels),
        (sds(5, CHUNK, lat), sds(5, CHUNK, lat), sds(1, 128)),
        (west, east, counts, counts_2, gram),
    )
    if lon_n == 8:
        near = [window, lax.ppermute(window, "lon", [(i, i ^ 4) for i in range(lon_n)])]
    else:
        near = [lax.psum(counts, "lon")]
    corner_a, corner_b = both(corner_a, corner_b)

    padded = cols + 3 * CHUNK
    state = (sds(levels + 4, padded, lat), sds(2, 3, cols + CHUNK, lat), sds(levels + 2, padded, lat))
    halo = (sds(3, levels, CHUNK, lat), sds(3, levels, CHUNK, lat))
    *state, halo_a, halo_b = call(
        functools.partial(first_kernel, levels, cols, lat), (*state, *halo), (v, vel, west, east, lev_a, lev_b),
        flops=4 << 20,
    )
    scratch = [pltpu.VMEM((CHUNK, lat), f32)]
    scratch += [pltpu.VMEM((levels + 2, padded, lat), f32)] * 10
    scratch += [pltpu.VMEM((levels + 4, cols + CHUNK, lat), f32)]
    operands = (lw, beta_row, prev, vel, owner, west, east, halo_a, halo_b, *state,
                corner_a, corner_b, *near)
    part, send_a, send_b = call(
        functools.partial(stencil_kernel, levels, cols, lat, float(cols * lon_n * lat), len(near)),
        (sds(levels, cols, lat), sds(SECOND, cols, lat), sds(SECOND, cols, lat), *(sds(*x.shape) for x in state)),
        operands, specs=[SM] + [VM] * (len(operands) - 1), scratch=scratch, flops=8 << 20,
        alias={9: 3, 10: 4, 11: 5},
    )[:3]
    got_a, got_b = both(send_a, send_b)
    applied, msg = call(
        functools.partial(gather_kernel, nvec, levels, cols, lat, count),
        (sds(levels, cols, lat), sds(count, gram_rows, 128)),
        (part, got_a, got_b, v, s, gram),
        scratch=[pltpu.VMEM((128, 128), f32)],
    )
    msg = lax.all_to_all(msg, ("lon", "lev"), 0, 0, tiled=True)
    cells = float(v.size * count)
    orthogonal, row, trust = call(
        functools.partial(orthogonal_kernel, nvec, levels, cols, lat, cells),
        (sds(levels, cols, lat), sds(1, 128), sds(1, 1)), (msg, applied, v, s),
    )

    def direct():
        square = lax.psum(jnp.sum(orthogonal * orthogonal), ("lon", "lev")) / cells
        return row.at[0, 1].set(jnp.sqrt(square + 1e-12))

    row = lax.cond(trust[0, 0] > 0.5, lambda: row, direct)
    result, coefs = call(
        functools.partial(scale_kernel, nvec),
        (sds(levels, cols, lat), sds(1, nvec + 2)),
        (row, orthogonal), out_specs=(HBM, HBM),
        scratch=[pltpu.VMEM((levels, cols, lat), f32), pltpu.VMEM((1, nvec + 2), f32),
                 pltpu.SemaphoreType.DMA((levels + 1,))],
    )
    return result, coefs.reshape(nvec + 2)


def solution(mesh):
    placed = (
        P("lev", "lon", None),
        P("lev", "lon", None),
        P(),
        P(None, "lev", "lon", None),
        P(None, None, "lev", "lon", None),
        P("lev"),
        P("lon", None),
    )
    return jax.shard_map(
        body, mesh=mesh, in_specs=placed, out_specs=(P("lev", "lon", None), P()), check_vma=False
    )
```

```python
import functools

import jax
import jax.numpy as jnp
from jax import lax
from jax.experimental import pallas as pl
from jax.experimental.pallas import tpu as pltpu
from jax.sharding import PartitionSpec as P

NBOX = 5
kappa = 0.1
centre = 1.0 - 6.0 * kappa
f32 = jnp.float32

VM = pl.BlockSpec(memory_space=pltpu.VMEM)
SM = pl.BlockSpec(memory_space=pltpu.SMEM)
HBM = pl.BlockSpec(memory_space=pltpu.HBM)
CHUNK = 8
WIDE = 4
SECOND = 2
V_ROWS, A_ROWS, B_ROWS = 4, 3, 2
LEVEL_ROWS = V_ROWS + 3 * (A_ROWS + B_ROWS)
B_AT = V_ROWS + 3 * A_ROWS


def sds(*shape):
    return jax.ShapeDtypeStruct(shape, f32)


def call(kernel, outs, operands, specs=None, scratch=(), flops=0, alias=None, out_specs=None):
    nbytes = sum(4 * x.size for x in operands)
    return pl.pallas_call(
        kernel,
        out_shape=outs,
        in_specs=specs or [VM] * len(operands),
        out_specs=out_specs or jax.tree.map(lambda _: VM, outs),
        scratch_shapes=list(scratch),
        input_output_aliases=alias or {},
        compiler_params=pltpu.CompilerParams(vmem_limit_bytes=16 << 20),
        cost_estimate=pl.CostEstimate(flops=flops, bytes_accessed=nbytes, transcendentals=0),
    )(*operands)


def in_hbm(x):
    return pltpu.with_memory_space_constraint(x, pltpu.HBM)


def lane_iota(shape):
    return lax.broadcasted_iota(jnp.int32, shape, len(shape) - 1)


def even_level():
    return lax.rem(lax.axis_index("lev"), 2) == 0


def pack_kernel(levels, cols, v_hbm, vel_hbm, owner_hbm, lo, hi, lev_a, lev_b, counts, v, vel, owner, sems):
    copies = [pltpu.make_async_copy(v_hbm, v, sems.at[0]), pltpu.make_async_copy(owner_hbm, owner, sems.at[1])]
    for section in range(2):
        for comp in range(3):
            sem = sems.at[2 + 3 * section + comp]
            copies.append(pltpu.make_async_copy(vel_hbm.at[section, comp], vel.at[section, comp], sem))
    for copy in copies:
        copy.start()

    def edge(low, n):
        return slice(0, n) if low else slice(cols - n, cols)

    sides = ((lo, True), (hi, False))
    even = even_level()
    tops = ((lev_a, even), (lev_b, jnp.logical_not(even)))
    copies[0].wait()
    for msg, low in sides:
        for lev in range(levels):
            msg[lev * LEVEL_ROWS : lev * LEVEL_ROWS + V_ROWS] = v[lev, edge(low, V_ROWS)]
    for msg, top in tops:
        msg[0] = v[jnp.where(top, levels - 1, 0)]
        msg[1] = v[jnp.where(top, levels - 2, 1)]
    copies[1].wait()
    lanes = lane_iota((1, 128))
    row = jnp.zeros((1, 128), f32)
    held = owner[...]
    for box in range(1, NBOX + 1):
        hot = jnp.sum((held == box).astype(f32), axis=0, keepdims=True)
        row = jnp.where(lanes == box - 1, jnp.sum(hot, axis=1, keepdims=True), row)
    counts[...] = row
    at = levels * LEVEL_ROWS
    for msg, low in sides:
        msg[at : at + B_ROWS] = owner[edge(low, B_ROWS)].astype(f32)
        msg[at + B_ROWS : at + B_ROWS + 1, 0:128] = row
    for section, n, start in ((0, A_ROWS, V_ROWS), (1, B_ROWS, B_AT)):
        for comp in range(3):
            copies[2 + 3 * section + comp].wait()
            for msg, low in sides:
                for lev in range(levels):
                    at = lev * LEVEL_ROWS + start + comp * n
                    msg[at : at + n] = vel[section, comp, lev, edge(low, n)]
            if section == 0:
                for msg, top in tops:
                    msg[2 + comp] = vel[0, comp, jnp.where(top, levels - 1, 0)]


def unpack(west, east, n, at):
    gap = jnp.zeros((CHUNK - 2 * n, west.shape[1]), f32)
    parts = [east[at : at + n], gap, west[at : at + n]]
    return jnp.concatenate([x for x in parts if x.shape[0]], axis=0)


def corner_kernel(levels, west, east, window, lev_a, lev_b, corner_a, corner_b):
    even = even_level()

    def put(item, top, bottom):
        corner_a[item] = jnp.where(even, top, bottom)
        corner_b[item] = jnp.where(even, bottom, top)

    def both(n, start, near=0):
        return [unpack(west, east, n, lev * LEVEL_ROWS + start) for lev in (levels - 1 - near, near)]

    put(0, *both(V_ROWS, 0))
    put(1, *both(V_ROWS, 0, 1))
    for comp in range(3):
        put(2 + comp, *both(A_ROWS, V_ROWS + comp * A_ROWS))


def window_kernel(levels, west, east, counts, counts_2, order, window):
    at = levels * LEVEL_ROWS + B_ROWS
    window[...] = counts[...] + counts_2[...] + west[at : at + 1, 0:128] + east[at : at + 1, 0:128]


class Block:
    def __init__(self, levels, cols, lat):
        self.levels, self.lat, self.chunks = levels, lat, cols // CHUNK
        level = lax.axis_index("lev")
        self.has = (level > 0, level < lax.axis_size("lev") - 1)
        self.even = even_level()
        lanes = lane_iota((CHUNK, lat))
        self.first_lane, self.last_lane = lanes == 0, lanes == lat - 1

    def put_west(self, ref, at, k, value):
        ref[at, rows(k)] = value
        if k == self.chunks:
            ref[at, 0:CHUNK] = value

    def put_east(self, ref, at, k, value):
        ref[at, rows(k)] = value
        if k == 0:
            ref[at, rows(self.chunks + 1)] = value

    def put_both(self, ref, at, k, value):
        self.put_west(ref, at, k, value)
        if k == 0:
            ref[at, rows(self.chunks + 1)] = value

    def from_south(self, x):
        return jnp.where(self.first_lane, 0.0, pltpu.roll(x, 1, 1))

    def from_north(self, x):
        return jnp.where(self.last_lane, 0.0, pltpu.roll(x, self.lat - 1, 1))

    def beyond(self, got_a, got_b, src, k, vv, la):
        for item in range(5):
            a, b = got_a[item, src], got_b[item, src]
            below, above = jnp.where(self.even, b, a), jnp.where(self.even, a, b)
            if item < 2:
                self.put_both(vv, 1 - item, k, jnp.where(self.has[0], below, 0.0))
                self.put_both(vv, self.levels + 2 + item, k, jnp.where(self.has[1], above, 0.0))
            else:
                la[0, item - 2, tile(k)] = below
                la[1, item - 2, tile(k)] = above

    def tangent(self, ref, at, k, abc):
        here = ref[at, rows(k)]
        e, w = ref[at, rows(k, 1)], ref[at, rows(k, -1)]
        n, s = self.from_north(here), self.from_south(here)
        u, d = ref[at + 1, rows(k)], ref[at - 1, rows(k)]
        a, b, c = abc
        around = ((e + w) + (n + s)) + (u + d)
        drift = a * (w - e) + b * (s - n) + c * (d - u)
        return centre * here + kappa * around + 0.5 * drift

    def push(self, x, abc, dst, at, k):
        inside, to_e, to_w, to_u, to_d = dst
        a, b, c = abc
        base, half = kappa * x, 0.5 * x
        a, b, c = a * half, b * half, c * half
        inside[at, rows(k)] = centre * x + (self.from_south(base - b) + self.from_north(base + b))
        self.put_west(to_e, at, k, base - a)
        self.put_east(to_w, at, k, base + a)
        to_u[at, rows(k)] = base - c
        to_d[at, rows(k)] = base + c


def rows(k, shift=0):
    return slice(CHUNK * (k + 1) + shift, CHUNK * (k + 2) + shift)


def tile(k):
    return slice(CHUNK * k, CHUNK * (k + 1))


def first_kernel(levels, cols, lat, v, vel, west, east, lev_a, lev_b, vv, la, ff, halo_a, halo_b):
    block = Block(levels, cols, lat)
    for k in range(block.chunks):
        block.beyond(lev_a, lev_b, tile(k), k, vv, la)
    for k in range(block.chunks + 1):
        for lev in range(levels):
            value = v[lev, tile(k)] if k < block.chunks else unpack(west, east, V_ROWS, lev * LEVEL_ROWS)
            block.put_both(vv, lev + 2, k, value)

    for lev in range(levels):
        for comp in range(3):
            base = lev * LEVEL_ROWS + V_ROWS
            halo_a[comp, lev] = unpack(west, east, A_ROWS, base + comp * A_ROWS)
            halo_b[comp, lev] = unpack(west, east, B_ROWS, base + 3 * A_ROWS + comp * B_ROWS)

    def first_level(lev, carry):
        for k in range(block.chunks):
            abc = [vel[0, comp, lev, tile(k)] for comp in range(3)]
            block.put_both(ff, lev + 1, k, block.tangent(vv, lev + 2, k, abc))
        return carry

    lax.fori_loop(0, levels, first_level, 0)


def stencil_kernel(
    levels, cols, lat, columns, n_counts,
    lw, vel, owner, west, east, halo_a, halo_b,
    vv_in, la_in, ff_in, corner_a, corner_b, *refs,
):
    count_refs = refs[:n_counts]
    applied, send_a, send_b, vv, la, ff = refs[n_counts : n_counts + 6]
    (own_h, w_in, w_e, w_w, w_u, w_d, u_in, u_e, u_w, u_u, u_d, out) = refs[n_counts + 6 :]
    block = Block(levels, cols, lat)
    chunks, has, even = block.chunks, block.has, block.even
    tangent, push, put_both = block.tangent, block.push, block.put_both

    block.beyond(corner_a, corner_b, slice(0, CHUNK), chunks, vv, la)
    own_h[...] = unpack(west, east, B_ROWS, levels * LEVEL_ROWS)

    def flow(section, k, lev):
        if k < chunks:
            return [vel[section, comp, lev, tile(k)] for comp in range(3)]
        return [(halo_b if section else halo_a)[comp, lev] for comp in range(3)]

    def flow_beyond(side, k):
        return [la[side, comp, tile(k)] for comp in range(3)]

    for k in range(chunks + 1):
        for side, at in ((0, 0), (1, levels + 1)):
            value = tangent(vv, at + 1, k, flow_beyond(side, k))
            put_both(ff, at, k, jnp.where(has[side], value, 0.0))

    def first_level(lev, carry):
        put_both(ff, lev + 1, chunks, tangent(vv, lev + 2, chunks, flow(0, chunks, lev)))
        return carry

    lax.fori_loop(0, levels, first_level, 0)

    total = count_refs[0][...]
    for ref in count_refs[1:]:
        total = total + ref[...]
    scales = columns / (NBOX * jnp.maximum(total, 1.0))
    for k in range(chunks + 1):
        mine = owner[CHUNK * k : CHUNK * (k + 1)].astype(f32) if k < chunks else own_h[...]
        factor = jnp.zeros((CHUNK, lat), f32)
        for box in range(1, NBOX + 1):
            factor = jnp.where(mine == float(box), jnp.broadcast_to(scales[:, box - 1 : box], (CHUNK, lat)), factor)
        out[0, CHUNK * k : CHUNK * (k + 1)] = factor

    def second_level(lev, carry):
        weight = lw[lev]
        for k in range(chunks + 1):
            abc = flow(1, k, lev)
            x = tangent(ff, lev + 1, k, abc)
            x = (weight * out[0, CHUNK * k : CHUNK * (k + 1)]) * x
            push(x, abc, (w_in, w_e, w_w, w_u, w_d), lev + 1, k)
        return carry

    lax.fori_loop(0, levels, second_level, 0)
    for k in range(chunks + 1):
        w_u[0, rows(k)] = jnp.zeros((CHUNK, lat), f32)
        w_d[levels + 1, rows(k)] = jnp.zeros((CHUNK, lat), f32)

    def third_level(lev, carry):
        for k in range(chunks + 1):
            x = (
                w_in[lev + 1, rows(k)]
                + (w_e[lev + 1, rows(k, -1)] + w_w[lev + 1, rows(k, 1)])
                + (w_u[lev, rows(k)] + w_d[lev + 2, rows(k)])
            )
            push(x, flow(0, k, lev), (u_in, u_e, u_w, u_u, u_d), lev + 1, k)
        return carry

    lax.fori_loop(0, levels, third_level, 0)
    for k in range(chunks + 1):
        for side, at, x in ((0, 0, w_d[1, rows(k)]), (1, levels + 1, w_u[levels, rows(k)])):
            x = jnp.where(has[side], x, 0.0)
            push(x, flow_beyond(side, k), (u_in, u_e, u_w, u_u, u_d), at, k)

    for k in range(chunks):
        cells = slice(CHUNK * k, CHUNK * (k + 1))
        out[0, cells] = u_d[0, rows(k)]
        out[levels + 3, cells] = u_u[levels + 1, rows(k)]
        for at in range(levels + 2):
            x = u_in[at, rows(k)] + (u_e[at, rows(k, -1)] + u_w[at, rows(k, 1)])
            if at > 0:
                x = x + u_u[at - 1, rows(k)]
            if at < levels + 1:
                x = x + u_d[at + 1, rows(k)]
            if 1 <= at <= levels:
                applied[at - 1, cells] = x
            else:
                out[at + 1, cells] = x
    up = jnp.where(even, levels + 2, 0)
    down = levels + 2 - up
    for i in range(SECOND):
        send_a[i] = out[up + i, 0:cols]
        send_b[i] = out[down + i, 0:cols]


def put_sum(rows_ref, at, acc):
    rows_ref[at : at + 1] = jnp.sum(acc, axis=0, keepdims=True)


def to_lanes(rows_ref, at):
    return jnp.sum(jnp.transpose(rows_ref[at : at + 128, :]), axis=0, keepdims=True)


def tiles(lat):
    return [slice(t, t + 128) for t in range(0, lat, 128)]


def load_kernel(beta_prev, s_hbm, prev_hbm, order, beta_out, s, prev, sems):
    copies = [pltpu.make_async_copy(s_hbm.at[i], s.at[i], sems.at[i]) for i in range(s.shape[0])]
    copies.append(pltpu.make_async_copy(prev_hbm, prev, sems.at[s.shape[0]]))
    for copy in copies:
        copy.start()
    beta_out[...] = jnp.full((1, 128), beta_prev[0], f32)
    for copy in copies:
        copy.wait()


def gram_kernel(nvec, levels, cols, lat, s, v, order, out, sums):
    sums[...] = jnp.zeros(sums.shape, f32)
    steps = levels * (cols // CHUNK)
    block = 4

    def place(step):
        lev = step // (cols // CHUNK)
        row = pl.multiple_of((step - lev * (cols // CHUNK)) * CHUNK, CHUNK)
        return lev, pl.ds(row, CHUNK)

    for i0 in range(0, nvec, block):
        for j0 in range(i0, nvec, block):
            pairs = [(i, j) for i in range(i0, i0 + block) for j in range(j0, j0 + block) if i <= j]

            def body(step, acc, pairs=pairs, need=sorted({*range(i0, i0 + block), *range(j0, j0 + block)})):
                lev, cells = place(step)
                for t in tiles(lat):
                    held = {i: s[i, lev, cells, t] for i in need}
                    acc = tuple(x + held[i] * held[j] for x, (i, j) in zip(acc, pairs))
                return acc

            acc = lax.fori_loop(0, steps, body, tuple(jnp.zeros((CHUNK, 128), f32) for _ in pairs), unroll=4)
            for (i, j), x in zip(pairs, acc):
                put_sum(sums, nvec * i + j, x)

    def body_v(step, acc):
        lev, cells = place(step)
        for t in tiles(lat):
            x = v[lev, cells, t]
            acc = tuple(y + x * s[i, lev, cells, t] for i, y in enumerate(acc[:-1])) + (acc[-1] + x * x,)
        return acc

    acc = lax.fori_loop(0, steps, body_v, tuple(jnp.zeros((CHUNK, 128), f32) for _ in range(nvec + 1)), unroll=2)
    base = nvec * nvec
    for i in range(nvec):
        put_sum(sums, base + nvec + i, acc[i])
    put_sum(sums, base + 2 * nvec + 2, acc[nvec])
    for r in range(base // 128 + 1):
        out[r : r + 1] = to_lanes(sums, 128 * r)


def gather_kernel(nvec, levels, cols, lat, count, part, got_a, got_b, prev, beta_prev, v, s, gram, applied, msg, sums):
    level = lax.axis_index("lev")
    has = (level > 0, level < lax.axis_size("lev") - 1)
    even = even_level()
    beta = jnp.broadcast_to(beta_prev[:, 0:1], (CHUNK, lat))
    for k in range(cols // CHUNK):
        cells = slice(CHUNK * k, CHUNK * (k + 1))
        for lev in range(levels):
            x = part[lev, cells] - beta * prev[lev, cells]
            if lev < SECOND:
                x = x + jnp.where(has[0], jnp.where(even, got_b[lev, cells], got_a[lev, cells]), 0.0)
            if lev >= levels - SECOND:
                i = lev - levels + SECOND
                x = x + jnp.where(has[1], jnp.where(even, got_a[i, cells], got_b[i, cells]), 0.0)
            applied[lev, cells] = x
    sums[...] = jnp.zeros(sums.shape, f32)
    steps = levels * (cols // CHUNK)

    def body(step, acc):
        lev = step // (cols // CHUNK)
        cells = pl.ds(pl.multiple_of((step - lev * (cols // CHUNK)) * CHUNK, CHUNK), CHUNK)
        for t in tiles(lat):
            x = applied[lev, cells, t]
            acc = tuple(y + x * s[i, lev, cells, t] for i, y in enumerate(acc[:nvec])) + (
                acc[nvec] + x * x,
                acc[nvec + 1] + x * v[lev, cells, t],
            )
        return acc

    acc = lax.fori_loop(0, steps, body, tuple(jnp.zeros((CHUNK, 128), f32) for _ in range(nvec + 2)), unroll=2)
    for i in range(nvec):
        put_sum(sums, i, acc[i])
    put_sum(sums, 2 * nvec, acc[nvec])
    put_sum(sums, 2 * nvec + 1, acc[nvec + 1])
    r = gram.shape[0] - 1
    row = to_lanes(sums, 0) + gram[r : r + 1]
    msg[:, 0:r] = jnp.broadcast_to(gram[0:r][None], (count, r, 128))
    msg[:, r : r + 1] = jnp.broadcast_to(row[None], (count, 1, 128))


def orthogonal_kernel(nvec, levels, cols, lat, cells_all, msg, applied, v, s, orthogonal, out, trust):
    total = jnp.sum(msg[...], axis=0) * (1.0 / cells_all)
    r = total.shape[0] - 1
    row = total[r : r + 1]
    aa = row[:, 2 * nvec : 2 * nvec + 1]
    alpha = row[:, 2 * nvec + 1 : 2 * nvec + 2]
    vv = row[:, 2 * nvec + 2 : 2 * nvec + 3]
    lanes = lane_iota((1, 128))
    pv = row - alpha * pltpu.roll(row, 128 - nvec, 1)
    p = [jnp.broadcast_to(pv[:, k : k + 1], (1, 128)) for k in range(nvec)]
    tiled = jnp.zeros((1, 128), f32)
    for k in range(nvec):
        tiled = jnp.where(lax.rem(lanes, nvec) == k, p[k], tiled)
    quad = jnp.zeros((1, 128), f32)
    per = 128 // nvec
    for g in range(r):
        rep = jnp.zeros((1, 128), f32)
        for i in range(per):
            rep = jnp.where(lanes // nvec == i, p[g * per + i], rep)
        i, j = g * per + lanes // nvec, lax.rem(lanes, nvec)
        weight = jnp.where(i == j, 1.0, jnp.where(i < j, 2.0, 0.0))
        quad = quad + weight * rep * tiled * total[g : g + 1]
    quad = jnp.sum(quad, axis=1, keepdims=True)
    pp = jnp.sum(jnp.where(lanes < nvec, pv * pv, 0.0), axis=1, keepdims=True)
    square = (aa - 2.0 * alpha * alpha + alpha * alpha * vv) + (quad - 2.0 * pp)
    size = aa + alpha * alpha * (2.0 + vv) + 2.0 * pp + jnp.abs(quad)
    trust[...] = jnp.where((square > 0.03125 * size) & (size < 1e36), 1.0, 0.0)
    beta = jnp.sqrt(square + 1e-12)
    out[...] = jnp.where(lanes == 0, alpha, jnp.where(lanes == 1, beta, pltpu.roll(pv, 2, 1)))


    a_w = jnp.broadcast_to(alpha, (CHUNK, 128))
    weights = [jnp.broadcast_to(x, (CHUNK, 128)) for x in p]

    def body(step, carry):
        lev = step // (cols // CHUNK)
        at = pl.ds(pl.multiple_of((step - lev * (cols // CHUNK)) * CHUNK, CHUNK), CHUNK)
        for t in tiles(lat):
            x = applied[lev, at, t] - a_w * v[lev, at, t]
            y = weights[0] * s[0, lev, at, t]
            for k in range(1, nvec):
                y = y + weights[k] * s[k, lev, at, t]
            orthogonal[lev, at, t] = x - y
        return carry

    lax.fori_loop(0, levels * (cols // CHUNK), body, 0)


def scale_kernel(nvec, row, orthogonal, result_out, coefs_out, result, coefs, sems):
    line = row[...]
    coefs[...] = line[:, 0 : nvec + 2]
    copies = [pltpu.make_async_copy(result.at[i], result_out.at[i], sems.at[i]) for i in range(result.shape[0])]
    copies.append(pltpu.make_async_copy(coefs, coefs_out, sems.at[result.shape[0]]))
    copies[-1].start()
    inverse = 1.0 / line[:, 1:2]
    for i in range(result.shape[0]):
        result[i] = orthogonal[i] * inverse
        copies[i].start()
    for copy in copies:
        copy.wait()


def body(v, prev, beta_prev, s, vel, lw, owner):
    lon_n, lev_n = lax.axis_size("lon"), lax.axis_size("lev")
    count = lon_n * lev_n
    levels, cols, lat = v.shape
    nvec = s.shape[0]
    lines = levels * LEVEL_ROWS + B_ROWS + 1
    lines += -lines % CHUNK

    lo, hi, lev_a, lev_b, counts, v, vel, owner = call(
        functools.partial(pack_kernel, levels, cols),
        (sds(lines, lat), sds(lines, lat), sds(5, cols, lat), sds(5, cols, lat), sds(1, 128),
         sds(*v.shape), sds(*vel.shape), jax.ShapeDtypeStruct(owner.shape, owner.dtype)),
        tuple(in_hbm(x) for x in (v, vel, owner)), specs=[HBM] * 3, scratch=[pltpu.SemaphoreType.DMA((8,))], flops=1 << 20,
    )
    east_of = [(i, (i + 1) % lon_n) for i in range(lon_n)]
    west_of = [((i + 1) % lon_n, i) for i in range(lon_n)]
    pairs_a = [(i, i ^ 1) for i in range(lev_n)]
    pairs_b = []
    for i in range(count):
        at, level = divmod(i, lev_n)
        if level in (0, lev_n - 1):
            pairs_b.append((i, (at ^ 1) * lev_n + level))
        else:
            pairs_b.append((i, i + 1 if level % 2 else i - 1))

    def both(a, b):
        return lax.ppermute(a, "lev", pairs_a), lax.ppermute(b, ("lon", "lev"), pairs_b)

    around = [(i, (i + 1) % lev_n if i % 2 else (i - 1) % lev_n) for i in range(lev_n)]

    west, east = lax.ppermute(hi, "lon", east_of), lax.ppermute(lo, "lon", west_of)
    lev_a, lev_b = lax.ppermute(lev_a, "lev", pairs_a), lax.ppermute(lev_b, "lev", around)
    counts_2 = lax.ppermute(counts, "lon", [((i + 2) % lon_n, i) for i in range(lon_n)])

    beta_row, s, prev = call(
        load_kernel, (sds(1, 128), sds(*s.shape), sds(*prev.shape)),
        (beta_prev.reshape(1), in_hbm(s), in_hbm(prev), counts), specs=[SM, HBM, HBM, VM],
        scratch=[pltpu.SemaphoreType.DMA((nvec + 1,))],
    )
    window = call(functools.partial(window_kernel, levels), sds(1, 128), (west, east, counts, counts_2, beta_row))
    if lon_n == 8:
        near = [window, lax.ppermute(window, "lon", [(i, i ^ 4) for i in range(lon_n)])]
    else:
        near = [lax.psum(counts, "lon")]
    corner_a, corner_b = call(
        functools.partial(corner_kernel, levels),
        (sds(5, CHUNK, lat), sds(5, CHUNK, lat)), (west, east, window, lev_a, lev_b),
    )
    corner_a, corner_b = both(corner_a, corner_b)

    padded = cols + 3 * CHUNK
    state = (sds(levels + 4, padded, lat), sds(2, 3, cols + CHUNK, lat), sds(levels + 2, padded, lat))
    halo = (sds(3, levels, CHUNK, lat), sds(3, levels, CHUNK, lat))
    *state, halo_a, halo_b = call(
        functools.partial(first_kernel, levels, cols, lat), (*state, *halo), (v, vel, west, east, lev_a, lev_b),
        flops=4 << 20,
    )
    scratch = [pltpu.VMEM((CHUNK, lat), f32)]
    scratch += [pltpu.VMEM((levels + 2, padded, lat), f32)] * 10
    scratch += [pltpu.VMEM((levels + 4, cols + CHUNK, lat), f32)]
    operands = (lw, vel, owner, west, east, halo_a, halo_b, *state,
                corner_a, corner_b, *near)
    part, send_a, send_b = call(
        functools.partial(stencil_kernel, levels, cols, lat, float(cols * lon_n * lat), len(near)),
        (sds(levels, cols, lat), sds(SECOND, cols, lat), sds(SECOND, cols, lat), *(sds(*x.shape) for x in state)),
        operands, specs=[SM] + [VM] * (len(operands) - 1), scratch=scratch, flops=8 << 20,
        alias={7: 3, 8: 4, 9: 5},
    )[:3]
    got_a, got_b = both(send_a, send_b)
    gram_rows = nvec * nvec // 128 + 1
    gram = call(
        functools.partial(gram_kernel, nvec, levels, cols, lat),
        sds(gram_rows, 128), (s, v, send_a),
        scratch=[pltpu.VMEM((128 * gram_rows, 128), f32)], flops=20 << 20,
    )
    applied, msg = call(
        functools.partial(gather_kernel, nvec, levels, cols, lat, count),
        (sds(levels, cols, lat), sds(count, gram_rows, 128)),
        (part, got_a, got_b, prev, beta_row, v, s, gram),
        scratch=[pltpu.VMEM((128, 128), f32)],
    )
    msg = lax.all_to_all(msg, ("lon", "lev"), 0, 0, tiled=True)
    cells = float(v.size * count)
    orthogonal, row, trust = call(
        functools.partial(orthogonal_kernel, nvec, levels, cols, lat, cells),
        (sds(levels, cols, lat), sds(1, 128), sds(1, 1)), (msg, applied, v, s),
    )

    def direct():
        square = lax.psum(jnp.sum(orthogonal * orthogonal), ("lon", "lev")) / cells
        return row.at[0, 1].set(jnp.sqrt(square + 1e-12))

    row = lax.cond(trust[0, 0] > 0.5, lambda: row, direct)
    result, coefs = call(
        functools.partial(scale_kernel, nvec),
        (sds(levels, cols, lat), sds(1, nvec + 2)),
        (row, orthogonal), out_specs=(HBM, HBM),
        scratch=[pltpu.VMEM((levels, cols, lat), f32), pltpu.VMEM((1, nvec + 2), f32),
                 pltpu.SemaphoreType.DMA((levels + 1,))],
    )
    return result, coefs.reshape(nvec + 2)


def solution(mesh):
    placed = (
        P("lev", "lon", None),
        P("lev", "lon", None),
        P(),
        P(None, "lev", "lon", None),
        P(None, None, "lev", "lon", None),
        P("lev"),
        P("lon", None),
    )
    return jax.shard_map(
        body, mesh=mesh, in_specs=placed, out_specs=(P("lev", "lon", None), P()), check_vma=False
    )
```

```python
import functools

import jax
import jax.numpy as jnp
from jax import lax
from jax.experimental import pallas as pl
from jax.experimental.pallas import tpu as pltpu
from jax.sharding import PartitionSpec as P

NBOX = 5
kappa = 0.1
centre = 1.0 - 6.0 * kappa
f32 = jnp.float32

VM = pl.BlockSpec(memory_space=pltpu.VMEM)
SM = pl.BlockSpec(memory_space=pltpu.SMEM)
HBM = pl.BlockSpec(memory_space=pltpu.HBM)
CHUNK = 8
WIDE = 4
SECOND = 2
V_ROWS, A_ROWS, B_ROWS = 4, 3, 2
LEVEL_ROWS = V_ROWS + 3 * (A_ROWS + B_ROWS)
B_AT = V_ROWS + 3 * A_ROWS


def sds(*shape):
    return jax.ShapeDtypeStruct(shape, f32)


def call(kernel, outs, operands, specs=None, scratch=(), flops=0, alias=None, out_specs=None, mib=4):
    nbytes = sum(4 * x.size for x in operands)
    return pl.pallas_call(
        kernel,
        out_shape=outs,
        in_specs=specs or [VM] * len(operands),
        out_specs=out_specs or jax.tree.map(lambda _: VM, outs),
        scratch_shapes=list(scratch),
        input_output_aliases=alias or {},
        compiler_params=pltpu.CompilerParams(vmem_limit_bytes=mib << 20),
        cost_estimate=pl.CostEstimate(flops=flops, bytes_accessed=nbytes, transcendentals=0),
    )(*operands)


def in_hbm(x):
    return pltpu.with_memory_space_constraint(x, pltpu.HBM)


def lane_iota(shape):
    return lax.broadcasted_iota(jnp.int32, shape, len(shape) - 1)


def even_level():
    return lax.rem(lax.axis_index("lev"), 2) == 0


def pack_kernel(levels, cols, v_hbm, vel_hbm, owner_hbm, lo, hi, lev_a, lev_b, counts, v, vel, owner, sems):
    copies = [pltpu.make_async_copy(v_hbm, v, sems.at[0]), pltpu.make_async_copy(owner_hbm, owner, sems.at[1])]
    for section in range(2):
        for comp in range(3):
            sem = sems.at[2 + 3 * section + comp]
            copies.append(pltpu.make_async_copy(vel_hbm.at[section, comp], vel.at[section, comp], sem))
    for copy in copies:
        copy.start()

    def edge(low, n):
        return slice(0, n) if low else slice(cols - n, cols)

    sides = ((lo, True), (hi, False))
    even = even_level()
    tops = ((lev_a, even), (lev_b, jnp.logical_not(even)))
    copies[0].wait()
    for msg, low in sides:
        for lev in range(levels):
            msg[lev * LEVEL_ROWS : lev * LEVEL_ROWS + V_ROWS] = v[lev, edge(low, V_ROWS)]
    for msg, top in tops:
        msg[0] = v[jnp.where(top, levels - 1, 0)]
        msg[1] = v[jnp.where(top, levels - 2, 1)]
    copies[1].wait()
    lanes = lane_iota((1, 128))
    row = jnp.zeros((1, 128), f32)
    held = owner[...]
    for box in range(1, NBOX + 1):
        hot = jnp.sum((held == box).astype(f32), axis=0, keepdims=True)
        row = jnp.where(lanes == box - 1, jnp.sum(hot, axis=1, keepdims=True), row)
    counts[...] = row
    at = levels * LEVEL_ROWS
    for msg, low in sides:
        msg[at : at + B_ROWS] = owner[edge(low, B_ROWS)].astype(f32)
        msg[at + B_ROWS : at + B_ROWS + 1, 0:128] = row
    for section, n, start in ((0, A_ROWS, V_ROWS), (1, B_ROWS, B_AT)):
        for comp in range(3):
            copies[2 + 3 * section + comp].wait()
            for msg, low in sides:
                for lev in range(levels):
                    at = lev * LEVEL_ROWS + start + comp * n
                    msg[at : at + n] = vel[section, comp, lev, edge(low, n)]
            if section == 0:
                for msg, top in tops:
                    msg[2 + comp] = vel[0, comp, jnp.where(top, levels - 1, 0)]


def unpack(west, east, n, at):
    gap = jnp.zeros((CHUNK - 2 * n, west.shape[1]), f32)
    parts = [east[at : at + n], gap, west[at : at + n]]
    return jnp.concatenate([x for x in parts if x.shape[0]], axis=0)


def corner_kernel(levels, west, east, window, corner_a, corner_b):
    even = even_level()

    def put(item, top, bottom):
        corner_a[item] = jnp.where(even, top, bottom)
        corner_b[item] = jnp.where(even, bottom, top)

    def both(n, start, near=0):
        return [unpack(west, east, n, lev * LEVEL_ROWS + start) for lev in (levels - 1 - near, near)]

    put(0, *both(V_ROWS, 0))
    put(1, *both(V_ROWS, 0, 1))
    for comp in range(3):
        put(2 + comp, *both(A_ROWS, V_ROWS + comp * A_ROWS))


def window_kernel(levels, west, east, counts, counts_2, order, after, window):
    at = levels * LEVEL_ROWS + B_ROWS
    window[...] = counts[...] + counts_2[...] + west[at : at + 1, 0:128] + east[at : at + 1, 0:128]


class Block:
    def __init__(self, levels, cols, lat):
        self.levels, self.lat, self.chunks = levels, lat, cols // CHUNK
        level = lax.axis_index("lev")
        self.has = (level > 0, level < lax.axis_size("lev") - 1)
        self.even = even_level()
        lanes = lane_iota((CHUNK, lat))
        self.first_lane, self.last_lane = lanes == 0, lanes == lat - 1

    def put_west(self, ref, at, k, value):
        ref[at, rows(k)] = value
        if k == self.chunks:
            ref[at, 0:CHUNK] = value

    def put_east(self, ref, at, k, value):
        ref[at, rows(k)] = value
        if k == 0:
            ref[at, rows(self.chunks + 1)] = value

    def put_both(self, ref, at, k, value):
        self.put_west(ref, at, k, value)
        if k == 0:
            ref[at, rows(self.chunks + 1)] = value

    def from_south(self, x):
        return jnp.where(self.first_lane, 0.0, pltpu.roll(x, 1, 1))

    def from_north(self, x):
        return jnp.where(self.last_lane, 0.0, pltpu.roll(x, self.lat - 1, 1))

    def beyond(self, got_a, got_b, src, k, vv, la):
        for item in range(5):
            a, b = got_a[item, src], got_b[item, src]
            below, above = jnp.where(self.even, b, a), jnp.where(self.even, a, b)
            if item < 2:
                self.put_both(vv, 1 - item, k, jnp.where(self.has[0], below, 0.0))
                self.put_both(vv, self.levels + 2 + item, k, jnp.where(self.has[1], above, 0.0))
            else:
                la[0, item - 2, tile(k)] = below
                la[1, item - 2, tile(k)] = above

    def tangent(self, ref, at, k, abc):
        here = ref[at, rows(k)]
        e, w = ref[at, rows(k, 1)], ref[at, rows(k, -1)]
        n, s = self.from_north(here), self.from_south(here)
        u, d = ref[at + 1, rows(k)], ref[at - 1, rows(k)]
        a, b, c = abc
        around = ((e + w) + (n + s)) + (u + d)
        drift = a * (w - e) + b * (s - n) + c * (d - u)
        return centre * here + kappa * around + 0.5 * drift

    def first_beyond(self, vv, la, ff, k):
        for side, at in ((0, 0), (1, self.levels + 1)):
            value = self.tangent(vv, at + 1, k, [la[side, comp, tile(k)] for comp in range(3)])
            self.put_both(ff, at, k, jnp.where(self.has[side], value, 0.0))

    def push(self, x, abc, dst, at, k):
        inside, to_e, to_w, to_u, to_d = dst
        a, b, c = abc
        base, half = kappa * x, 0.5 * x
        a, b, c = a * half, b * half, c * half
        inside[at, rows(k)] = centre * x + (self.from_south(base - b) + self.from_north(base + b))
        self.put_west(to_e, at, k, base - a)
        self.put_east(to_w, at, k, base + a)
        to_u[at, rows(k)] = base - c
        to_d[at, rows(k)] = base + c


def rows(k, shift=0):
    return slice(CHUNK * (k + 1) + shift, CHUNK * (k + 2) + shift)


def tile(k):
    return slice(CHUNK * k, CHUNK * (k + 1))


def lev_kernel(levels, cols, lat, lev_a, lev_b, vv, la):
    block = Block(levels, cols, lat)
    for k in range(block.chunks):
        block.beyond(lev_a, lev_b, tile(k), k, vv, la)


def first_kernel(levels, cols, lat, v, vel, west, east, vv_in, la, vv, ff, xx, halo_a, halo_b):
    block = Block(levels, cols, lat)
    last = block.chunks
    for lev in range(levels):
        for k in range(last):
            block.put_both(vv, lev + 2, k, v[lev, tile(k)])
        block.put_both(vv, lev + 2, last, unpack(west, east, V_ROWS, lev * LEVEL_ROWS))
        for comp in range(3):
            base = lev * LEVEL_ROWS + V_ROWS
            halo_a[comp, lev] = unpack(west, east, A_ROWS, base + comp * A_ROWS)
            halo_b[comp, lev] = unpack(west, east, B_ROWS, base + 3 * A_ROWS + comp * B_ROWS)

    def flow(section, lev, k):
        return [vel[section, comp, lev, tile(k)] for comp in range(3)]

    def first_level(lev, carry):
        for k in range(last):
            block.put_both(ff, lev + 1, k, block.tangent(vv, lev + 2, k, flow(0, lev, k)))
        return carry

    lax.fori_loop(0, levels, first_level, 0)
    for k in range(1, last - 1):
        block.first_beyond(vv, la, ff, k)

    def inner_level(lev, carry):
        abc = [halo_a[comp, lev] for comp in range(3)]
        block.put_both(ff, lev + 1, last, block.tangent(vv, lev + 2, last, abc))
        for k in range(last):
            xx[lev, tile(k)] = block.tangent(ff, lev + 1, k, flow(1, lev, k))
        return carry

    lax.fori_loop(1, levels - 1, inner_level, 0)


def edge_kernel(levels, cols, lat, vel, halo_a, halo_b, corner_a, corner_b, vv_in, la_in, ff_in, xx_in, vv, la, ff, xx):
    block = Block(levels, cols, lat)
    last = block.chunks
    block.beyond(corner_a, corner_b, slice(0, CHUNK), last, vv, la)
    for k in (0, last - 1, last):
        block.first_beyond(vv, la, ff, k)
    for lev in (0, levels - 1):
        abc = [halo_a[comp, lev] for comp in range(3)]
        block.put_both(ff, lev + 1, last, block.tangent(vv, lev + 2, last, abc))
    for lev in range(levels):
        if lev in (0, levels - 1):
            for k in range(last):
                abc = [vel[1, comp, lev, tile(k)] for comp in range(3)]
                xx[lev, tile(k)] = block.tangent(ff, lev + 1, k, abc)
        xx[lev, tile(last)] = block.tangent(ff, lev + 1, last, [halo_b[comp, lev] for comp in range(3)])


def stencil_kernel(
    levels, cols, lat, columns, n_counts, lw, vel, owner, west, east, halo_a, halo_b, la, xx, *refs
):
    count_refs = refs[:n_counts]
    applied, send_a, send_b = refs[n_counts : n_counts + 3]
    (own_h, w_in, w_e, w_w, w_u, w_d, u_in, u_e, u_w, u_u, u_d, out) = refs[n_counts + 3 :]
    block = Block(levels, cols, lat)
    chunks, has, even, push = block.chunks, block.has, block.even, block.push
    own_h[...] = unpack(west, east, B_ROWS, levels * LEVEL_ROWS)

    def flow(section, k, lev):
        if k < chunks:
            return [vel[section, comp, lev, tile(k)] for comp in range(3)]
        return [(halo_b if section else halo_a)[comp, lev] for comp in range(3)]

    def flow_beyond(side, k):
        return [la[side, comp, tile(k)] for comp in range(3)]

    total = count_refs[0][...]
    for ref in count_refs[1:]:
        total = total + ref[...]
    scales = columns / (NBOX * jnp.maximum(total, 1.0))
    for k in range(chunks + 1):
        mine = owner[CHUNK * k : CHUNK * (k + 1)].astype(f32) if k < chunks else own_h[...]
        factor = jnp.zeros((CHUNK, lat), f32)
        for box in range(1, NBOX + 1):
            factor = jnp.where(mine == float(box), jnp.broadcast_to(scales[:, box - 1 : box], (CHUNK, lat)), factor)
        out[0, CHUNK * k : CHUNK * (k + 1)] = factor

    def second_level(lev, carry):
        weight = lw[lev]
        for k in range(chunks + 1):
            abc = flow(1, k, lev)
            x = (weight * out[0, tile(k)]) * xx[lev, tile(k)]
            push(x, abc, (w_in, w_e, w_w, w_u, w_d), lev + 1, k)
        return carry

    lax.fori_loop(0, levels, second_level, 0)
    for k in range(chunks + 1):
        w_u[0, rows(k)] = jnp.zeros((CHUNK, lat), f32)
        w_d[levels + 1, rows(k)] = jnp.zeros((CHUNK, lat), f32)

    def third_level(lev, carry):
        for k in range(chunks + 1):
            x = (
                w_in[lev + 1, rows(k)]
                + (w_e[lev + 1, rows(k, -1)] + w_w[lev + 1, rows(k, 1)])
                + (w_u[lev, rows(k)] + w_d[lev + 2, rows(k)])
            )
            push(x, flow(0, k, lev), (u_in, u_e, u_w, u_u, u_d), lev + 1, k)
        return carry

    lax.fori_loop(0, levels, third_level, 0)
    for k in range(chunks + 1):
        for side, at, x in ((0, 0, w_d[1, rows(k)]), (1, levels + 1, w_u[levels, rows(k)])):
            x = jnp.where(has[side], x, 0.0)
            push(x, flow_beyond(side, k), (u_in, u_e, u_w, u_u, u_d), at, k)

    for k in range(chunks):
        cells = slice(CHUNK * k, CHUNK * (k + 1))
        out[0, cells] = u_d[0, rows(k)]
        out[levels + 3, cells] = u_u[levels + 1, rows(k)]
        for at in range(levels + 2):
            x = u_in[at, rows(k)] + (u_e[at, rows(k, -1)] + u_w[at, rows(k, 1)])
            if at > 0:
                x = x + u_u[at - 1, rows(k)]
            if at < levels + 1:
                x = x + u_d[at + 1, rows(k)]
            if 1 <= at <= levels:
                applied[at - 1, cells] = x
            else:
                out[at + 1, cells] = x
    up = jnp.where(even, levels + 2, 0)
    down = levels + 2 - up
    for i in range(SECOND):
        send_a[i] = out[up + i, 0:cols]
        send_b[i] = out[down + i, 0:cols]


def put_sum(rows_ref, at, acc):
    rows_ref[at : at + 1] = jnp.sum(acc, axis=0, keepdims=True)


def to_lanes(rows_ref, at):
    return jnp.sum(jnp.transpose(rows_ref[at : at + 128, :]), axis=0, keepdims=True)


def tiles(lat):
    return [slice(t, t + 128) for t in range(0, lat, 128)]


def load_kernel(beta_prev, s_hbm, prev_hbm, order, beta_out, s, prev, sems):
    copies = [pltpu.make_async_copy(s_hbm.at[i], s.at[i], sems.at[i]) for i in range(s.shape[0])]
    copies.append(pltpu.make_async_copy(prev_hbm, prev, sems.at[s.shape[0]]))
    for copy in copies:
        copy.start()
    beta_out[...] = jnp.full((1, 128), beta_prev[0], f32)
    for copy in copies:
        copy.wait()


def gram_kernel(nvec, levels, cols, lat, s, v, order, out, sums):
    sums[...] = jnp.zeros(sums.shape, f32)
    steps = levels * (cols // CHUNK)
    block = 4

    def place(step):
        lev = step // (cols // CHUNK)
        row = pl.multiple_of((step - lev * (cols // CHUNK)) * CHUNK, CHUNK)
        return lev, pl.ds(row, CHUNK)

    for i0 in range(0, nvec, block):
        for j0 in range(i0, nvec, block):
            pairs = [(i, j) for i in range(i0, i0 + block) for j in range(j0, j0 + block) if i <= j]

            def body(step, acc, pairs=pairs, need=sorted({*range(i0, i0 + block), *range(j0, j0 + block)})):
                lev, cells = place(step)
                for t in tiles(lat):
                    held = {i: s[i, lev, cells, t] for i in need}
                    acc = tuple(x + held[i] * held[j] for x, (i, j) in zip(acc, pairs))
                return acc

            acc = lax.fori_loop(0, steps, body, tuple(jnp.zeros((CHUNK, 128), f32) for _ in pairs), unroll=4)
            for (i, j), x in zip(pairs, acc):
                put_sum(sums, nvec * i + j, x)

    def body_v(step, acc):
        lev, cells = place(step)
        for t in tiles(lat):
            x = v[lev, cells, t]
            acc = tuple(y + x * s[i, lev, cells, t] for i, y in enumerate(acc[:-1])) + (acc[-1] + x * x,)
        return acc

    acc = lax.fori_loop(0, steps, body_v, tuple(jnp.zeros((CHUNK, 128), f32) for _ in range(nvec + 1)), unroll=2)
    base = nvec * nvec
    for i in range(nvec):
        put_sum(sums, base + nvec + i, acc[i])
    put_sum(sums, base + 2 * nvec + 2, acc[nvec])
    for r in range(base // 128 + 1):
        out[r : r + 1] = to_lanes(sums, 128 * r)


def gather_kernel(nvec, levels, cols, lat, count, part, got_a, got_b, prev, beta_prev, v, s, gram, applied, msg, sums):
    level = lax.axis_index("lev")
    has = (level > 0, level < lax.axis_size("lev") - 1)
    even = even_level()
    beta = jnp.broadcast_to(beta_prev[:, 0:1], (CHUNK, lat))
    for k in range(cols // CHUNK):
        cells = slice(CHUNK * k, CHUNK * (k + 1))
        for lev in range(levels):
            x = part[lev, cells] - beta * prev[lev, cells]
            if lev < SECOND:
                x = x + jnp.where(has[0], jnp.where(even, got_b[lev, cells], got_a[lev, cells]), 0.0)
            if lev >= levels - SECOND:
                i = lev - levels + SECOND
                x = x + jnp.where(has[1], jnp.where(even, got_a[i, cells], got_b[i, cells]), 0.0)
            applied[lev, cells] = x
    sums[...] = jnp.zeros(sums.shape, f32)
    steps = levels * (cols // CHUNK)

    def body(step, acc):
        lev = step // (cols // CHUNK)
        cells = pl.ds(pl.multiple_of((step - lev * (cols // CHUNK)) * CHUNK, CHUNK), CHUNK)
        for t in tiles(lat):
            x = applied[lev, cells, t]
            acc = tuple(y + x * s[i, lev, cells, t] for i, y in enumerate(acc[:nvec])) + (
                acc[nvec] + x * x,
                acc[nvec + 1] + x * v[lev, cells, t],
            )
        return acc

    acc = lax.fori_loop(0, steps, body, tuple(jnp.zeros((CHUNK, 128), f32) for _ in range(nvec + 2)), unroll=4)
    for i in range(nvec):
        put_sum(sums, i, acc[i])
    put_sum(sums, 2 * nvec, acc[nvec])
    put_sum(sums, 2 * nvec + 1, acc[nvec + 1])
    r = gram.shape[0] - 1
    row = to_lanes(sums, 0) + gram[r : r + 1]
    msg[:, 0:r] = jnp.broadcast_to(gram[0:r][None], (count, r, 128))
    msg[:, r : r + 1] = jnp.broadcast_to(row[None], (count, 1, 128))


def orthogonal_kernel(nvec, levels, cols, lat, cells_all, msg, applied, v, s, orthogonal, out, trust):
    total = jnp.sum(msg[...], axis=0) * (1.0 / cells_all)
    r = total.shape[0] - 1
    row = total[r : r + 1]
    aa = row[:, 2 * nvec : 2 * nvec + 1]
    alpha = row[:, 2 * nvec + 1 : 2 * nvec + 2]
    vv = row[:, 2 * nvec + 2 : 2 * nvec + 3]
    lanes = lane_iota((1, 128))
    pv = row - alpha * pltpu.roll(row, 128 - nvec, 1)
    p = [jnp.broadcast_to(pv[:, k : k + 1], (1, 128)) for k in range(nvec)]
    tiled = jnp.zeros((1, 128), f32)
    for k in range(nvec):
        tiled = jnp.where(lax.rem(lanes, nvec) == k, p[k], tiled)
    quad = jnp.zeros((1, 128), f32)
    per = 128 // nvec
    for g in range(r):
        rep = jnp.zeros((1, 128), f32)
        for i in range(per):
            rep = jnp.where(lanes // nvec == i, p[g * per + i], rep)
        i, j = g * per + lanes // nvec, lax.rem(lanes, nvec)
        weight = jnp.where(i == j, 1.0, jnp.where(i < j, 2.0, 0.0))
        quad = quad + weight * rep * tiled * total[g : g + 1]
    quad = jnp.sum(quad, axis=1, keepdims=True)
    pp = jnp.sum(jnp.where(lanes < nvec, pv * pv, 0.0), axis=1, keepdims=True)
    square = (aa - 2.0 * alpha * alpha + alpha * alpha * vv) + (quad - 2.0 * pp)
    size = aa + alpha * alpha * (2.0 + vv) + 2.0 * pp + jnp.abs(quad)
    trust[...] = jnp.where((square > 0.03125 * size) & (size < 1e36), 1.0, 0.0)
    beta = jnp.sqrt(square + 1e-12)
    out[...] = jnp.where(lanes == 0, alpha, jnp.where(lanes == 1, beta, pltpu.roll(pv, 2, 1)))


    a_w = jnp.broadcast_to(alpha, (CHUNK, 128))
    weights = [jnp.broadcast_to(x, (CHUNK, 128)) for x in p]

    for lev in range(levels):
        for k in range(cols // CHUNK):
            for t in tiles(lat):
                x = applied[lev, tile(k), t] - a_w * v[lev, tile(k), t]
                y = [weights[k0] * s[k0, lev, tile(k), t] for k0 in range(nvec)]
                while len(y) > 1:
                    y = [a + b for a, b in zip(y[::2], y[1::2])] + y[len(y) & ~1 :]
                orthogonal[lev, tile(k), t] = x - y[0]


def scale_kernel(nvec, row, orthogonal, result_out, coefs_out, result, coefs, sems):
    line = row[...]
    coefs[...] = line[:, 0 : nvec + 2]
    copies = [pltpu.make_async_copy(result.at[i], result_out.at[i], sems.at[i]) for i in range(result.shape[0])]
    copies.append(pltpu.make_async_copy(coefs, coefs_out, sems.at[result.shape[0]]))
    copies[-1].start()
    inverse = 1.0 / line[:, 1:2]
    for i in range(result.shape[0]):
        result[i] = orthogonal[i] * inverse
        copies[i].start()
    for copy in copies:
        copy.wait()


def body(v, prev, beta_prev, s, vel, lw, owner):
    lon_n, lev_n = lax.axis_size("lon"), lax.axis_size("lev")
    count = lon_n * lev_n
    levels, cols, lat = v.shape
    nvec = s.shape[0]
    lines = levels * LEVEL_ROWS + B_ROWS + 1
    lines += -lines % CHUNK

    lo, hi, lev_a, lev_b, counts, v, vel, owner = call(
        functools.partial(pack_kernel, levels, cols),
        (sds(lines, lat), sds(lines, lat), sds(5, cols, lat), sds(5, cols, lat), sds(1, 128),
         sds(*v.shape), sds(*vel.shape), jax.ShapeDtypeStruct(owner.shape, owner.dtype)),
        tuple(in_hbm(x) for x in (v, vel, owner)), specs=[HBM] * 3, scratch=[pltpu.SemaphoreType.DMA((8,))], flops=1 << 20,
    )
    east_of = [(i, (i + 1) % lon_n) for i in range(lon_n)]
    west_of = [((i + 1) % lon_n, i) for i in range(lon_n)]
    pairs_a = [(i, i ^ 1) for i in range(lev_n)]
    pairs_b = []
    for i in range(count):
        at, level = divmod(i, lev_n)
        if level in (0, lev_n - 1):
            pairs_b.append((i, (at ^ 1) * lev_n + level))
        else:
            pairs_b.append((i, i + 1 if level % 2 else i - 1))

    def both(a, b):
        return lax.ppermute(a, "lev", pairs_a), lax.ppermute(b, ("lon", "lev"), pairs_b)

    around = [(i, (i + 1) % lev_n if i % 2 else (i - 1) % lev_n) for i in range(lev_n)]

    west, east = lax.ppermute(hi, "lon", east_of), lax.ppermute(lo, "lon", west_of)
    lev_a, lev_b = lax.ppermute(lev_a, "lev", pairs_a), lax.ppermute(lev_b, "lev", around)
    counts_2 = lax.ppermute(counts, "lon", [((i + 2) % lon_n, i) for i in range(lon_n)])

    beta_row, s, prev = call(
        load_kernel, (sds(1, 128), sds(*s.shape), sds(*prev.shape)),
        (beta_prev.reshape(1), in_hbm(s), in_hbm(prev), counts), specs=[SM, HBM, HBM, VM],
        scratch=[pltpu.SemaphoreType.DMA((nvec + 1,))],
    )
    padded = cols + 3 * CHUNK
    vv, la = call(
        functools.partial(lev_kernel, levels, cols, lat),
        (sds(levels + 4, padded, lat), sds(2, 3, cols + CHUNK, lat)), (lev_a, lev_b),
    )
    window = call(
        functools.partial(window_kernel, levels), sds(1, 128), (west, east, counts, counts_2, beta_row, la)
    )
    if lon_n == 8:
        near = [window, lax.ppermute(window, "lon", [(i, i ^ 4) for i in range(lon_n)])]
    else:
        near = [lax.psum(counts, "lon")]
    corner_a, corner_b = call(
        functools.partial(corner_kernel, levels),
        (sds(5, CHUNK, lat), sds(5, CHUNK, lat)), (west, east, window),
    )
    corner_a, corner_b = both(corner_a, corner_b)

    vv, ff, xx, halo_a, halo_b = call(
        functools.partial(first_kernel, levels, cols, lat),
        (sds(*vv.shape), sds(levels + 2, padded, lat), sds(levels, cols + CHUNK, lat),
         sds(3, levels, CHUNK, lat), sds(3, levels, CHUNK, lat)),
        (v, vel, west, east, vv, la), alias={4: 0}, flops=4 << 20,
    )
    vv, la, ff, xx = call(
        functools.partial(edge_kernel, levels, cols, lat), tuple(sds(*x.shape) for x in (vv, la, ff, xx)),
        (vel, halo_a, halo_b, corner_a, corner_b, vv, la, ff, xx), alias={5: 0, 6: 1, 7: 2, 8: 3}, flops=2 << 20,
    )
    scratch = [pltpu.VMEM((CHUNK, lat), f32)]
    scratch += [pltpu.VMEM((levels + 2, padded, lat), f32)] * 10
    scratch += [pltpu.VMEM((levels + 4, cols + CHUNK, lat), f32)]
    operands = (lw, vel, owner, west, east, halo_a, halo_b, la, xx, *near)
    part, send_a, send_b = call(
        functools.partial(stencil_kernel, levels, cols, lat, float(cols * lon_n * lat), len(near)),
        (sds(levels, cols, lat), sds(SECOND, cols, lat), sds(SECOND, cols, lat)),
        operands, specs=[SM] + [VM] * (len(operands) - 1), scratch=scratch, flops=8 << 20, mib=12,
    )
    got_a, got_b = both(send_a, send_b)
    gram_rows = nvec * nvec // 128 + 1
    gram = call(
        functools.partial(gram_kernel, nvec, levels, cols, lat),
        sds(gram_rows, 128), (s, v, send_a),
        scratch=[pltpu.VMEM((128 * gram_rows, 128), f32)], flops=20 << 20,
    )
    applied, msg = call(
        functools.partial(gather_kernel, nvec, levels, cols, lat, count),
        (sds(levels, cols, lat), sds(count, gram_rows, 128)),
        (part, got_a, got_b, prev, beta_row, v, s, gram),
        scratch=[pltpu.VMEM((128, 128), f32)],
    )
    msg = lax.all_to_all(msg, ("lon", "lev"), 0, 0, tiled=True)
    cells = float(v.size * count)
    orthogonal, row, trust = call(
        functools.partial(orthogonal_kernel, nvec, levels, cols, lat, cells),
        (sds(levels, cols, lat), sds(1, 128), sds(1, 1)), (msg, applied, v, s),
    )

    def direct():
        square = lax.psum(jnp.sum(orthogonal * orthogonal), ("lon", "lev")) / cells
        return row.at[0, 1].set(jnp.sqrt(square + 1e-12))

    row = lax.cond(trust[0, 0] > 0.5, lambda: row, direct)
    result, coefs = call(
        functools.partial(scale_kernel, nvec),
        (sds(levels, cols, lat), sds(1, nvec + 2)),
        (row, orthogonal), out_specs=(HBM, HBM),
        scratch=[pltpu.VMEM((levels, cols, lat), f32), pltpu.VMEM((1, nvec + 2), f32),
                 pltpu.SemaphoreType.DMA((levels + 1,))],
    )
    return result, coefs.reshape(nvec + 2)


def solution(mesh):
    placed = (
        P("lev", "lon", None),
        P("lev", "lon", None),
        P(),
        P(None, "lev", "lon", None),
        P(None, None, "lev", "lon", None),
        P("lev"),
        P("lon", None),
    )
    return jax.shard_map(
        body, mesh=mesh, in_specs=placed, out_specs=(P("lev", "lon", None), P()), check_vma=False
    )
```

```python
import functools

import jax
import jax.numpy as jnp
from jax import lax
from jax.experimental import pallas as pl
from jax.experimental.pallas import tpu as pltpu
from jax.sharding import PartitionSpec as P

NBOX = 5
kappa = 0.1
centre = 1.0 - 6.0 * kappa
f32 = jnp.float32

VM = pl.BlockSpec(memory_space=pltpu.VMEM)
SM = pl.BlockSpec(memory_space=pltpu.SMEM)
HBM = pl.BlockSpec(memory_space=pltpu.HBM)
CHUNK = 8
WIDE = 4
SECOND = 2
V_ROWS, A_ROWS, B_ROWS = 4, 3, 2
LEVEL_ROWS = V_ROWS + 3 * (A_ROWS + B_ROWS)
B_AT = V_ROWS + 3 * A_ROWS


def sds(*shape):
    return jax.ShapeDtypeStruct(shape, f32)


def call(kernel, outs, operands, specs=None, scratch=(), flops=0, alias=None, out_specs=None, mib=4):
    nbytes = sum(4 * x.size for x in operands)
    return pl.pallas_call(
        kernel,
        out_shape=outs,
        in_specs=specs or [VM] * len(operands),
        out_specs=out_specs or jax.tree.map(lambda _: VM, outs),
        scratch_shapes=list(scratch),
        input_output_aliases=alias or {},
        compiler_params=pltpu.CompilerParams(vmem_limit_bytes=mib << 20),
        cost_estimate=pl.CostEstimate(flops=flops, bytes_accessed=nbytes, transcendentals=0),
    )(*operands)


def in_hbm(x):
    return pltpu.with_memory_space_constraint(x, pltpu.HBM)


def lane_iota(shape):
    return lax.broadcasted_iota(jnp.int32, shape, len(shape) - 1)


def even_level():
    return lax.rem(lax.axis_index("lev"), 2) == 0


def pack_kernel(levels, cols, v_hbm, vel_hbm, owner_hbm, lo, hi, lev_a, lev_b, counts, v, vel, owner, sems):
    copies = [pltpu.make_async_copy(v_hbm, v, sems.at[0]), pltpu.make_async_copy(owner_hbm, owner, sems.at[1])]
    for section in range(2):
        for comp in range(3):
            sem = sems.at[2 + 3 * section + comp]
            copies.append(pltpu.make_async_copy(vel_hbm.at[section, comp], vel.at[section, comp], sem))
    for copy in copies:
        copy.start()

    def edge(low, n):
        return slice(0, n) if low else slice(cols - n, cols)

    sides = ((lo, True), (hi, False))
    even = even_level()
    tops = ((lev_a, even), (lev_b, jnp.logical_not(even)))
    copies[0].wait()
    for msg, low in sides:
        for lev in range(levels):
            msg[lev * LEVEL_ROWS : lev * LEVEL_ROWS + V_ROWS] = v[lev, edge(low, V_ROWS)]
    for msg, top in tops:
        msg[0] = v[jnp.where(top, levels - 1, 0)]
        msg[1] = v[jnp.where(top, levels - 2, 1)]
    copies[1].wait()
    lanes = lane_iota((1, 128))
    row = jnp.zeros((1, 128), f32)
    held = owner[...]
    for box in range(1, NBOX + 1):
        hot = jnp.sum((held == box).astype(f32), axis=0, keepdims=True)
        row = jnp.where(lanes == box - 1, jnp.sum(hot, axis=1, keepdims=True), row)
    counts[...] = row
    at = levels * LEVEL_ROWS
    for msg, low in sides:
        msg[at : at + B_ROWS] = owner[edge(low, B_ROWS)].astype(f32)
        msg[at + B_ROWS : at + B_ROWS + 1, 0:128] = row
    for section, n, start in ((0, A_ROWS, V_ROWS), (1, B_ROWS, B_AT)):
        for comp in range(3):
            copies[2 + 3 * section + comp].wait()
            for msg, low in sides:
                for lev in range(levels):
                    at = lev * LEVEL_ROWS + start + comp * n
                    msg[at : at + n] = vel[section, comp, lev, edge(low, n)]
            if section == 0:
                for msg, top in tops:
                    msg[2 + comp] = vel[0, comp, jnp.where(top, levels - 1, 0)]


def unpack(west, east, n, at):
    gap = jnp.zeros((CHUNK - 2 * n, west.shape[1]), f32)
    parts = [east[at : at + n], gap, west[at : at + n]]
    return jnp.concatenate([x for x in parts if x.shape[0]], axis=0)


def corner_kernel(levels, west, east, window, corner_a, corner_b):
    even = even_level()

    def put(item, top, bottom):
        corner_a[item] = jnp.where(even, top, bottom)
        corner_b[item] = jnp.where(even, bottom, top)

    def both(n, start, near=0):
        return [unpack(west, east, n, lev * LEVEL_ROWS + start) for lev in (levels - 1 - near, near)]

    put(0, *both(V_ROWS, 0))
    put(1, *both(V_ROWS, 0, 1))
    for comp in range(3):
        put(2 + comp, *both(A_ROWS, V_ROWS + comp * A_ROWS))


def window_kernel(levels, west, east, counts, counts_2, order, after, window):
    at = levels * LEVEL_ROWS + B_ROWS
    window[...] = counts[...] + counts_2[...] + west[at : at + 1, 0:128] + east[at : at + 1, 0:128]


class Block:
    def __init__(self, levels, cols, lat):
        self.levels, self.lat, self.chunks = levels, lat, cols // CHUNK
        level = lax.axis_index("lev")
        self.has = (level > 0, level < lax.axis_size("lev") - 1)
        self.even = even_level()
        lanes = lane_iota((CHUNK, lat))
        self.first_lane, self.last_lane = lanes == 0, lanes == lat - 1

    def put_west(self, ref, at, k, value):
        ref[at, rows(k)] = value
        if k == self.chunks:
            ref[at, 0:CHUNK] = value

    def put_east(self, ref, at, k, value):
        ref[at, rows(k)] = value
        if k == 0:
            ref[at, rows(self.chunks + 1)] = value

    def put_both(self, ref, at, k, value):
        self.put_west(ref, at, k, value)
        if k == 0:
            ref[at, rows(self.chunks + 1)] = value

    def from_south(self, x):
        return jnp.where(self.first_lane, 0.0, pltpu.roll(x, 1, 1))

    def from_north(self, x):
        return jnp.where(self.last_lane, 0.0, pltpu.roll(x, self.lat - 1, 1))

    def beyond(self, got_a, got_b, src, k, vv, la):
        for item in range(5):
            a, b = got_a[item, src], got_b[item, src]
            below, above = jnp.where(self.even, b, a), jnp.where(self.even, a, b)
            if item < 2:
                self.put_both(vv, 1 - item, k, jnp.where(self.has[0], below, 0.0))
                self.put_both(vv, self.levels + 2 + item, k, jnp.where(self.has[1], above, 0.0))
            else:
                la[0, item - 2, tile(k)] = below
                la[1, item - 2, tile(k)] = above

    def tangent(self, ref, at, k, abc):
        here = ref[at, rows(k)]
        e, w = ref[at, rows(k, 1)], ref[at, rows(k, -1)]
        n, s = self.from_north(here), self.from_south(here)
        u, d = ref[at + 1, rows(k)], ref[at - 1, rows(k)]
        a, b, c = abc
        around = ((e + w) + (n + s)) + (u + d)
        drift = a * (w - e) + b * (s - n) + c * (d - u)
        return centre * here + kappa * around + 0.5 * drift

    def first_beyond(self, vv, la, ff, k):
        for side, at in ((0, 0), (1, self.levels + 1)):
            value = self.tangent(vv, at + 1, k, [la[side, comp, tile(k)] for comp in range(3)])
            self.put_both(ff, at, k, jnp.where(self.has[side], value, 0.0))

    def push(self, x, abc, dst, at, k):
        inside, to_e, to_w, to_u, to_d = dst
        a, b, c = abc
        base, half = kappa * x, 0.5 * x
        a, b, c = a * half, b * half, c * half
        inside[at, rows(k)] = centre * x + (self.from_south(base - b) + self.from_north(base + b))
        self.put_west(to_e, at, k, base - a)
        self.put_east(to_w, at, k, base + a)
        to_u[at, rows(k)] = base - c
        to_d[at, rows(k)] = base + c


def rows(k, shift=0):
    return slice(CHUNK * (k + 1) + shift, CHUNK * (k + 2) + shift)


def tile(k):
    return slice(CHUNK * k, CHUNK * (k + 1))


def lev_kernel(levels, cols, lat, lev_a, lev_b, vv, la):
    block = Block(levels, cols, lat)
    for k in range(block.chunks):
        block.beyond(lev_a, lev_b, tile(k), k, vv, la)


def first_kernel(levels, cols, lat, v, vel, west, east, vv_in, la, vv, ff, xx, halo_a, halo_b):
    block = Block(levels, cols, lat)
    last = block.chunks
    for lev in range(levels):
        for k in range(last):
            block.put_both(vv, lev + 2, k, v[lev, tile(k)])
        block.put_both(vv, lev + 2, last, unpack(west, east, V_ROWS, lev * LEVEL_ROWS))
        for comp in range(3):
            base = lev * LEVEL_ROWS + V_ROWS
            halo_a[comp, lev] = unpack(west, east, A_ROWS, base + comp * A_ROWS)
            halo_b[comp, lev] = unpack(west, east, B_ROWS, base + 3 * A_ROWS + comp * B_ROWS)

    def flow(section, lev, k):
        return [vel[section, comp, lev, tile(k)] for comp in range(3)]

    def first_level(lev, carry):
        for k in range(last):
            block.put_both(ff, lev + 1, k, block.tangent(vv, lev + 2, k, flow(0, lev, k)))
        return carry

    lax.fori_loop(0, levels, first_level, 0, unroll=True)
    for k in range(1, last - 1):
        block.first_beyond(vv, la, ff, k)

    def inner_level(lev, carry):
        abc = [halo_a[comp, lev] for comp in range(3)]
        block.put_both(ff, lev + 1, last, block.tangent(vv, lev + 2, last, abc))
        for k in range(last):
            xx[lev, tile(k)] = block.tangent(ff, lev + 1, k, flow(1, lev, k))
        return carry

    lax.fori_loop(1, levels - 1, inner_level, 0, unroll=True)


def edge_kernel(levels, cols, lat, vel, halo_a, halo_b, corner_a, corner_b, vv_in, la_in, ff_in, xx_in, vv, la, ff, xx):
    block = Block(levels, cols, lat)
    last = block.chunks
    block.beyond(corner_a, corner_b, slice(0, CHUNK), last, vv, la)
    for k in (0, last - 1, last):
        block.first_beyond(vv, la, ff, k)
    for lev in (0, levels - 1):
        abc = [halo_a[comp, lev] for comp in range(3)]
        block.put_both(ff, lev + 1, last, block.tangent(vv, lev + 2, last, abc))
    for lev in range(levels):
        if lev in (0, levels - 1):
            for k in range(last):
                abc = [vel[1, comp, lev, tile(k)] for comp in range(3)]
                xx[lev, tile(k)] = block.tangent(ff, lev + 1, k, abc)
        xx[lev, tile(last)] = block.tangent(ff, lev + 1, last, [halo_b[comp, lev] for comp in range(3)])


def stencil_kernel(
    levels, cols, lat, columns, n_counts, lw, vel, owner, west, east, halo_a, halo_b, la, xx, *refs
):
    count_refs = refs[:n_counts]
    applied, send_a, send_b = refs[n_counts : n_counts + 3]
    (own_h, w_in, w_e, w_w, w_u, w_d, u_in, u_e, u_w, u_u, u_d, out) = refs[n_counts + 3 :]
    block = Block(levels, cols, lat)
    chunks, has, even, push = block.chunks, block.has, block.even, block.push
    own_h[...] = unpack(west, east, B_ROWS, levels * LEVEL_ROWS)

    def flow(section, k, lev):
        if k < chunks:
            return [vel[section, comp, lev, tile(k)] for comp in range(3)]
        return [(halo_b if section else halo_a)[comp, lev] for comp in range(3)]

    def flow_beyond(side, k):
        return [la[side, comp, tile(k)] for comp in range(3)]

    total = count_refs[0][...]
    for ref in count_refs[1:]:
        total = total + ref[...]
    scales = columns / (NBOX * jnp.maximum(total, 1.0))
    for k in range(chunks + 1):
        mine = owner[CHUNK * k : CHUNK * (k + 1)].astype(f32) if k < chunks else own_h[...]
        factor = jnp.zeros((CHUNK, lat), f32)
        for box in range(1, NBOX + 1):
            factor = jnp.where(mine == float(box), jnp.broadcast_to(scales[:, box - 1 : box], (CHUNK, lat)), factor)
        out[0, CHUNK * k : CHUNK * (k + 1)] = factor

    def second_level(lev, carry):
        weight = lw[lev]
        for k in range(chunks + 1):
            abc = flow(1, k, lev)
            x = (weight * out[0, tile(k)]) * xx[lev, tile(k)]
            push(x, abc, (w_in, w_e, w_w, w_u, w_d), lev + 1, k)
        return carry

    lax.fori_loop(0, levels, second_level, 0, unroll=True)
    for k in range(chunks + 1):
        w_u[0, rows(k)] = jnp.zeros((CHUNK, lat), f32)
        w_d[levels + 1, rows(k)] = jnp.zeros((CHUNK, lat), f32)

    def third_level(lev, carry):
        for k in range(chunks + 1):
            x = (
                w_in[lev + 1, rows(k)]
                + (w_e[lev + 1, rows(k, -1)] + w_w[lev + 1, rows(k, 1)])
                + (w_u[lev, rows(k)] + w_d[lev + 2, rows(k)])
            )
            push(x, flow(0, k, lev), (u_in, u_e, u_w, u_u, u_d), lev + 1, k)
        return carry

    lax.fori_loop(0, levels, third_level, 0, unroll=True)
    for k in range(chunks + 1):
        for side, at, x in ((0, 0, w_d[1, rows(k)]), (1, levels + 1, w_u[levels, rows(k)])):
            x = jnp.where(has[side], x, 0.0)
            push(x, flow_beyond(side, k), (u_in, u_e, u_w, u_u, u_d), at, k)

    for k in range(chunks):
        cells = slice(CHUNK * k, CHUNK * (k + 1))
        out[0, cells] = u_d[0, rows(k)]
        out[levels + 3, cells] = u_u[levels + 1, rows(k)]
        for at in range(levels + 2):
            x = u_in[at, rows(k)] + (u_e[at, rows(k, -1)] + u_w[at, rows(k, 1)])
            if at > 0:
                x = x + u_u[at - 1, rows(k)]
            if at < levels + 1:
                x = x + u_d[at + 1, rows(k)]
            if 1 <= at <= levels:
                applied[at - 1, cells] = x
            else:
                out[at + 1, cells] = x
    up = jnp.where(even, levels + 2, 0)
    down = levels + 2 - up
    for i in range(SECOND):
        send_a[i] = out[up + i, 0:cols]
        send_b[i] = out[down + i, 0:cols]


def put_sum(rows_ref, at, acc):
    rows_ref[at : at + 1] = jnp.sum(acc, axis=0, keepdims=True)


def to_lanes(rows_ref, at):
    return jnp.sum(jnp.transpose(rows_ref[at : at + 128, :]), axis=0, keepdims=True)


def tiles(lat):
    return [slice(t, t + 128) for t in range(0, lat, 128)]


def load_kernel(beta_prev, s_hbm, prev_hbm, order, beta_out, s, prev, sems):
    copies = [pltpu.make_async_copy(s_hbm.at[i], s.at[i], sems.at[i]) for i in range(s.shape[0])]
    copies.append(pltpu.make_async_copy(prev_hbm, prev, sems.at[s.shape[0]]))
    for copy in copies:
        copy.start()
    beta_out[...] = jnp.full((1, 128), beta_prev[0], f32)
    for copy in copies:
        copy.wait()


def gram_kernel(nvec, levels, cols, lat, s, v, order, out, sums):
    sums[...] = jnp.zeros(sums.shape, f32)
    steps = levels * (cols // CHUNK)
    block = 4

    def place(step):
        lev = step // (cols // CHUNK)
        row = pl.multiple_of((step - lev * (cols // CHUNK)) * CHUNK, CHUNK)
        return lev, pl.ds(row, CHUNK)

    for i0 in range(0, nvec, block):
        for j0 in range(i0, nvec, block):
            pairs = [(i, j) for i in range(i0, i0 + block) for j in range(j0, j0 + block) if i <= j]

            def body(step, acc, pairs=pairs, need=sorted({*range(i0, i0 + block), *range(j0, j0 + block)})):
                lev, cells = place(step)
                for t in tiles(lat):
                    held = {i: s[i, lev, cells, t] for i in need}
                    acc = tuple(x + held[i] * held[j] for x, (i, j) in zip(acc, pairs))
                return acc

            acc = lax.fori_loop(0, steps, body, tuple(jnp.zeros((CHUNK, 128), f32) for _ in pairs), unroll=4)
            for (i, j), x in zip(pairs, acc):
                put_sum(sums, nvec * i + j, x)

    def body_v(step, acc):
        lev, cells = place(step)
        for t in tiles(lat):
            x = v[lev, cells, t]
            acc = tuple(y + x * s[i, lev, cells, t] for i, y in enumerate(acc[:-1])) + (acc[-1] + x * x,)
        return acc

    acc = lax.fori_loop(0, steps, body_v, tuple(jnp.zeros((CHUNK, 128), f32) for _ in range(nvec + 1)), unroll=2)
    base = nvec * nvec
    for i in range(nvec):
        put_sum(sums, base + nvec + i, acc[i])
    put_sum(sums, base + 2 * nvec + 2, acc[nvec])
    for r in range(base // 128 + 1):
        out[r : r + 1] = to_lanes(sums, 128 * r)


def gather_kernel(nvec, levels, cols, lat, count, part, got_a, got_b, prev, beta_prev, v, s, gram, applied, msg, sums):
    level = lax.axis_index("lev")
    has = (level > 0, level < lax.axis_size("lev") - 1)
    even = even_level()
    beta = jnp.broadcast_to(beta_prev[:, 0:1], (CHUNK, lat))
    for k in range(cols // CHUNK):
        cells = slice(CHUNK * k, CHUNK * (k + 1))
        for lev in range(levels):
            x = part[lev, cells] - beta * prev[lev, cells]
            if lev < SECOND:
                x = x + jnp.where(has[0], jnp.where(even, got_b[lev, cells], got_a[lev, cells]), 0.0)
            if lev >= levels - SECOND:
                i = lev - levels + SECOND
                x = x + jnp.where(has[1], jnp.where(even, got_a[i, cells], got_b[i, cells]), 0.0)
            applied[lev, cells] = x
    sums[...] = jnp.zeros(sums.shape, f32)
    steps = levels * (cols // CHUNK)

    def body(step, acc):
        lev = step // (cols // CHUNK)
        cells = pl.ds(pl.multiple_of((step - lev * (cols // CHUNK)) * CHUNK, CHUNK), CHUNK)
        for t in tiles(lat):
            x = applied[lev, cells, t]
            acc = tuple(y + x * s[i, lev, cells, t] for i, y in enumerate(acc[:nvec])) + (
                acc[nvec] + x * x,
                acc[nvec + 1] + x * v[lev, cells, t],
            )
        return acc

    acc = lax.fori_loop(0, steps, body, tuple(jnp.zeros((CHUNK, 128), f32) for _ in range(nvec + 2)), unroll=4)
    for i in range(nvec):
        put_sum(sums, i, acc[i])
    put_sum(sums, 2 * nvec, acc[nvec])
    put_sum(sums, 2 * nvec + 1, acc[nvec + 1])
    r = gram.shape[0] - 1
    row = to_lanes(sums, 0) + gram[r : r + 1]
    msg[:, 0:r] = jnp.broadcast_to(gram[0:r][None], (count, r, 128))
    msg[:, r : r + 1] = jnp.broadcast_to(row[None], (count, 1, 128))


def orthogonal_kernel(nvec, levels, cols, lat, cells_all, msg, applied, v, s, orthogonal, out, trust):
    total = jnp.sum(msg[...], axis=0) * (1.0 / cells_all)
    r = total.shape[0] - 1
    row = total[r : r + 1]
    aa = row[:, 2 * nvec : 2 * nvec + 1]
    alpha = row[:, 2 * nvec + 1 : 2 * nvec + 2]
    vv = row[:, 2 * nvec + 2 : 2 * nvec + 3]
    lanes = lane_iota((1, 128))
    pv = row - alpha * pltpu.roll(row, 128 - nvec, 1)
    p = [jnp.broadcast_to(pv[:, k : k + 1], (1, 128)) for k in range(nvec)]
    tiled = jnp.zeros((1, 128), f32)
    for k in range(nvec):
        tiled = jnp.where(lax.rem(lanes, nvec) == k, p[k], tiled)
    quad = jnp.zeros((1, 128), f32)
    per = 128 // nvec
    for g in range(r):
        rep = jnp.zeros((1, 128), f32)
        for i in range(per):
            rep = jnp.where(lanes // nvec == i, p[g * per + i], rep)
        i, j = g * per + lanes // nvec, lax.rem(lanes, nvec)
        weight = jnp.where(i == j, 1.0, jnp.where(i < j, 2.0, 0.0))
        quad = quad + weight * rep * tiled * total[g : g + 1]
    quad = jnp.sum(quad, axis=1, keepdims=True)
    pp = jnp.sum(jnp.where(lanes < nvec, pv * pv, 0.0), axis=1, keepdims=True)
    square = (aa - 2.0 * alpha * alpha + alpha * alpha * vv) + (quad - 2.0 * pp)
    size = aa + alpha * alpha * (2.0 + vv) + 2.0 * pp + jnp.abs(quad)
    trust[...] = jnp.where((square > 0.03125 * size) & (size < 1e36), 1.0, 0.0)
    beta = jnp.sqrt(square + 1e-12)
    out[...] = jnp.where(lanes == 0, alpha, jnp.where(lanes == 1, beta, pltpu.roll(pv, 2, 1)))


    a_w = jnp.broadcast_to(alpha, (CHUNK, 128))
    weights = [jnp.broadcast_to(x, (CHUNK, 128)) for x in p]

    for lev in range(levels):
        for k in range(cols // CHUNK):
            for t in tiles(lat):
                x = applied[lev, tile(k), t] - a_w * v[lev, tile(k), t]
                y = [weights[k0] * s[k0, lev, tile(k), t] for k0 in range(nvec)]
                while len(y) > 1:
                    y = [a + b for a, b in zip(y[::2], y[1::2])] + y[len(y) & ~1 :]
                orthogonal[lev, tile(k), t] = x - y[0]


def scale_kernel(nvec, row, orthogonal, result_out, coefs_out, result, coefs, sems):
    line = row[...]
    coefs[...] = line[:, 0 : nvec + 2]
    copies = [pltpu.make_async_copy(result.at[i], result_out.at[i], sems.at[i]) for i in range(result.shape[0])]
    copies.append(pltpu.make_async_copy(coefs, coefs_out, sems.at[result.shape[0]]))
    copies[-1].start()
    inverse = 1.0 / line[:, 1:2]
    for i in range(result.shape[0]):
        result[i] = orthogonal[i] * inverse
        copies[i].start()
    for copy in copies:
        copy.wait()


def body(v, prev, beta_prev, s, vel, lw, owner):
    lon_n, lev_n = lax.axis_size("lon"), lax.axis_size("lev")
    count = lon_n * lev_n
    levels, cols, lat = v.shape
    nvec = s.shape[0]
    lines = levels * LEVEL_ROWS + B_ROWS + 1
    lines += -lines % CHUNK

    lo, hi, lev_a, lev_b, counts, v, vel, owner = call(
        functools.partial(pack_kernel, levels, cols),
        (sds(lines, lat), sds(lines, lat), sds(5, cols, lat), sds(5, cols, lat), sds(1, 128),
         sds(*v.shape), sds(*vel.shape), jax.ShapeDtypeStruct(owner.shape, owner.dtype)),
        tuple(in_hbm(x) for x in (v, vel, owner)), specs=[HBM] * 3, scratch=[pltpu.SemaphoreType.DMA((8,))], flops=1 << 20,
    )
    east_of = [(i, (i + 1) % lon_n) for i in range(lon_n)]
    west_of = [((i + 1) % lon_n, i) for i in range(lon_n)]
    pairs_a = [(i, i ^ 1) for i in range(lev_n)]
    pairs_b = []
    for i in range(count):
        at, level = divmod(i, lev_n)
        if level in (0, lev_n - 1):
            pairs_b.append((i, (at ^ 1) * lev_n + level))
        else:
            pairs_b.append((i, i + 1 if level % 2 else i - 1))

    def both(a, b):
        return lax.ppermute(a, "lev", pairs_a), lax.ppermute(b, ("lon", "lev"), pairs_b)

    around = [(i, (i + 1) % lev_n if i % 2 else (i - 1) % lev_n) for i in range(lev_n)]

    west, east = lax.ppermute(hi, "lon", east_of), lax.ppermute(lo, "lon", west_of)
    lev_a, lev_b = lax.ppermute(lev_a, "lev", pairs_a), lax.ppermute(lev_b, "lev", around)
    counts_2 = lax.ppermute(counts, "lon", [((i + 2) % lon_n, i) for i in range(lon_n)])

    beta_row, s, prev = call(
        load_kernel, (sds(1, 128), sds(*s.shape), sds(*prev.shape)),
        (beta_prev.reshape(1), in_hbm(s), in_hbm(prev), counts), specs=[SM, HBM, HBM, VM],
        scratch=[pltpu.SemaphoreType.DMA((nvec + 1,))],
    )
    padded = cols + 3 * CHUNK
    vv, la = call(
        functools.partial(lev_kernel, levels, cols, lat),
        (sds(levels + 4, padded, lat), sds(2, 3, cols + CHUNK, lat)), (lev_a, lev_b),
    )
    window = call(
        functools.partial(window_kernel, levels), sds(1, 128), (west, east, counts, counts_2, beta_row, la)
    )
    if lon_n == 8:
        near = [window, lax.ppermute(window, "lon", [(i, i ^ 4) for i in range(lon_n)])]
    else:
        near = [lax.psum(counts, "lon")]
    corner_a, corner_b = call(
        functools.partial(corner_kernel, levels),
        (sds(5, CHUNK, lat), sds(5, CHUNK, lat)), (west, east, window),
    )
    corner_a, corner_b = both(corner_a, corner_b)

    vv, ff, xx, halo_a, halo_b = call(
        functools.partial(first_kernel, levels, cols, lat),
        (sds(*vv.shape), sds(levels + 2, padded, lat), sds(levels, cols + CHUNK, lat),
         sds(3, levels, CHUNK, lat), sds(3, levels, CHUNK, lat)),
        (v, vel, west, east, vv, la), alias={4: 0}, flops=4 << 20,
    )
    vv, la, ff, xx = call(
        functools.partial(edge_kernel, levels, cols, lat), tuple(sds(*x.shape) for x in (vv, la, ff, xx)),
        (vel, halo_a, halo_b, corner_a, corner_b, vv, la, ff, xx), alias={5: 0, 6: 1, 7: 2, 8: 3}, flops=2 << 20,
    )
    scratch = [pltpu.VMEM((CHUNK, lat), f32)]
    scratch += [pltpu.VMEM((levels + 2, padded, lat), f32)] * 10
    scratch += [pltpu.VMEM((levels + 4, cols + CHUNK, lat), f32)]
    operands = (lw, vel, owner, west, east, halo_a, halo_b, la, xx, *near)
    part, send_a, send_b = call(
        functools.partial(stencil_kernel, levels, cols, lat, float(cols * lon_n * lat), len(near)),
        (sds(levels, cols, lat), sds(SECOND, cols, lat), sds(SECOND, cols, lat)),
        operands, specs=[SM] + [VM] * (len(operands) - 1), scratch=scratch, flops=8 << 20, mib=12,
    )
    got_a, got_b = both(send_a, send_b)
    gram_rows = nvec * nvec // 128 + 1
    gram = call(
        functools.partial(gram_kernel, nvec, levels, cols, lat),
        sds(gram_rows, 128), (s, v, send_a),
        scratch=[pltpu.VMEM((128 * gram_rows, 128), f32)], flops=20 << 20,
    )
    applied, msg = call(
        functools.partial(gather_kernel, nvec, levels, cols, lat, count),
        (sds(levels, cols, lat), sds(count, gram_rows, 128)),
        (part, got_a, got_b, prev, beta_row, v, s, gram),
        scratch=[pltpu.VMEM((128, 128), f32)],
    )
    msg = lax.all_to_all(msg, ("lon", "lev"), 0, 0, tiled=True)
    cells = float(v.size * count)
    orthogonal, row, trust = call(
        functools.partial(orthogonal_kernel, nvec, levels, cols, lat, cells),
        (sds(levels, cols, lat), sds(1, 128), sds(1, 1)), (msg, applied, v, s),
    )

    def direct():
        square = lax.psum(jnp.sum(orthogonal * orthogonal), ("lon", "lev")) / cells
        return row.at[0, 1].set(jnp.sqrt(square + 1e-12))

    row = lax.cond(trust[0, 0] > 0.5, lambda: row, direct)
    result, coefs = call(
        functools.partial(scale_kernel, nvec),
        (sds(levels, cols, lat), sds(1, nvec + 2)),
        (row, orthogonal), out_specs=(HBM, HBM),
        scratch=[pltpu.VMEM((levels, cols, lat), f32), pltpu.VMEM((1, nvec + 2), f32),
                 pltpu.SemaphoreType.DMA((levels + 1,))],
    )
    return result, coefs.reshape(nvec + 2)


def solution(mesh):
    placed = (
        P("lev", "lon", None),
        P("lev", "lon", None),
        P(),
        P(None, "lev", "lon", None),
        P(None, None, "lev", "lon", None),
        P("lev"),
        P("lon", None),
    )
    return jax.shard_map(
        body, mesh=mesh, in_specs=placed, out_specs=(P("lev", "lon", None), P()), check_vma=False
    )
```

```python
import functools

import jax
import jax.numpy as jnp
from jax import lax
from jax.experimental import pallas as pl
from jax.experimental.pallas import tpu as pltpu
from jax.sharding import PartitionSpec as P

NBOX = 5
kappa = 0.1
centre = 1.0 - 6.0 * kappa
f32 = jnp.float32

VM = pl.BlockSpec(memory_space=pltpu.VMEM)
SM = pl.BlockSpec(memory_space=pltpu.SMEM)
HBM = pl.BlockSpec(memory_space=pltpu.HBM)
CHUNK = 8
WIDE = 4
SECOND = 2
V_ROWS, A_ROWS, B_ROWS = 4, 3, 2
LEVEL_ROWS = V_ROWS + 3 * (A_ROWS + B_ROWS)
B_AT = V_ROWS + 3 * A_ROWS


def sds(*shape):
    return jax.ShapeDtypeStruct(shape, f32)


def call(kernel, outs, operands, specs=None, scratch=(), flops=0, alias=None, out_specs=None, mib=4):
    nbytes = sum(4 * x.size for x in operands)
    return pl.pallas_call(
        kernel,
        out_shape=outs,
        in_specs=specs or [VM] * len(operands),
        out_specs=out_specs or jax.tree.map(lambda _: VM, outs),
        scratch_shapes=list(scratch),
        input_output_aliases=alias or {},
        compiler_params=pltpu.CompilerParams(vmem_limit_bytes=mib << 20),
        cost_estimate=pl.CostEstimate(flops=flops, bytes_accessed=nbytes, transcendentals=0),
    )(*operands)


def in_hbm(x):
    return pltpu.with_memory_space_constraint(x, pltpu.HBM)


def lane_iota(shape):
    return lax.broadcasted_iota(jnp.int32, shape, len(shape) - 1)


def even_level():
    return lax.rem(lax.axis_index("lev"), 2) == 0


def pack_kernel(levels, cols, v_hbm, vel_hbm, owner_hbm, lo, hi, lev_a, lev_b, counts, v, vel, owner, sems):
    copies = [pltpu.make_async_copy(v_hbm, v, sems.at[0]), pltpu.make_async_copy(owner_hbm, owner, sems.at[1])]
    for section in range(2):
        for comp in range(3):
            sem = sems.at[2 + 3 * section + comp]
            copies.append(pltpu.make_async_copy(vel_hbm.at[section, comp], vel.at[section, comp], sem))
    for copy in copies:
        copy.start()

    def edge(low, n):
        return slice(0, n) if low else slice(cols - n, cols)

    sides = ((lo, True), (hi, False))
    even = even_level()
    tops = ((lev_a, even), (lev_b, jnp.logical_not(even)))
    copies[0].wait()
    for msg, low in sides:
        for lev in range(levels):
            msg[lev * LEVEL_ROWS : lev * LEVEL_ROWS + V_ROWS] = v[lev, edge(low, V_ROWS)]
    for msg, top in tops:
        msg[0] = v[jnp.where(top, levels - 1, 0)]
        msg[1] = v[jnp.where(top, levels - 2, 1)]
    copies[1].wait()
    lanes = lane_iota((1, 128))
    row = jnp.zeros((1, 128), f32)
    held = owner[...]
    for box in range(1, NBOX + 1):
        hot = jnp.sum((held == box).astype(f32), axis=0, keepdims=True)
        row = jnp.where(lanes == box - 1, jnp.sum(hot, axis=1, keepdims=True), row)
    counts[...] = row
    at = levels * LEVEL_ROWS
    for msg, low in sides:
        msg[at : at + B_ROWS] = owner[edge(low, B_ROWS)].astype(f32)
        msg[at + B_ROWS : at + B_ROWS + 1, 0:128] = row
    for section, n, start in ((0, A_ROWS, V_ROWS), (1, B_ROWS, B_AT)):
        for comp in range(3):
            copies[2 + 3 * section + comp].wait()
            for msg, low in sides:
                for lev in range(levels):
                    at = lev * LEVEL_ROWS + start + comp * n
                    msg[at : at + n] = vel[section, comp, lev, edge(low, n)]
            if section == 0:
                for msg, top in tops:
                    msg[2 + comp] = vel[0, comp, jnp.where(top, levels - 1, 0)]


def unpack(west, east, n, at):
    gap = jnp.zeros((CHUNK - 2 * n, west.shape[1]), f32)
    parts = [east[at : at + n], gap, west[at : at + n]]
    return jnp.concatenate([x for x in parts if x.shape[0]], axis=0)


CORNER_ROWS = (3, 2, 2, 2, 2)


def corner_at(item):
    return 2 * sum(CORNER_ROWS[:item])


def corner_kernel(levels, west, east, window, corner_a, corner_b):
    even = even_level()

    def part(item, lev):
        n = CORNER_ROWS[item]
        held = V_ROWS if item < 2 else A_ROWS
        at = lev * LEVEL_ROWS + (0 if item < 2 else V_ROWS + (item - 2) * A_ROWS)
        return east[at : at + n], west[at + held - n : at + held]

    for item, n in enumerate(CORNER_ROWS):
        near = int(item == 1)
        for i, (top, bottom) in enumerate(zip(part(item, levels - 1 - near), part(item, near))):
            at = corner_at(item) + i * n
            corner_a[at : at + n] = jnp.where(even, top, bottom)
            corner_b[at : at + n] = jnp.where(even, bottom, top)


def window_kernel(levels, west, east, counts, counts_2, order, window):
    at = levels * LEVEL_ROWS + B_ROWS
    window[...] = counts[...] + counts_2[...] + west[at : at + 1, 0:128] + east[at : at + 1, 0:128]


class Block:
    def __init__(self, levels, cols, lat):
        self.levels, self.lat, self.chunks = levels, lat, cols // CHUNK
        level = lax.axis_index("lev")
        self.has = (level > 0, level < lax.axis_size("lev") - 1)
        self.even = even_level()
        lanes = lane_iota((CHUNK, lat))
        self.first_lane, self.last_lane = lanes == 0, lanes == lat - 1

    def put_west(self, ref, at, k, value):
        ref[at, rows(k)] = value
        if k == self.chunks:
            ref[at, 0:CHUNK] = value

    def put_east(self, ref, at, k, value):
        ref[at, rows(k)] = value
        if k == 0:
            ref[at, rows(self.chunks + 1)] = value

    def put_both(self, ref, at, k, value):
        self.put_west(ref, at, k, value)
        if k == 0:
            ref[at, rows(self.chunks + 1)] = value

    def from_south(self, x):
        return jnp.where(self.first_lane, 0.0, pltpu.roll(x, 1, 1))

    def from_north(self, x):
        return jnp.where(self.last_lane, 0.0, pltpu.roll(x, self.lat - 1, 1))

    def beyond(self, got_a, got_b, k, vv, la):
        for item in range(5):
            if k < self.chunks:
                a, b = got_a[item, tile(k)], got_b[item, tile(k)]
            else:
                n, at = CORNER_ROWS[item], corner_at(item)
                gap = jnp.zeros((CHUNK - 2 * n, self.lat), f32)
                a, b = (jnp.concatenate([x[at : at + n], gap, x[at + n : at + 2 * n]], axis=0) for x in (got_a, got_b))
            below, above = jnp.where(self.even, b, a), jnp.where(self.even, a, b)
            if item < 2:
                self.put_both(vv, 1 - item, k, jnp.where(self.has[0], below, 0.0))
                self.put_both(vv, self.levels + 2 + item, k, jnp.where(self.has[1], above, 0.0))
            else:
                la[0, item - 2, tile(k)] = below
                la[1, item - 2, tile(k)] = above

    def tangent(self, ref, at, k, abc):
        here = ref[at, rows(k)]
        e, w = ref[at, rows(k, 1)], ref[at, rows(k, -1)]
        n, s = self.from_north(here), self.from_south(here)
        u, d = ref[at + 1, rows(k)], ref[at - 1, rows(k)]
        a, b, c = abc
        around = ((e + w) + (n + s)) + (u + d)
        drift = a * (w - e) + b * (s - n) + c * (d - u)
        return centre * here + kappa * around + 0.5 * drift

    def first_beyond(self, vv, la, ff, k):
        for side, at in ((0, 0), (1, self.levels + 1)):
            value = self.tangent(vv, at + 1, k, [la[side, comp, tile(k)] for comp in range(3)])
            self.put_both(ff, at, k, jnp.where(self.has[side], value, 0.0))

    def push(self, x, abc, dst, at, k):
        inside, to_e, to_w, to_u, to_d = dst
        a, b, c = abc
        base, half = kappa * x, 0.5 * x
        a, b, c = a * half, b * half, c * half
        inside[at, rows(k)] = centre * x + (self.from_south(base - b) + self.from_north(base + b))
        self.put_west(to_e, at, k, base - a)
        self.put_east(to_w, at, k, base + a)
        to_u[at, rows(k)] = base - c
        to_d[at, rows(k)] = base + c


def rows(k, shift=0):
    return slice(CHUNK * (k + 1) + shift, CHUNK * (k + 2) + shift)


def tile(k):
    return slice(CHUNK * k, CHUNK * (k + 1))


def lev_kernel(levels, cols, lat, lev_a, lev_b, vv, la):
    block = Block(levels, cols, lat)
    for k in range(block.chunks):
        block.beyond(lev_a, lev_b, k, vv, la)


def first_kernel(levels, cols, lat, v, vel, west, east, vv_in, la, vv, ff, xx, halo_a, halo_b):
    block = Block(levels, cols, lat)
    last = block.chunks
    for lev in range(levels):
        for k in range(last):
            block.put_both(vv, lev + 2, k, v[lev, tile(k)])
        block.put_both(vv, lev + 2, last, unpack(west, east, V_ROWS, lev * LEVEL_ROWS))
        for comp in range(3):
            base = lev * LEVEL_ROWS + V_ROWS
            halo_a[comp, lev] = unpack(west, east, A_ROWS, base + comp * A_ROWS)
            halo_b[comp, lev] = unpack(west, east, B_ROWS, base + 3 * A_ROWS + comp * B_ROWS)

    def flow(section, lev, k):
        return [vel[section, comp, lev, tile(k)] for comp in range(3)]

    def first_level(lev, carry):
        for k in range(last):
            block.put_both(ff, lev + 1, k, block.tangent(vv, lev + 2, k, flow(0, lev, k)))
        return carry

    lax.fori_loop(0, levels, first_level, 0, unroll=True)
    for k in range(1, last - 1):
        block.first_beyond(vv, la, ff, k)

    def inner_level(lev, carry):
        abc = [halo_a[comp, lev] for comp in range(3)]
        block.put_both(ff, lev + 1, last, block.tangent(vv, lev + 2, last, abc))
        for k in range(last):
            xx[lev, tile(k)] = block.tangent(ff, lev + 1, k, flow(1, lev, k))
        return carry

    lax.fori_loop(1, levels - 1, inner_level, 0, unroll=True)


def edge_kernel(levels, cols, lat, vel, halo_a, halo_b, corner_a, corner_b, vv_in, la_in, ff_in, xx_in, factor, vv, la, ff, xx):
    block = Block(levels, cols, lat)
    last = block.chunks
    block.beyond(corner_a, corner_b, last, vv, la)
    for k in (0, last - 1, last):
        block.first_beyond(vv, la, ff, k)
    for lev in (0, levels - 1):
        abc = [halo_a[comp, lev] for comp in range(3)]
        block.put_both(ff, lev + 1, last, block.tangent(vv, lev + 2, last, abc))
    for lev in range(levels):
        if lev in (0, levels - 1):
            for k in range(last):
                abc = [vel[1, comp, lev, tile(k)] for comp in range(3)]
                xx[lev, tile(k)] = block.tangent(ff, lev + 1, k, abc)
        xx[lev, tile(last)] = block.tangent(ff, lev + 1, last, [halo_b[comp, lev] for comp in range(3)])


def factor_kernel(levels, cols, lat, columns, owner, west, east, *refs):
    factor = refs[-1]
    total = refs[0][...]
    for ref in refs[1:-1]:
        total = total + ref[...]
    scales = columns / (NBOX * jnp.maximum(total, 1.0))
    for k in range(cols // CHUNK + 1):
        if k < cols // CHUNK:
            mine = owner[tile(k)].astype(f32)
        else:
            mine = unpack(west, east, B_ROWS, levels * LEVEL_ROWS)
        value = jnp.zeros((CHUNK, lat), f32)
        for box in range(1, NBOX + 1):
            value = jnp.where(mine == float(box), jnp.broadcast_to(scales[:, box - 1 : box], (CHUNK, lat)), value)
        factor[tile(k)] = value


def stencil_kernel(
    levels, cols, lat, lw, vel, factor, halo_a, halo_b, la, xx, *refs
):
    applied, send_a, send_b = refs[:3]
    (w_in, w_e, w_w, w_u, w_d, u_in, u_e, u_w, u_u, u_d, out) = refs[3:]
    block = Block(levels, cols, lat)
    chunks, has, even, push = block.chunks, block.has, block.even, block.push

    def flow(section, k, lev):
        if k < chunks:
            return [vel[section, comp, lev, tile(k)] for comp in range(3)]
        return [(halo_b if section else halo_a)[comp, lev] for comp in range(3)]

    def flow_beyond(side, k):
        return [la[side, comp, tile(k)] for comp in range(3)]

    def second_level(lev, carry):
        weight = lw[lev]
        for k in range(chunks + 1):
            abc = flow(1, k, lev)
            x = (weight * factor[tile(k)]) * xx[lev, tile(k)]
            push(x, abc, (w_in, w_e, w_w, w_u, w_d), lev + 1, k)
        return carry

    lax.fori_loop(0, levels, second_level, 0, unroll=True)
    for k in range(chunks + 1):
        w_u[0, rows(k)] = jnp.zeros((CHUNK, lat), f32)
        w_d[levels + 1, rows(k)] = jnp.zeros((CHUNK, lat), f32)

    def third_level(lev, carry):
        for k in range(chunks + 1):
            x = (
                w_in[lev + 1, rows(k)]
                + (w_e[lev + 1, rows(k, -1)] + w_w[lev + 1, rows(k, 1)])
                + (w_u[lev, rows(k)] + w_d[lev + 2, rows(k)])
            )
            push(x, flow(0, k, lev), (u_in, u_e, u_w, u_u, u_d), lev + 1, k)
        return carry

    lax.fori_loop(0, levels, third_level, 0, unroll=True)
    for k in range(chunks + 1):
        for side, at, x in ((0, 0, w_d[1, rows(k)]), (1, levels + 1, w_u[levels, rows(k)])):
            x = jnp.where(has[side], x, 0.0)
            push(x, flow_beyond(side, k), (u_in, u_e, u_w, u_u, u_d), at, k)

    for k in range(chunks):
        cells = slice(CHUNK * k, CHUNK * (k + 1))
        out[0, cells] = u_d[0, rows(k)]
        out[levels + 3, cells] = u_u[levels + 1, rows(k)]
        for at in range(levels + 2):
            x = u_in[at, rows(k)] + (u_e[at, rows(k, -1)] + u_w[at, rows(k, 1)])
            if at > 0:
                x = x + u_u[at - 1, rows(k)]
            if at < levels + 1:
                x = x + u_d[at + 1, rows(k)]
            if 1 <= at <= levels:
                applied[at - 1, cells] = x
            else:
                out[at + 1, cells] = x
    up = jnp.where(even, levels + 2, 0)
    down = levels + 2 - up
    for i in range(SECOND):
        send_a[i] = out[up + i, 0:cols]
        send_b[i] = out[down + i, 0:cols]


def put_sum(rows_ref, at, acc):
    rows_ref[at : at + 1] = jnp.sum(acc, axis=0, keepdims=True)


def to_lanes(rows_ref, at):
    return jnp.sum(jnp.transpose(rows_ref[at : at + 128, :]), axis=0, keepdims=True)


def tiles(lat):
    return [slice(t, t + 128) for t in range(0, lat, 128)]


def load_kernel(beta_prev, s_hbm, prev_hbm, order, beta_out, s, prev, sems):
    copies = [pltpu.make_async_copy(s_hbm.at[i], s.at[i], sems.at[i]) for i in range(s.shape[0])]
    copies.append(pltpu.make_async_copy(prev_hbm, prev, sems.at[s.shape[0]]))
    for copy in copies:
        copy.start()
    beta_out[...] = jnp.full((1, 128), beta_prev[0], f32)
    for copy in copies:
        copy.wait()


def gram_kernel(nvec, levels, cols, lat, s, v, order, out, sums):
    sums[...] = jnp.zeros(sums.shape, f32)
    steps = levels * (cols // CHUNK)
    block = 4

    def place(step):
        lev = step // (cols // CHUNK)
        row = pl.multiple_of((step - lev * (cols // CHUNK)) * CHUNK, CHUNK)
        return lev, pl.ds(row, CHUNK)

    for i0 in range(0, nvec, block):
        for j0 in range(i0, nvec, block):
            pairs = [(i, j) for i in range(i0, i0 + block) for j in range(j0, j0 + block) if i <= j]

            def body(step, acc, pairs=pairs, need=sorted({*range(i0, i0 + block), *range(j0, j0 + block)})):
                lev, cells = place(step)
                for t in tiles(lat):
                    held = {i: s[i, lev, cells, t] for i in need}
                    acc = tuple(x + held[i] * held[j] for x, (i, j) in zip(acc, pairs))
                return acc

            acc = lax.fori_loop(0, steps, body, tuple(jnp.zeros((CHUNK, 128), f32) for _ in pairs), unroll=4)
            for (i, j), x in zip(pairs, acc):
                put_sum(sums, nvec * i + j, x)

    def body_v(step, acc):
        lev, cells = place(step)
        for t in tiles(lat):
            x = v[lev, cells, t]
            acc = tuple(y + x * s[i, lev, cells, t] for i, y in enumerate(acc[:-1])) + (acc[-1] + x * x,)
        return acc

    acc = lax.fori_loop(0, steps, body_v, tuple(jnp.zeros((CHUNK, 128), f32) for _ in range(nvec + 1)), unroll=2)
    base = nvec * nvec
    for i in range(nvec):
        put_sum(sums, base + nvec + i, acc[i])
    put_sum(sums, base + 2 * nvec + 2, acc[nvec])
    for r in range(base // 128 + 1):
        out[r : r + 1] = to_lanes(sums, 128 * r)


def gather_kernel(nvec, levels, cols, lat, count, part, got_a, got_b, prev, beta_prev, v, s, gram, applied, msg, sums):
    level = lax.axis_index("lev")
    has = (level > 0, level < lax.axis_size("lev") - 1)
    even = even_level()
    beta = jnp.broadcast_to(beta_prev[:, 0:1], (CHUNK, lat))
    for k in range(cols // CHUNK):
        cells = slice(CHUNK * k, CHUNK * (k + 1))
        for lev in range(levels):
            x = part[lev, cells] - beta * prev[lev, cells]
            if lev < SECOND:
                x = x + jnp.where(has[0], jnp.where(even, got_b[lev, cells], got_a[lev, cells]), 0.0)
            if lev >= levels - SECOND:
                i = lev - levels + SECOND
                x = x + jnp.where(has[1], jnp.where(even, got_a[i, cells], got_b[i, cells]), 0.0)
            applied[lev, cells] = x
    sums[...] = jnp.zeros(sums.shape, f32)
    steps = levels * (cols // CHUNK)

    def body(step, acc):
        lev = step // (cols // CHUNK)
        cells = pl.ds(pl.multiple_of((step - lev * (cols // CHUNK)) * CHUNK, CHUNK), CHUNK)
        for t in tiles(lat):
            x = applied[lev, cells, t]
            acc = tuple(y + x * s[i, lev, cells, t] for i, y in enumerate(acc[:nvec])) + (
                acc[nvec] + x * x,
                acc[nvec + 1] + x * v[lev, cells, t],
            )
        return acc

    acc = lax.fori_loop(0, steps, body, tuple(jnp.zeros((CHUNK, 128), f32) for _ in range(nvec + 2)), unroll=4)
    for i in range(nvec):
        put_sum(sums, i, acc[i])
    put_sum(sums, 2 * nvec, acc[nvec])
    put_sum(sums, 2 * nvec + 1, acc[nvec + 1])
    r = gram.shape[0] - 1
    row = to_lanes(sums, 0) + gram[r : r + 1]
    msg[:, 0:r] = jnp.broadcast_to(gram[0:r][None], (count, r, 128))
    msg[:, r : r + 1] = jnp.broadcast_to(row[None], (count, 1, 128))


def orthogonal_kernel(nvec, levels, cols, lat, cells_all, msg, applied, v, s, orthogonal, out, trust):
    total = jnp.sum(msg[...], axis=0) * (1.0 / cells_all)
    r = total.shape[0] - 1
    row = total[r : r + 1]
    aa = row[:, 2 * nvec : 2 * nvec + 1]
    alpha = row[:, 2 * nvec + 1 : 2 * nvec + 2]
    vv = row[:, 2 * nvec + 2 : 2 * nvec + 3]
    lanes = lane_iota((1, 128))
    pv = row - alpha * pltpu.roll(row, 128 - nvec, 1)
    p = [jnp.broadcast_to(pv[:, k : k + 1], (1, 128)) for k in range(nvec)]
    tiled = jnp.zeros((1, 128), f32)
    for k in range(nvec):
        tiled = jnp.where(lax.rem(lanes, nvec) == k, p[k], tiled)
    quad = jnp.zeros((1, 128), f32)
    per = 128 // nvec
    for g in range(r):
        rep = jnp.zeros((1, 128), f32)
        for i in range(per):
            rep = jnp.where(lanes // nvec == i, p[g * per + i], rep)
        i, j = g * per + lanes // nvec, lax.rem(lanes, nvec)
        weight = jnp.where(i == j, 1.0, jnp.where(i < j, 2.0, 0.0))
        quad = quad + weight * rep * tiled * total[g : g + 1]
    quad = jnp.sum(quad, axis=1, keepdims=True)
    pp = jnp.sum(jnp.where(lanes < nvec, pv * pv, 0.0), axis=1, keepdims=True)
    square = (aa - 2.0 * alpha * alpha + alpha * alpha * vv) + (quad - 2.0 * pp)
    size = aa + alpha * alpha * (2.0 + vv) + 2.0 * pp + jnp.abs(quad)
    trust[...] = jnp.where((square > 0.03125 * size) & (size < 1e36), 1.0, 0.0)
    beta = jnp.sqrt(square + 1e-12)
    out[...] = jnp.where(lanes == 0, alpha, jnp.where(lanes == 1, beta, pltpu.roll(pv, 2, 1)))


    a_w = jnp.broadcast_to(alpha, (CHUNK, 128))
    weights = [jnp.broadcast_to(x, (CHUNK, 128)) for x in p]

    for lev in range(levels):
        for k in range(cols // CHUNK):
            for t in tiles(lat):
                x = applied[lev, tile(k), t] - a_w * v[lev, tile(k), t]
                y = [weights[k0] * s[k0, lev, tile(k), t] for k0 in range(nvec)]
                while len(y) > 1:
                    y = [a + b for a, b in zip(y[::2], y[1::2])] + y[len(y) & ~1 :]
                orthogonal[lev, tile(k), t] = x - y[0]


def scale_kernel(nvec, row, orthogonal, result_out, coefs_out, result, coefs, sems):
    line = row[...]
    coefs[...] = line[:, 0 : nvec + 2]
    copies = [pltpu.make_async_copy(result.at[i], result_out.at[i], sems.at[i]) for i in range(result.shape[0])]
    copies.append(pltpu.make_async_copy(coefs, coefs_out, sems.at[result.shape[0]]))
    copies[-1].start()
    inverse = 1.0 / line[:, 1:2]
    for i in range(result.shape[0]):
        result[i] = orthogonal[i] * inverse
        copies[i].start()
    for copy in copies:
        copy.wait()


def body(v, prev, beta_prev, s, vel, lw, owner):
    lon_n, lev_n = lax.axis_size("lon"), lax.axis_size("lev")
    count = lon_n * lev_n
    levels, cols, lat = v.shape
    nvec = s.shape[0]
    lines = levels * LEVEL_ROWS + B_ROWS + 1
    lines += -lines % CHUNK

    lo, hi, lev_a, lev_b, counts, v, vel, owner = call(
        functools.partial(pack_kernel, levels, cols),
        (sds(lines, lat), sds(lines, lat), sds(5, cols, lat), sds(5, cols, lat), sds(1, 128),
         sds(*v.shape), sds(*vel.shape), jax.ShapeDtypeStruct(owner.shape, owner.dtype)),
        tuple(in_hbm(x) for x in (v, vel, owner)), specs=[HBM] * 3, scratch=[pltpu.SemaphoreType.DMA((8,))], flops=1 << 20,
    )
    east_of = [(i, (i + 1) % lon_n) for i in range(lon_n)]
    west_of = [((i + 1) % lon_n, i) for i in range(lon_n)]
    pairs_a = [(i, i ^ 1) for i in range(lev_n)]
    pairs_b = []
    for i in range(count):
        at, level = divmod(i, lev_n)
        if level in (0, lev_n - 1):
            pairs_b.append((i, (at ^ 1) * lev_n + level))
        else:
            pairs_b.append((i, i + 1 if level % 2 else i - 1))

    def both(a, b):
        return lax.ppermute(a, "lev", pairs_a), lax.ppermute(b, ("lon", "lev"), pairs_b)

    around = [(i, (i + 1) % lev_n if i % 2 else (i - 1) % lev_n) for i in range(lev_n)]

    west, east = lax.ppermute(hi, "lon", east_of), lax.ppermute(lo, "lon", west_of)
    lev_a, lev_b = lax.ppermute(lev_a, "lev", pairs_a), lax.ppermute(lev_b, "lev", around)
    counts_2 = lax.ppermute(counts, "lon", [((i + 2) % lon_n, i) for i in range(lon_n)])

    beta_row, s, prev = call(
        load_kernel, (sds(1, 128), sds(*s.shape), sds(*prev.shape)),
        (beta_prev.reshape(1), in_hbm(s), in_hbm(prev), counts), specs=[SM, HBM, HBM, VM],
        scratch=[pltpu.SemaphoreType.DMA((nvec + 1,))],
    )
    padded = cols + 3 * CHUNK
    vv, la = call(
        functools.partial(lev_kernel, levels, cols, lat),
        (sds(levels + 4, padded, lat), sds(2, 3, cols + CHUNK, lat)), (lev_a, lev_b),
    )
    window = call(
        functools.partial(window_kernel, levels), sds(1, 128), (west, east, counts, counts_2, beta_row)
    )
    if lon_n == 8:
        near = [window, lax.ppermute(window, "lon", [(i, i ^ 4) for i in range(lon_n)])]
    else:
        near = [lax.psum(counts, "lon")]
    corners = corner_at(5) + -corner_at(5) % CHUNK
    corner_a, corner_b = call(
        functools.partial(corner_kernel, levels),
        (sds(corners, lat), sds(corners, lat)), (west, east, window), flops=1 << 33,
    )
    corner_a, corner_b = both(corner_a, corner_b)

    vv, ff, xx, halo_a, halo_b = call(
        functools.partial(first_kernel, levels, cols, lat),
        (sds(*vv.shape), sds(levels + 2, padded, lat), sds(levels, cols + CHUNK, lat),
         sds(3, levels, CHUNK, lat), sds(3, levels, CHUNK, lat)),
        (v, vel, west, east, vv, la), alias={4: 0}, flops=4 << 20,
    )
    factor = call(
        functools.partial(factor_kernel, levels, cols, lat, float(cols * lon_n * lat)),
        sds(cols + CHUNK, lat), (owner, west, east, *near), flops=1 << 33,
    )
    vv, la, ff, xx = call(
        functools.partial(edge_kernel, levels, cols, lat), tuple(sds(*x.shape) for x in (vv, la, ff, xx)),
        (vel, halo_a, halo_b, corner_a, corner_b, vv, la, ff, xx, factor), alias={5: 0, 6: 1, 7: 2, 8: 3}, flops=2 << 20,
    )
    scratch = [pltpu.VMEM((levels + 2, padded, lat), f32)] * 10
    scratch += [pltpu.VMEM((levels + 4, cols + CHUNK, lat), f32)]
    operands = (lw, vel, factor, halo_a, halo_b, la, xx)
    part, send_a, send_b = call(
        functools.partial(stencil_kernel, levels, cols, lat),
        (sds(levels, cols, lat), sds(SECOND, cols, lat), sds(SECOND, cols, lat)),
        operands, specs=[SM] + [VM] * (len(operands) - 1), scratch=scratch, flops=8 << 20, mib=12,
    )
    got_a, got_b = both(send_a, send_b)
    gram_rows = nvec * nvec // 128 + 1
    gram = call(
        functools.partial(gram_kernel, nvec, levels, cols, lat),
        sds(gram_rows, 128), (s, v, send_a),
        scratch=[pltpu.VMEM((128 * gram_rows, 128), f32)], flops=20 << 20,
    )
    applied, msg = call(
        functools.partial(gather_kernel, nvec, levels, cols, lat, count),
        (sds(levels, cols, lat), sds(count, gram_rows, 128)),
        (part, got_a, got_b, prev, beta_row, v, s, gram),
        scratch=[pltpu.VMEM((128, 128), f32)],
    )
    msg = lax.all_to_all(msg, ("lon", "lev"), 0, 0, tiled=True)
    cells = float(v.size * count)
    orthogonal, row, trust = call(
        functools.partial(orthogonal_kernel, nvec, levels, cols, lat, cells),
        (sds(levels, cols, lat), sds(1, 128), sds(1, 1)), (msg, applied, v, s),
    )

    def direct():
        square = lax.psum(jnp.sum(orthogonal * orthogonal), ("lon", "lev")) / cells
        return row.at[0, 1].set(jnp.sqrt(square + 1e-12))

    row = lax.cond(trust[0, 0] > 0.5, lambda: row, direct)
    result, coefs = call(
        functools.partial(scale_kernel, nvec),
        (sds(levels, cols, lat), sds(1, nvec + 2)),
        (row, orthogonal), out_specs=(HBM, HBM),
        scratch=[pltpu.VMEM((levels, cols, lat), f32), pltpu.VMEM((1, nvec + 2), f32),
                 pltpu.SemaphoreType.DMA((levels + 1,))],
    )
    return result, coefs.reshape(nvec + 2)


def solution(mesh):
    placed = (
        P("lev", "lon", None),
        P("lev", "lon", None),
        P(),
        P(None, "lev", "lon", None),
        P(None, None, "lev", "lon", None),
        P("lev"),
        P("lon", None),
    )
    return jax.shard_map(
        body, mesh=mesh, in_specs=placed, out_specs=(P("lev", "lon", None), P()), check_vma=False
    )
```

```python
import functools

import jax
import jax.numpy as jnp
from jax import lax
from jax.experimental import pallas as pl
from jax.experimental.pallas import tpu as pltpu
from jax.sharding import PartitionSpec as P

NBOX = 5
kappa = 0.1
centre = 1.0 - 6.0 * kappa
f32 = jnp.float32

VM = pl.BlockSpec(memory_space=pltpu.VMEM)
SM = pl.BlockSpec(memory_space=pltpu.SMEM)
HBM = pl.BlockSpec(memory_space=pltpu.HBM)
CHUNK = 8
WIDE = 4
SECOND = 2
V_ROWS, A_ROWS, B_ROWS = 4, 3, 2
LEVEL_ROWS = V_ROWS + 3 * (A_ROWS + B_ROWS)
B_AT = V_ROWS + 3 * A_ROWS


def sds(*shape):
    return jax.ShapeDtypeStruct(shape, f32)


def call(kernel, outs, operands, specs=None, scratch=(), flops=0, alias=None, out_specs=None, mib=4):
    nbytes = sum(4 * x.size for x in operands)
    return pl.pallas_call(
        kernel,
        out_shape=outs,
        in_specs=specs or [VM] * len(operands),
        out_specs=out_specs or jax.tree.map(lambda _: VM, outs),
        scratch_shapes=list(scratch),
        input_output_aliases=alias or {},
        compiler_params=pltpu.CompilerParams(vmem_limit_bytes=mib << 20),
        cost_estimate=pl.CostEstimate(flops=flops, bytes_accessed=nbytes, transcendentals=0),
    )(*operands)


def in_hbm(x):
    return pltpu.with_memory_space_constraint(x, pltpu.HBM)


def lane_iota(shape):
    return lax.broadcasted_iota(jnp.int32, shape, len(shape) - 1)


def even_level():
    return lax.rem(lax.axis_index("lev"), 2) == 0


def pack_kernel(levels, cols, v_hbm, vel_hbm, owner_hbm, lo, hi, lev_a, lev_b, counts, v, vel, owner, sems):
    copies = [pltpu.make_async_copy(v_hbm, v, sems.at[0]), pltpu.make_async_copy(owner_hbm, owner, sems.at[1])]
    for section in range(2):
        for comp in range(3):
            sem = sems.at[2 + 3 * section + comp]
            copies.append(pltpu.make_async_copy(vel_hbm.at[section, comp], vel.at[section, comp], sem))
    for copy in copies:
        copy.start()

    def edge(low, n):
        return slice(0, n) if low else slice(cols - n, cols)

    sides = ((lo, True), (hi, False))
    even = even_level()
    tops = ((lev_a, even), (lev_b, jnp.logical_not(even)))
    copies[0].wait()
    for msg, low in sides:
        for lev in range(levels):
            msg[lev * LEVEL_ROWS : lev * LEVEL_ROWS + V_ROWS] = v[lev, edge(low, V_ROWS)]
    for msg, top in tops:
        msg[0] = v[jnp.where(top, levels - 1, 0)]
        msg[1] = v[jnp.where(top, levels - 2, 1)]
    copies[1].wait()
    lanes = lane_iota((1, 128))
    row = jnp.zeros((1, 128), f32)
    held = owner[...]
    for box in range(1, NBOX + 1):
        hot = jnp.sum((held == box).astype(f32), axis=0, keepdims=True)
        row = jnp.where(lanes == box - 1, jnp.sum(hot, axis=1, keepdims=True), row)
    counts[...] = row
    at = levels * LEVEL_ROWS
    for msg, low in sides:
        msg[at : at + B_ROWS] = owner[edge(low, B_ROWS)].astype(f32)
        msg[at + B_ROWS : at + B_ROWS + 1, 0:128] = row
    for section, n, start in ((0, A_ROWS, V_ROWS), (1, B_ROWS, B_AT)):
        for comp in range(3):
            copies[2 + 3 * section + comp].wait()
            for msg, low in sides:
                for lev in range(levels):
                    at = lev * LEVEL_ROWS + start + comp * n
                    msg[at : at + n] = vel[section, comp, lev, edge(low, n)]
            if section == 0:
                for msg, top in tops:
                    msg[2 + comp] = vel[0, comp, jnp.where(top, levels - 1, 0)]


def unpack(west, east, n, at):
    gap = jnp.zeros((CHUNK - 2 * n, west.shape[1]), f32)
    parts = [east[at : at + n], gap, west[at : at + n]]
    return jnp.concatenate([x for x in parts if x.shape[0]], axis=0)


CORNER_ROWS = (3, 2, 2, 2, 2)


def corner_at(item):
    return 2 * sum(CORNER_ROWS[:item])


def corner_kernel(levels, west, east, window, corner_a, corner_b):
    even = even_level()

    def part(item, lev):
        n = CORNER_ROWS[item]
        held = V_ROWS if item < 2 else A_ROWS
        at = lev * LEVEL_ROWS + (0 if item < 2 else V_ROWS + (item - 2) * A_ROWS)
        return east[at : at + n], west[at + held - n : at + held]

    for item, n in enumerate(CORNER_ROWS):
        near = int(item == 1)
        for i, (top, bottom) in enumerate(zip(part(item, levels - 1 - near), part(item, near))):
            at = corner_at(item) + i * n
            corner_a[at : at + n] = jnp.where(even, top, bottom)
            corner_b[at : at + n] = jnp.where(even, bottom, top)


def window_kernel(levels, west, east, counts, counts_2, order, window):
    at = levels * LEVEL_ROWS + B_ROWS
    window[...] = counts[...] + counts_2[...] + west[at : at + 1, 0:128] + east[at : at + 1, 0:128]


class Block:
    def __init__(self, levels, cols, lat):
        self.levels, self.lat, self.chunks = levels, lat, cols // CHUNK
        level = lax.axis_index("lev")
        self.has = (level > 0, level < lax.axis_size("lev") - 1)
        self.even = even_level()
        lanes = lane_iota((CHUNK, lat))
        self.first_lane, self.last_lane = lanes == 0, lanes == lat - 1

    def put_west(self, ref, at, k, value):
        ref[at, rows(k)] = value
        if k == self.chunks:
            ref[at, 0:CHUNK] = value

    def put_east(self, ref, at, k, value):
        ref[at, rows(k)] = value
        if k == 0:
            ref[at, rows(self.chunks + 1)] = value

    def put_both(self, ref, at, k, value):
        self.put_west(ref, at, k, value)
        if k == 0:
            ref[at, rows(self.chunks + 1)] = value

    def from_south(self, x):
        return jnp.where(self.first_lane, 0.0, pltpu.roll(x, 1, 1))

    def from_north(self, x):
        return jnp.where(self.last_lane, 0.0, pltpu.roll(x, self.lat - 1, 1))

    def beyond(self, got_a, got_b, k, vv, la):
        for item in range(5):
            if k < self.chunks:
                a, b = got_a[item, tile(k)], got_b[item, tile(k)]
            else:
                n, at = CORNER_ROWS[item], corner_at(item)
                gap = jnp.zeros((CHUNK - 2 * n, self.lat), f32)
                a, b = (jnp.concatenate([x[at : at + n], gap, x[at + n : at + 2 * n]], axis=0) for x in (got_a, got_b))
            below, above = jnp.where(self.even, b, a), jnp.where(self.even, a, b)
            if item < 2:
                self.put_both(vv, 1 - item, k, jnp.where(self.has[0], below, 0.0))
                self.put_both(vv, self.levels + 2 + item, k, jnp.where(self.has[1], above, 0.0))
            else:
                la[0, item - 2, tile(k)] = below
                la[1, item - 2, tile(k)] = above

    def tangent(self, ref, at, k, abc):
        here = ref[at, rows(k)]
        e, w = ref[at, rows(k, 1)], ref[at, rows(k, -1)]
        n, s = self.from_north(here), self.from_south(here)
        u, d = ref[at + 1, rows(k)], ref[at - 1, rows(k)]
        a, b, c = abc
        around = ((e + w) + (n + s)) + (u + d)
        drift = a * (w - e) + b * (s - n) + c * (d - u)
        return centre * here + kappa * around + 0.5 * drift

    def first_beyond(self, vv, la, ff, k):
        for side, at in ((0, 0), (1, self.levels + 1)):
            value = self.tangent(vv, at + 1, k, [la[side, comp, tile(k)] for comp in range(3)])
            self.put_both(ff, at, k, jnp.where(self.has[side], value, 0.0))

    def push(self, x, abc, dst, at, k):
        inside, to_e, to_w, to_u, to_d = dst
        a, b, c = abc
        base, half = kappa * x, 0.5 * x
        a, b, c = a * half, b * half, c * half
        inside[at, rows(k)] = centre * x + (self.from_south(base - b) + self.from_north(base + b))
        self.put_west(to_e, at, k, base - a)
        self.put_east(to_w, at, k, base + a)
        to_u[at, rows(k)] = base - c
        to_d[at, rows(k)] = base + c


def rows(k, shift=0):
    return slice(CHUNK * (k + 1) + shift, CHUNK * (k + 2) + shift)


def tile(k):
    return slice(CHUNK * k, CHUNK * (k + 1))


def lev_kernel(levels, cols, lat, lev_a, lev_b, vv, la):
    block = Block(levels, cols, lat)
    for k in range(block.chunks):
        block.beyond(lev_a, lev_b, k, vv, la)


def first_kernel(levels, cols, lat, v, vel, west, east, vv_in, la, vv, ff, xx, halo_a, halo_b):
    block = Block(levels, cols, lat)
    last = block.chunks
    for lev in range(levels):
        for k in range(last):
            block.put_both(vv, lev + 2, k, v[lev, tile(k)])
        block.put_both(vv, lev + 2, last, unpack(west, east, V_ROWS, lev * LEVEL_ROWS))
        for comp in range(3):
            base = lev * LEVEL_ROWS + V_ROWS
            halo_a[comp, lev] = unpack(west, east, A_ROWS, base + comp * A_ROWS)
            halo_b[comp, lev] = unpack(west, east, B_ROWS, base + 3 * A_ROWS + comp * B_ROWS)

    def flow(section, lev, k):
        return [vel[section, comp, lev, tile(k)] for comp in range(3)]

    def first_level(lev, carry):
        for k in range(last):
            block.put_both(ff, lev + 1, k, block.tangent(vv, lev + 2, k, flow(0, lev, k)))
        return carry

    lax.fori_loop(0, levels, first_level, 0, unroll=True)
    for k in range(1, last - 1):
        block.first_beyond(vv, la, ff, k)

    def inner_level(lev, carry):
        abc = [halo_a[comp, lev] for comp in range(3)]
        block.put_both(ff, lev + 1, last, block.tangent(vv, lev + 2, last, abc))
        for k in range(last):
            xx[lev, tile(k)] = block.tangent(ff, lev + 1, k, flow(1, lev, k))
        return carry

    lax.fori_loop(1, levels - 1, inner_level, 0, unroll=True)


def edge_kernel(levels, cols, lat, vel, halo_a, halo_b, corner_a, corner_b, vv_in, la_in, ff_in, xx_in, factor, vv, la, ff, xx):
    block = Block(levels, cols, lat)
    last = block.chunks
    block.beyond(corner_a, corner_b, last, vv, la)
    for k in (0, last - 1, last):
        block.first_beyond(vv, la, ff, k)
    for lev in (0, levels - 1):
        abc = [halo_a[comp, lev] for comp in range(3)]
        block.put_both(ff, lev + 1, last, block.tangent(vv, lev + 2, last, abc))
    for lev in range(levels):
        if lev in (0, levels - 1):
            for k in range(last):
                abc = [vel[1, comp, lev, tile(k)] for comp in range(3)]
                xx[lev, tile(k)] = block.tangent(ff, lev + 1, k, abc)
        xx[lev, tile(last)] = block.tangent(ff, lev + 1, last, [halo_b[comp, lev] for comp in range(3)])


def factor_kernel(levels, cols, lat, columns, owner, west, east, after, *refs):
    factor = refs[-1]
    total = refs[0][...]
    for ref in refs[1:-1]:
        total = total + ref[...]
    scales = columns / (NBOX * jnp.maximum(total, 1.0))
    for k in range(cols // CHUNK + 1):
        if k < cols // CHUNK:
            mine = owner[tile(k)].astype(f32)
        else:
            mine = unpack(west, east, B_ROWS, levels * LEVEL_ROWS)
        value = jnp.zeros((CHUNK, lat), f32)
        for box in range(1, NBOX + 1):
            value = jnp.where(mine == float(box), jnp.broadcast_to(scales[:, box - 1 : box], (CHUNK, lat)), value)
        factor[tile(k)] = value


def stencil_kernel(
    levels, cols, lat, lw, vel, factor, halo_a, halo_b, la, xx, *refs
):
    applied, send_a, send_b = refs[:3]
    (w_in, w_e, w_w, w_u, w_d, u_in, u_e, u_w, u_u, u_d, out) = refs[3:]
    block = Block(levels, cols, lat)
    chunks, has, even, push = block.chunks, block.has, block.even, block.push

    def flow(section, k, lev):
        if k < chunks:
            return [vel[section, comp, lev, tile(k)] for comp in range(3)]
        return [(halo_b if section else halo_a)[comp, lev] for comp in range(3)]

    def flow_beyond(side, k):
        return [la[side, comp, tile(k)] for comp in range(3)]

    def second_level(lev, carry):
        weight = lw[lev]
        for k in range(chunks + 1):
            abc = flow(1, k, lev)
            x = (weight * factor[tile(k)]) * xx[lev, tile(k)]
            push(x, abc, (w_in, w_e, w_w, w_u, w_d), lev + 1, k)
        return carry

    lax.fori_loop(0, levels, second_level, 0, unroll=True)
    for k in range(chunks + 1):
        w_u[0, rows(k)] = jnp.zeros((CHUNK, lat), f32)
        w_d[levels + 1, rows(k)] = jnp.zeros((CHUNK, lat), f32)

    def third_level(lev, carry):
        for k in range(chunks + 1):
            x = (
                w_in[lev + 1, rows(k)]
                + (w_e[lev + 1, rows(k, -1)] + w_w[lev + 1, rows(k, 1)])
                + (w_u[lev, rows(k)] + w_d[lev + 2, rows(k)])
            )
            push(x, flow(0, k, lev), (u_in, u_e, u_w, u_u, u_d), lev + 1, k)
        return carry

    lax.fori_loop(0, levels, third_level, 0, unroll=True)
    for k in range(chunks + 1):
        for side, at, x in ((0, 0, w_d[1, rows(k)]), (1, levels + 1, w_u[levels, rows(k)])):
            x = jnp.where(has[side], x, 0.0)
            push(x, flow_beyond(side, k), (u_in, u_e, u_w, u_u, u_d), at, k)

    for k in range(chunks):
        cells = slice(CHUNK * k, CHUNK * (k + 1))
        out[0, cells] = u_d[0, rows(k)]
        out[levels + 3, cells] = u_u[levels + 1, rows(k)]
        for at in range(levels + 2):
            x = u_in[at, rows(k)] + (u_e[at, rows(k, -1)] + u_w[at, rows(k, 1)])
            if at > 0:
                x = x + u_u[at - 1, rows(k)]
            if at < levels + 1:
                x = x + u_d[at + 1, rows(k)]
            if 1 <= at <= levels:
                applied[at - 1, cells] = x
            else:
                out[at + 1, cells] = x
    up = jnp.where(even, levels + 2, 0)
    down = levels + 2 - up
    for i in range(SECOND):
        send_a[i] = out[up + i, 0:cols]
        send_b[i] = out[down + i, 0:cols]


def put_sum(rows_ref, at, acc):
    rows_ref[at : at + 1] = jnp.sum(acc, axis=0, keepdims=True)


def to_lanes(rows_ref, at):
    return jnp.sum(jnp.transpose(rows_ref[at : at + 128, :]), axis=0, keepdims=True)


def tiles(lat):
    return [slice(t, t + 128) for t in range(0, lat, 128)]


def load_kernel(beta_prev, s_hbm, prev_hbm, order, beta_out, s, prev, sems):
    copies = [pltpu.make_async_copy(s_hbm.at[i], s.at[i], sems.at[i]) for i in range(s.shape[0])]
    copies.append(pltpu.make_async_copy(prev_hbm, prev, sems.at[s.shape[0]]))
    for copy in copies:
        copy.start()
    beta_out[...] = jnp.full((1, 128), beta_prev[0], f32)
    for copy in copies:
        copy.wait()


def gram_kernel(nvec, levels, cols, lat, s, v, order, out, sums):
    sums[...] = jnp.zeros(sums.shape, f32)
    steps = levels * (cols // CHUNK)
    block = 4

    def place(step):
        lev = step // (cols // CHUNK)
        row = pl.multiple_of((step - lev * (cols // CHUNK)) * CHUNK, CHUNK)
        return lev, pl.ds(row, CHUNK)

    for i0 in range(0, nvec, block):
        for j0 in range(i0, nvec, block):
            pairs = [(i, j) for i in range(i0, i0 + block) for j in range(j0, j0 + block) if i <= j]

            def body(step, acc, pairs=pairs, need=sorted({*range(i0, i0 + block), *range(j0, j0 + block)})):
                lev, cells = place(step)
                for t in tiles(lat):
                    held = {i: s[i, lev, cells, t] for i in need}
                    acc = tuple(x + held[i] * held[j] for x, (i, j) in zip(acc, pairs))
                return acc

            acc = lax.fori_loop(0, steps, body, tuple(jnp.zeros((CHUNK, 128), f32) for _ in pairs), unroll=4)
            for (i, j), x in zip(pairs, acc):
                put_sum(sums, nvec * i + j, x)

    def body_v(step, acc):
        lev, cells = place(step)
        for t in tiles(lat):
            x = v[lev, cells, t]
            acc = tuple(y + x * s[i, lev, cells, t] for i, y in enumerate(acc[:-1])) + (acc[-1] + x * x,)
        return acc

    acc = lax.fori_loop(0, steps, body_v, tuple(jnp.zeros((CHUNK, 128), f32) for _ in range(nvec + 1)), unroll=2)
    base = nvec * nvec
    for i in range(nvec):
        put_sum(sums, base + nvec + i, acc[i])
    put_sum(sums, base + 2 * nvec + 2, acc[nvec])
    for r in range(base // 128 + 1):
        out[r : r + 1] = to_lanes(sums, 128 * r)


def gather_kernel(nvec, levels, cols, lat, count, part, got_a, got_b, prev, beta_prev, v, s, gram, applied, msg, sums):
    level = lax.axis_index("lev")
    has = (level > 0, level < lax.axis_size("lev") - 1)
    even = even_level()
    beta = jnp.broadcast_to(beta_prev[:, 0:1], (CHUNK, lat))
    for k in range(cols // CHUNK):
        cells = slice(CHUNK * k, CHUNK * (k + 1))
        for lev in range(levels):
            x = part[lev, cells] - beta * prev[lev, cells]
            if lev < SECOND:
                x = x + jnp.where(has[0], jnp.where(even, got_b[lev, cells], got_a[lev, cells]), 0.0)
            if lev >= levels - SECOND:
                i = lev - levels + SECOND
                x = x + jnp.where(has[1], jnp.where(even, got_a[i, cells], got_b[i, cells]), 0.0)
            applied[lev, cells] = x
    sums[...] = jnp.zeros(sums.shape, f32)
    steps = levels * (cols // CHUNK)

    def body(step, acc):
        lev = step // (cols // CHUNK)
        cells = pl.ds(pl.multiple_of((step - lev * (cols // CHUNK)) * CHUNK, CHUNK), CHUNK)
        for t in tiles(lat):
            x = applied[lev, cells, t]
            acc = tuple(y + x * s[i, lev, cells, t] for i, y in enumerate(acc[:nvec])) + (
                acc[nvec] + x * x,
                acc[nvec + 1] + x * v[lev, cells, t],
            )
        return acc

    acc = lax.fori_loop(0, steps, body, tuple(jnp.zeros((CHUNK, 128), f32) for _ in range(nvec + 2)), unroll=4)
    for i in range(nvec):
        put_sum(sums, i, acc[i])
    put_sum(sums, 2 * nvec, acc[nvec])
    put_sum(sums, 2 * nvec + 1, acc[nvec + 1])
    r = gram.shape[0] - 1
    row = to_lanes(sums, 0) + gram[r : r + 1]
    msg[:, 0:r] = jnp.broadcast_to(gram[0:r][None], (count, r, 128))
    msg[:, r : r + 1] = jnp.broadcast_to(row[None], (count, 1, 128))


def orthogonal_kernel(nvec, levels, cols, lat, cells_all, msg, applied, v, s, orthogonal, out, trust):
    total = jnp.sum(msg[...], axis=0) * (1.0 / cells_all)
    r = total.shape[0] - 1
    row = total[r : r + 1]
    aa = row[:, 2 * nvec : 2 * nvec + 1]
    alpha = row[:, 2 * nvec + 1 : 2 * nvec + 2]
    vv = row[:, 2 * nvec + 2 : 2 * nvec + 3]
    lanes = lane_iota((1, 128))
    pv = row - alpha * pltpu.roll(row, 128 - nvec, 1)
    p = [jnp.broadcast_to(pv[:, k : k + 1], (1, 128)) for k in range(nvec)]
    tiled = jnp.zeros((1, 128), f32)
    for k in range(nvec):
        tiled = jnp.where(lax.rem(lanes, nvec) == k, p[k], tiled)
    quad = jnp.zeros((1, 128), f32)
    per = 128 // nvec
    for g in range(r):
        rep = jnp.zeros((1, 128), f32)
        for i in range(per):
            rep = jnp.where(lanes // nvec == i, p[g * per + i], rep)
        i, j = g * per + lanes // nvec, lax.rem(lanes, nvec)
        weight = jnp.where(i == j, 1.0, jnp.where(i < j, 2.0, 0.0))
        quad = quad + weight * rep * tiled * total[g : g + 1]
    quad = jnp.sum(quad, axis=1, keepdims=True)
    pp = jnp.sum(jnp.where(lanes < nvec, pv * pv, 0.0), axis=1, keepdims=True)
    square = (aa - 2.0 * alpha * alpha + alpha * alpha * vv) + (quad - 2.0 * pp)
    size = aa + alpha * alpha * (2.0 + vv) + 2.0 * pp + jnp.abs(quad)
    trust[...] = jnp.where((square > 0.03125 * size) & (size < 1e36), 1.0, 0.0)
    beta = jnp.sqrt(square + 1e-12)
    out[...] = jnp.where(lanes == 0, alpha, jnp.where(lanes == 1, beta, pltpu.roll(pv, 2, 1)))


    a_w = jnp.broadcast_to(alpha, (CHUNK, 128))
    weights = [jnp.broadcast_to(x, (CHUNK, 128)) for x in p]

    for lev in range(levels):
        for k in range(cols // CHUNK):
            for t in tiles(lat):
                x = applied[lev, tile(k), t] - a_w * v[lev, tile(k), t]
                y = [weights[k0] * s[k0, lev, tile(k), t] for k0 in range(nvec)]
                while len(y) > 1:
                    y = [a + b for a, b in zip(y[::2], y[1::2])] + y[len(y) & ~1 :]
                orthogonal[lev, tile(k), t] = x - y[0]


def scale_kernel(nvec, row, orthogonal, result_out, coefs_out, result, coefs, sems):
    line = row[...]
    coefs[...] = line[:, 0 : nvec + 2]
    copies = [pltpu.make_async_copy(result.at[i], result_out.at[i], sems.at[i]) for i in range(result.shape[0])]
    copies.append(pltpu.make_async_copy(coefs, coefs_out, sems.at[result.shape[0]]))
    copies[-1].start()
    inverse = 1.0 / line[:, 1:2]
    for i in range(result.shape[0]):
        result[i] = orthogonal[i] * inverse
        copies[i].start()
    for copy in copies:
        copy.wait()


def body(v, prev, beta_prev, s, vel, lw, owner):
    lon_n, lev_n = lax.axis_size("lon"), lax.axis_size("lev")
    count = lon_n * lev_n
    levels, cols, lat = v.shape
    nvec = s.shape[0]
    lines = levels * LEVEL_ROWS + B_ROWS + 1
    lines += -lines % CHUNK

    lo, hi, lev_a, lev_b, counts, v, vel, owner = call(
        functools.partial(pack_kernel, levels, cols),
        (sds(lines, lat), sds(lines, lat), sds(5, cols, lat), sds(5, cols, lat), sds(1, 128),
         sds(*v.shape), sds(*vel.shape), jax.ShapeDtypeStruct(owner.shape, owner.dtype)),
        tuple(in_hbm(x) for x in (v, vel, owner)), specs=[HBM] * 3, scratch=[pltpu.SemaphoreType.DMA((8,))], flops=1 << 20,
    )
    east_of = [(i, (i + 1) % lon_n) for i in range(lon_n)]
    west_of = [((i + 1) % lon_n, i) for i in range(lon_n)]
    pairs_a = [(i, i ^ 1) for i in range(lev_n)]
    pairs_b = []
    for i in range(count):
        at, level = divmod(i, lev_n)
        if level in (0, lev_n - 1):
            pairs_b.append((i, (at ^ 1) * lev_n + level))
        else:
            pairs_b.append((i, i + 1 if level % 2 else i - 1))

    def both(a, b):
        return lax.ppermute(a, "lev", pairs_a), lax.ppermute(b, ("lon", "lev"), pairs_b)

    around = [(i, (i + 1) % lev_n if i % 2 else (i - 1) % lev_n) for i in range(lev_n)]

    west, east = lax.ppermute(hi, "lon", east_of), lax.ppermute(lo, "lon", west_of)
    lev_a, lev_b = lax.ppermute(lev_a, "lev", pairs_a), lax.ppermute(lev_b, "lev", around)
    counts_2 = lax.ppermute(counts, "lon", [((i + 2) % lon_n, i) for i in range(lon_n)])

    beta_row, s, prev = call(
        load_kernel, (sds(1, 128), sds(*s.shape), sds(*prev.shape)),
        (beta_prev.reshape(1), in_hbm(s), in_hbm(prev), counts), specs=[SM, HBM, HBM, VM],
        scratch=[pltpu.SemaphoreType.DMA((nvec + 1,))],
    )
    padded = cols + 3 * CHUNK
    vv, la = call(
        functools.partial(lev_kernel, levels, cols, lat),
        (sds(levels + 4, padded, lat), sds(2, 3, cols + CHUNK, lat)), (lev_a, lev_b),
    )
    window = call(
        functools.partial(window_kernel, levels), sds(1, 128), (west, east, counts, counts_2, beta_row)
    )
    if lon_n == 8:
        near = [window, lax.ppermute(window, "lon", [(i, i ^ 4) for i in range(lon_n)])]
    else:
        near = [lax.psum(counts, "lon")]
    corners = corner_at(5) + -corner_at(5) % CHUNK
    corner_a, corner_b = call(
        functools.partial(corner_kernel, levels),
        (sds(corners, lat), sds(corners, lat)), (west, east, window), flops=1 << 33,
    )
    corner_a, corner_b = both(corner_a, corner_b)

    vv, ff, xx, halo_a, halo_b = call(
        functools.partial(first_kernel, levels, cols, lat),
        (sds(*vv.shape), sds(levels + 2, padded, lat), sds(levels, cols + CHUNK, lat),
         sds(3, levels, CHUNK, lat), sds(3, levels, CHUNK, lat)),
        (v, vel, west, east, vv, la), alias={4: 0}, flops=4 << 20,
    )
    factor = call(
        functools.partial(factor_kernel, levels, cols, lat, float(cols * lon_n * lat)),
        sds(cols + CHUNK, lat), (owner, west, east, halo_a, *near), flops=1 << 33,
    )
    vv, la, ff, xx = call(
        functools.partial(edge_kernel, levels, cols, lat), tuple(sds(*x.shape) for x in (vv, la, ff, xx)),
        (vel, halo_a, halo_b, corner_a, corner_b, vv, la, ff, xx, factor), alias={5: 0, 6: 1, 7: 2, 8: 3}, flops=2 << 20,
    )
    scratch = [pltpu.VMEM((levels + 2, padded, lat), f32)] * 10
    scratch += [pltpu.VMEM((levels + 4, cols + CHUNK, lat), f32)]
    operands = (lw, vel, factor, halo_a, halo_b, la, xx)
    part, send_a, send_b = call(
        functools.partial(stencil_kernel, levels, cols, lat),
        (sds(levels, cols, lat), sds(SECOND, cols, lat), sds(SECOND, cols, lat)),
        operands, specs=[SM] + [VM] * (len(operands) - 1), scratch=scratch, flops=8 << 20, mib=12,
    )
    got_a, got_b = both(send_a, send_b)
    gram_rows = nvec * nvec // 128 + 1
    gram = call(
        functools.partial(gram_kernel, nvec, levels, cols, lat),
        sds(gram_rows, 128), (s, v, send_a),
        scratch=[pltpu.VMEM((128 * gram_rows, 128), f32)], flops=20 << 20,
    )
    applied, msg = call(
        functools.partial(gather_kernel, nvec, levels, cols, lat, count),
        (sds(levels, cols, lat), sds(count, gram_rows, 128)),
        (part, got_a, got_b, prev, beta_row, v, s, gram),
        scratch=[pltpu.VMEM((128, 128), f32)],
    )
    msg = lax.all_to_all(msg, ("lon", "lev"), 0, 0, tiled=True)
    cells = float(v.size * count)
    orthogonal, row, trust = call(
        functools.partial(orthogonal_kernel, nvec, levels, cols, lat, cells),
        (sds(levels, cols, lat), sds(1, 128), sds(1, 1)), (msg, applied, v, s),
    )

    def direct():
        square = lax.psum(jnp.sum(orthogonal * orthogonal), ("lon", "lev")) / cells
        return row.at[0, 1].set(jnp.sqrt(square + 1e-12))

    row = lax.cond(trust[0, 0] > 0.5, lambda: row, direct)
    result, coefs = call(
        functools.partial(scale_kernel, nvec),
        (sds(levels, cols, lat), sds(1, nvec + 2)),
        (row, orthogonal), out_specs=(HBM, HBM),
        scratch=[pltpu.VMEM((levels, cols, lat), f32), pltpu.VMEM((1, nvec + 2), f32),
                 pltpu.SemaphoreType.DMA((levels + 1,))],
    )
    return result, coefs.reshape(nvec + 2)


def solution(mesh):
    placed = (
        P("lev", "lon", None),
        P("lev", "lon", None),
        P(),
        P(None, "lev", "lon", None),
        P(None, None, "lev", "lon", None),
        P("lev"),
        P("lon", None),
    )
    return jax.shard_map(
        body, mesh=mesh, in_specs=placed, out_specs=(P("lev", "lon", None), P()), check_vma=False
    )
```
